256 devices in a mesh: tile: 64 (over y, z, core), freq: 4 (over x).
Axes of the slice: x: 4, y: 4, z: 8, core: 2. Of those that a mesh axis runs over, the one named last changes fastest.
Arguments:
- spectrum: float32 [32, 24, 131072], P('freq', None, 'tile'), may hold values from 0.02 to 8, as said below
- forcing: float32 [4, 131072], P(None, 'tile'), may hold values from -24 to 24, as said below
- send_rows: int32 [4096, 256], P('tile'), may hold values from 0 to 2047
- point_slot: int32 [4, 131072], P(None, 'tile'), may hold values from 0 to 16383, as said below
- remap_weight: float32 [4, 131072], P(None, 'tile'), may hold values from 0 to 1, as said below
- neighbours: int32 [4, 131072], P(None, 'tile'), may hold values from 0 to 2303
- halo_send: int32 [16384], P('tile'), may hold values from 0 to 2047
Outputs:
- new_spectrum: float32 [32, 24, 131072], P('freq', None, 'tile')
- returned: float32 [4, 131072], P('freq', 'tile')
The draws below stay inside these ranges and needn't reach their ends.
Inputs may be any that keep to these rules, and one draw needn't show every extreme that they name: `point_slot`: the four corners of a point name the same band. Of the list from a band to a tile only the first n slots are named, 1 <= n <= 256, n differing from list to list; for one tile n = 256 on the lists from every band. `remap_weight`: the four weights of a point are positive and sum to one. `spectrum`: Positive. `forcing`: winds within -24 to 24, density 1.0 to 1.4, gustiness 0 to 2.
All inputs are finite; a program needn't handle non-finite values.
Results may differ from the reference program's by a relative error of at most 0.0001.
Values sent between devices are 32-bit elements; how exact they have to be, the bound alone decides.
No kernel may reach another device: no remote copies, remote signals or barrier semaphores. Data moves between devices by JAX's collectives and lax.ppermute only.
A program may use at most 128 MiB of HBM per device.

```python
import math
import jax
import jax.numpy as jnp
from jax import lax

NF = 32
ND = 24
P_DEV = 2048
A_DEV = 2048
HALO = 128
CAP = 256
NPTS = 131072
NA = 131072
N_TILE = 64


def draw_point_slot(key, part):
    key = jax.random.fold_in(key, 11)
    count_key, full_key, band_key, slot_key = jax.random.split(key, 4)
    list_counts = jax.random.randint(count_key, (N_TILE, N_TILE), 1, CAP + 1)
    full_tile = jax.random.randint(full_key, (), 0, N_TILE)
    list_counts = jnp.where(jnp.arange(N_TILE)[None, :] == full_tile, CAP, list_counts)
    npoints = N_TILE * P_DEV
    tile_of = jnp.arange(npoints) // P_DEV
    band_index = jax.random.randint(band_key, (npoints,), 0, N_TILE)
    slot_limit = list_counts[band_index, tile_of]
    list_slot = jax.random.randint(slot_key, (4, npoints), 0, slot_limit)
    return (band_index[None, :] * CAP + list_slot).astype(jnp.int32)


def draw_remap_weight(key, part):
    key = jax.random.fold_in(key, 12)
    raw_weight = jax.random.uniform(key, (4, NPTS), jnp.float32, 0.1, 1.0)
    return raw_weight / jnp.sum(raw_weight, axis=0, keepdims=True)


def draw_forcing(key, part):
    key = jax.random.fold_in(key, 13)
    wind_key, density_key, gust_key = jax.random.split(key, 3)
    winds = 8.0 * jnp.clip(jax.random.normal(wind_key, (2, NA), jnp.float32), -3.0, 3.0)
    density = jax.random.uniform(density_key, (1, NA), jnp.float32, 1.0, 1.4)
    gust = jax.random.uniform(gust_key, (1, NA), jnp.float32, 0.0, 2.0)
    return jnp.concatenate([winds, density, gust], axis=0)


def draw_spectrum(key, part):
    key = jax.random.fold_in(key, 14)
    rough_key = jax.random.fold_in(key, 0)
    freq_shape = jnp.power(4.0, -jnp.arange(NF, dtype=jnp.float32) / (NF - 1))[:, None, None]
    rough = jnp.exp(jax.random.uniform(rough_key, (NF, ND, NPTS), jnp.float32, math.log(0.5), math.log(2.0)))
    return freq_shape * rough


def with_ends(result, stream_key, smallest, top_value):
    longest = result.shape.index(max(result.shape))
    spots = []
    for shift in (0, 1):
        where = [jax.random.randint(jax.random.fold_in(stream_key, axis), (), 0, length) for axis, length in enumerate(result.shape)]
        where[longest] = (where[longest] + shift) % result.shape[longest]
        spots.append(tuple(where))
    return result.at[spots[0]].set(smallest).at[spots[1]].set(top_value)


def setup_inputs(seed: int = 0) -> dict:
    splits = jax.random.split(jax.random.key(seed), 8)
    return {
        "spectrum": draw_spectrum(jax.random.fold_in(splits[7], 71), 0),
        "forcing": draw_forcing(jax.random.fold_in(splits[7], 71), 0),
        "send_rows": with_ends(jax.random.randint(splits[2], (N_TILE * N_TILE, CAP), 0, A_DEV), jax.random.fold_in(splits[2], 1), 0, A_DEV - 1).astype(jnp.int32),
        "point_slot": draw_point_slot(jax.random.fold_in(splits[7], 71), 0),
        "remap_weight": draw_remap_weight(jax.random.fold_in(splits[7], 71), 0),
        "neighbours": with_ends(jax.random.randint(splits[5], (4, NPTS), 0, P_DEV + 2 * HALO), jax.random.fold_in(splits[5], 1), 0, (P_DEV + 2 * HALO) - 1).astype(jnp.int32),
        "halo_send": with_ends(jax.random.randint(splits[6], (2 * HALO * N_TILE,), 0, P_DEV), jax.random.fold_in(splits[6], 1), 0, P_DEV - 1).astype(jnp.int32),
    }


G_ACC = 9.81
WATER_DENSITY = 1025.0
FREQ_LOW = 0.03453
FREQ_RATIO = 1.1
E_UNIT = 0.001
DT_SRC = 120.0
COURANT_MAX = 0.7
DISSIP_COEF = 2.33e-05
STEEP_PM = 0.00302
TOP_EXPONENT = 31.0

def spectral_bins(findex):
    radian_freq = 2.0 * math.pi * FREQ_LOW * jnp.power(FREQ_RATIO, findex)
    phase_speed = G_ACC / radian_freq
    wavenum = radian_freq * radian_freq / G_ACC
    courant = COURANT_MAX * jnp.power(FREQ_RATIO, -findex)
    return (radian_freq, phase_speed, wavenum, courant)

def direction_tables(count):
    theta = (jnp.arange(count, dtype=jnp.float32) + 0.5) * (2.0 * math.pi / count)
    return (jnp.cos(theta), jnp.sin(theta))

def surface_wind(wind_field):
    east_wind, north_wind, density, gust = (wind_field[0], wind_field[1], wind_field[2], wind_field[3])
    wind_speed = jnp.sqrt(east_wind * east_wind + north_wind * north_wind + 1.0)
    friction_vel = jnp.sqrt(0.001 * (0.8 + 0.065 * wind_speed)) * wind_speed * (1.0 + 0.15 * gust)
    return (east_wind, north_wind, density, wind_speed, friction_vel)

def wind_input(radian_freq, phase_speed, aligned_cos, friction_vel, density):
    excess = jnp.maximum(28.0 * friction_vel * aligned_cos / phase_speed - 1.0, 0.0)
    return 0.25 * (density / WATER_DENSITY) * excess * radian_freq

def partial_moments(spectra, findex, cos_dir, sin_dir, aligned_cos, friction_vel, density):
    radian_freq, phase_speed, wavenum, courant = spectral_bins(findex)
    sum_axes = tuple(range(spectra.ndim - friction_vel.ndim))
    growth = wind_input(radian_freq, phase_speed, aligned_cos, friction_vel, density)
    momentum = growth * spectra / phase_speed
    return jnp.stack([lax.optimization_barrier(jnp.sum(spectra, axis=sum_axes)), lax.optimization_barrier(jnp.sum(spectra / radian_freq, axis=sum_axes)), lax.optimization_barrier(jnp.sum(spectra / jnp.sqrt(wavenum), axis=sum_axes)), lax.optimization_barrier(jnp.sum(momentum * cos_dir, axis=sum_axes)), lax.optimization_barrier(jnp.sum(momentum * sin_dir, axis=sum_axes))])

def finish_moments(moments, east_wind, north_wind, density, wind_speed, friction_vel):
    total_energy, inv_sigma_sum, inv_root_sum = (moments[0], moments[1], moments[2])
    stress_east, stress_north = (moments[3], moments[4])
    mean_sigma = total_energy / inv_sigma_sum
    mean_wavenum = jnp.square(total_energy / inv_root_sum)
    steepness = mean_wavenum * mean_wavenum * total_energy * E_UNIT
    dissipation = DISSIP_COEF * mean_sigma * jnp.square(steepness / STEEP_PM) / mean_wavenum
    stress_scale = WATER_DENSITY / density * G_ACC * E_UNIT
    friction_sq = friction_vel * friction_vel
    east_ratio = stress_scale * stress_east / friction_sq
    north_ratio = stress_scale * stress_north / friction_sq
    aligned = (east_ratio * east_wind + north_ratio * north_wind) / wind_speed
    charnock = 0.01 / jnp.sqrt(1.0 - 0.9 * aligned / (1.0 + jnp.abs(aligned)))
    wave_height = 4.0 * jnp.sqrt(E_UNIT * total_energy)
    return (dissipation, jnp.stack([east_ratio, north_ratio, charnock / 0.01, wave_height]))

def advance(spectra, extended, upwind_east, upwind_north, findex, cos_dir, sin_dir, aligned_cos, friction_vel, density, dissipation):
    radian_freq, phase_speed, wavenum, courant = spectral_bins(findex)
    from_x = jnp.take_along_axis(extended, jnp.broadcast_to(upwind_east, spectra.shape), axis=-1)
    from_y = jnp.take_along_axis(extended, jnp.broadcast_to(upwind_north, spectra.shape), axis=-1)
    moved = spectra - courant * jnp.abs(cos_dir) * (spectra - from_x) - courant * jnp.abs(sin_dir) * (spectra - from_y)
    growth = wind_input(radian_freq, phase_speed, aligned_cos, friction_vel, density) - dissipation * wavenum
    return moved * jnp.exp(DT_SRC * growth)

def reference(spectrum, forcing, send_rows, point_slot, remap_weight, neighbours, halo_send):
    npoints = spectrum.shape[2]
    tile_of = jnp.arange(npoints, dtype=jnp.int32) // P_DEV
    band_index = point_slot // CAP
    list_slot = point_slot % CAP
    source = band_index * A_DEV + send_rows[band_index * N_TILE + tile_of[None, :], list_slot]
    corners = forcing[:, source]
    wind_field = lax.optimization_barrier(jnp.sum(corners * remap_weight[None], axis=1)).reshape(4, N_TILE, P_DEV)
    east_wind, north_wind, density, wind_speed, friction_vel = surface_wind(wind_field)
    cos_dir, sin_dir = direction_tables(ND)
    cos_dir = cos_dir[:, None, None]
    sin_dir = sin_dir[:, None, None]
    aligned_cos = (east_wind * cos_dir + north_wind * sin_dir) / wind_speed
    findex = jnp.arange(NF, dtype=jnp.float32) * (TOP_EXPONENT / (NF - 1))
    spec_tiles = spectrum.reshape(NF, ND, N_TILE, P_DEV)

    def accumulate(carry, inputs):
        spectra, index_now = inputs
        return (carry + partial_moments(spectra, index_now, cos_dir, sin_dir, aligned_cos, friction_vel, density), None)
    moments, unused = lax.scan(accumulate, jnp.zeros((5, N_TILE, P_DEV), jnp.float32), (spec_tiles, findex))
    dissipation, fields = finish_moments(moments, east_wind, north_wind, density, wind_speed, friction_vel)
    near = neighbours.reshape(4, N_TILE, P_DEV)
    upwind_east = jnp.where(cos_dir > 0, near[0], near[1])
    upwind_north = jnp.where(sin_dir > 0, near[2], near[3])
    rim_lists = jnp.broadcast_to(halo_send.reshape(N_TILE, 2 * HALO)[None], (ND, N_TILE, 2 * HALO))

    def step_one(inputs):
        spectra, index_now = inputs
        sent_rows = jnp.take_along_axis(spectra, rim_lists, axis=2)
        zero_rim = jnp.zeros((ND, 1, HALO), jnp.float32)
        lower_rim = jnp.concatenate([zero_rim, sent_rows[:, :-1, HALO:]], axis=1)
        upper_rim = jnp.concatenate([sent_rows[:, 1:, :HALO], zero_rim], axis=1)
        extended = jnp.concatenate([lower_rim, spectra, upper_rim], axis=2)
        return advance(spectra, extended, upwind_east, upwind_north, index_now, cos_dir, sin_dir, aligned_cos, friction_vel, density, dissipation)
    new_spectrum = lax.map(step_one, (spec_tiles, findex)).reshape(NF, ND, npoints)
    flat_fields = fields.reshape(4, npoints)
    weighted = remap_weight[None, :, :] * flat_fields[:, None, :]
    returned = jnp.zeros((4, forcing.shape[1]), jnp.float32).at[:, source.reshape(-1)].add(weighted.reshape(4, -1))
    return (new_spectrum, returned)
```

```python
import math

import jax
import jax.numpy as jnp
import numpy as np
from jax import lax
from jax.experimental import pallas as pl
from jax.experimental.pallas import tpu as pltpu
from jax.sharding import PartitionSpec as P

G_ACC = 9.81
WATER_DENSITY = 1025.0
FREQ_LOW = 0.03453
FREQ_RATIO = 1.1
E_UNIT = 0.001
DT_SRC = 120.0
COURANT_MAX = 0.7
DISSIP_COEF = 2.33e-05
STEEP_PM = 0.00302
TOP_EXPONENT = 31.0

NF = 32
ND = 24
GS = 8
PTS = 2048
TILES = 64
CAP = 256
RIM = 128
EXT = PTS + 2 * RIM

F32 = jnp.float32
BF = jnp.bfloat16
I32 = jnp.int32

THETA = [(k + 0.5) * 2.0 * math.pi / ND for k in range(ND)]
COS = [math.cos(t) for t in THETA]
SIN = [math.sin(t) for t in THETA]

OMEGA, INV_C, WAVENUM, COURANT, INV_OMEGA, INV_ROOT, OMEGA_C = range(7)


def frequency_table():
    e = np.arange(NF, dtype=np.float64) * (TOP_EXPONENT / (NF - 1))
    omega = 2.0 * math.pi * FREQ_LOW * FREQ_RATIO**e
    speed = G_ACC / omega
    wavenum = omega * omega / G_ACC
    courant = COURANT_MAX * FREQ_RATIO ** (-e)
    rows = [omega, 1 / speed, wavenum, courant, 1 / omega, 1 / np.sqrt(wavenum), omega / speed]
    return np.stack(rows).astype(np.float32)


def direction_tiles():
    both = np.stack([np.array(COS), np.array(SIN)]).astype(np.float32)
    return np.broadcast_to(both[:, :, None], (2, ND, 128)).copy()


def lane_gather(block, index):
    return jnp.take_along_axis(block, index, axis=1, mode="promise_in_bounds")


def parts2(x):
    first = x.astype(BF)
    return first, (x - first.astype(F32)).astype(BF)


def parts3(x):
    first = x.astype(BF)
    rest = x - first.astype(F32)
    second = rest.astype(BF)
    return first, second, (rest - second.astype(F32)).astype(BF)


def outgoing_kernel(forcing_ref, rows_ref, out_ref):
    def eight_tiles(q, carry):
        d = pl.ds(pl.multiple_of(q * 8, 8), 8)
        for half in range(2):
            index = rows_ref[d, half * 128 : half * 128 + 128]
            low, high = index & 127, index >> 7
            for i in range(4):
                got = None
                for h in range(16):
                    block = jnp.broadcast_to(forcing_ref[i : i + 1, h * 128 : h * 128 + 128], (8, 128))
                    piece = lane_gather(block, low)
                    got = piece if h == 0 else jnp.where(high == h, piece, got)
                out_ref[d, 2 * i + half, :] = got
        return carry

    lax.fori_loop(0, TILES // 8, eight_tiles, 0)


def rim_kernel(spec_ref, list_ref, before_ref, after_ref):
    for side, out_ref in ((0, before_ref), (1, after_ref)):
        index = jnp.broadcast_to(list_ref[side : side + 1, :], (8, 128))
        low, high = index & 127, index >> 7

        def one_freq(i, carry):
            for g in range(3):
                got = None
                for h in range(16):
                    piece = lane_gather(spec_ref[i, 8 * g : 8 * g + 8, h * 128 : h * 128 + 128], low)
                    got = piece if h == 0 else jnp.where(high == h, piece, got)
                out_ref[i, 8 * g : 8 * g + 8, :] = got
            return carry

        lax.fori_loop(0, GS, one_freq, 0)


def weight_matrix(slot_ref, weight_ref, cols, width):
    slots = lax.broadcasted_iota(I32, (CAP, width), 0)
    total = None
    for j in range(4):
        index = slot_ref[j : j + 1, cols] & (CAP - 1)
        term = jnp.where(slots == index, weight_ref[j : j + 1, cols], 0.0)
        total = term if j == 0 else total + term
    return total, slot_ref[0:1, cols] >> 8


WB = 256


def wind_kernel(tab_ref, freq_ref, arrived_ref, slot_ref, weight_ref, spec_ref, dir_ref, wind_ref, mom_ref, left_ref):
    base = freq_ref[0] * GS
    for i in range(4):
        for half in range(2):
            p0, p1, p2 = parts3(arrived_ref[:, 2 * i + half, :])
            for n, part in enumerate((p0, p1, p2, p0, p1, p0)):
                left_ref[i * 64 : i * 64 + 64, n * 256 + half * 128 : n * 256 + half * 128 + 128] = part

    def block(c, carry):
        cols = pl.ds(pl.multiple_of(c * WB, WB), WB)
        weights, band = weight_matrix(slot_ref, weight_ref, cols, WB)
        w0, w1, w2 = parts3(weights)
        right = jnp.concatenate([w0, w0, w0, w1, w1, w2], axis=0)
        mixed = jnp.dot(left_ref[...], right, preferred_element_type=F32)
        mine = lax.broadcasted_iota(I32, (TILES, WB), 0) == band
        east, north, density, gust = (
            jnp.sum(jnp.where(mine, mixed[i * 64 : i * 64 + 64], 0.0), axis=0, keepdims=True) for i in range(4)
        )
        speed = jnp.sqrt(east * east + north * north + 1.0)
        friction = jnp.sqrt(0.001 * (0.8 + 0.065 * speed)) * speed * (1.0 + 0.15 * gust)
        pull = 28.0 * friction
        share = 0.25 * (density / WATER_DENSITY)
        spread = lambda v: jnp.broadcast_to(v, (8, WB))
        east8, north8, speed8, pull8 = spread(east), spread(north), spread(speed), spread(pull)
        m0 = jnp.zeros((8, WB), F32)
        ms, mk, sx, sy = m0, m0, m0, m0
        for g in range(3):
            cos8 = jnp.concatenate([dir_ref[0, 8 * g : 8 * g + 8, :]] * (WB // 128), axis=1)
            sin8 = jnp.concatenate([dir_ref[1, 8 * g : 8 * g + 8, :]] * (WB // 128), axis=1)
            push = pull8 * ((east8 * cos8 + north8 * sin8) / speed8)
            stress = jnp.zeros((8, WB), F32)
            for i in range(GS):
                spec = spec_ref[i, 8 * g : 8 * g + 8, cols]
                m0 = m0 + spec
                ms = ms + spec * tab_ref[INV_OMEGA, base + i]
                mk = mk + spec * tab_ref[INV_ROOT, base + i]
                excess = jnp.maximum(push * tab_ref[INV_C, base + i] - 1.0, 0.0)
                stress = stress + (excess * tab_ref[OMEGA_C, base + i]) * spec
            sx = sx + stress * cos8
            sy = sy + stress * sin8
        down = lambda v: jnp.sum(v, axis=0, keepdims=True)
        for n, row in enumerate((down(m0), down(ms), down(mk), down(sx) * share, down(sy) * share)):
            for half in range(WB // 128):
                mom_ref[pl.ds(n * 16 + c * (WB // 128) + half, 1), :] = row[:, half * 128 : half * 128 + 128]
        for n, row in enumerate((east, north, density, speed, friction)):
            for half in range(WB // 128):
                wind_ref[pl.ds(n * 16 + c * (WB // 128) + half, 1), :] = row[:, half * 128 : half * 128 + 128]
        return carry

    lax.fori_loop(0, PTS // WB, block, 0)


def field_kernel(freq_ref, m0_ref, m1_ref, m2_ref, m3_ref, wind_ref, slot_ref, weight_ref, diss_ref, sums_ref, own_ref):
    moments = m0_ref[...] + m1_ref[...] + m2_ref[...] + m3_ref[...]
    total, inv_sigma, inv_root, stress_e, stress_n = (moments[16 * n : 16 * n + 16] for n in range(5))
    east, north, density, speed, friction = (wind_ref[16 * n : 16 * n + 16, :] for n in range(5))
    mean_sigma = total / inv_sigma
    mean_wavenum = jnp.square(total / inv_root)
    steepness = mean_wavenum * mean_wavenum * total * E_UNIT
    diss_ref[...] = DISSIP_COEF * mean_sigma * jnp.square(steepness / STEEP_PM) / mean_wavenum
    scale = WATER_DENSITY / density * G_ACC * E_UNIT
    friction_sq = friction * friction
    east_ratio = scale * stress_e / friction_sq
    north_ratio = scale * stress_n / friction_sq
    aligned = (east_ratio * east + north_ratio * north) / speed
    charnock = 1.0 / jnp.sqrt(1.0 - 0.9 * aligned / (1.0 + jnp.abs(aligned)))
    height = 4.0 * jnp.sqrt(E_UNIT * total)
    f = freq_ref[0]
    own_ref[...] = jnp.where(f == 0, east_ratio, jnp.where(f == 1, north_ratio, jnp.where(f == 2, charnock, height)))

    def block(c, acc):
        cols = pl.ds(pl.multiple_of(c * WB, WB), WB)
        weights, band = weight_matrix(slot_ref, weight_ref, cols, WB)
        w0, w1 = parts2(weights)
        field = jnp.concatenate([own_ref[pl.ds(c * (WB // 128) + half, 1), :] for half in range(WB // 128)], axis=1)
        spread = jnp.where(lax.broadcasted_iota(I32, (TILES, WB), 0) == band, field, 0.0)
        f0, f1 = parts2(spread)
        left = jnp.concatenate([f0, f1, f0], axis=1)
        right = jnp.concatenate([w0, w0, w1], axis=1)
        return acc + lax.dot_general(left, right, (((1,), (1,)), ((), ())), preferred_element_type=F32)

    acc = lax.fori_loop(0, PTS // WB, block, jnp.zeros((TILES, CAP), F32))
    for half in range(2):
        sums_ref[:, half, :] = acc[:, half * 128 : half * 128 + 128]


def band_kernel(arrived_ref, rows_ref, out_ref):
    def eight_tiles(q, acc):
        ones, values = [], []
        for t in range(8):
            index = rows_ref[pl.ds(q * 8 + t, 1), :]
            tile = arrived_ref[q * 8 + t]
            row = jnp.concatenate([tile[0:1, :], tile[1:2, :]], axis=1)
            v0, v1 = parts2(row)
            high = lax.broadcasted_iota(I32, (16, CAP), 0) == (index >> 7)
            v0, v1 = v0.astype(F32), v1.astype(F32)
            values.append(jnp.concatenate([jnp.where(high, v0, 0.0), jnp.where(high, v1, 0.0)], axis=0).astype(BF))
            ones.append((lax.broadcasted_iota(I32, (128, CAP), 0) == (index & 127)).astype(F32).astype(BF))
        left = jnp.concatenate(ones, axis=1)
        right = jnp.concatenate(values, axis=1)
        return acc + lax.dot_general(left, right, (((1,), (1,)), ((), ())), preferred_element_type=F32)

    acc = lax.fori_loop(0, TILES // 8, eight_tiles, jnp.zeros((128, 32), F32))
    out_ref[...] = jnp.transpose(acc[:, :16] + acc[:, 16:])


ROLL = 6
KCOPIES = 30
NB = 512


def move_kernel(tab_ref, freq_ref, spec_ref, low_ref, high_ref, near_ref, out_ref, x_ref):
    base = freq_ref[0] * GS

    def put(ref, source, target):
        for kp in range(KCOPIES):
            k = (kp + ND - ROLL) % ND
            v = ref[:, k, source]
            p0 = v.astype(BF).astype(F32)
            x_ref[kp * 16 : kp * 16 + 16, target] = jnp.concatenate([p0, v - p0], axis=0).astype(BF)

    put(low_ref, slice(0, 128), slice(0, 128))
    put(high_ref, slice(0, 128), slice(EXT - 128, EXT))

    def put_block(h, carry):
        put(spec_ref, pl.ds(pl.multiple_of(h * 128, 128), 128), pl.ds(pl.multiple_of(h * 128 + 128, 128), 128))
        return carry

    lax.fori_loop(0, PTS // 128, put_block, 0)
    which = lax.broadcasted_iota(I32, (8, NB), 0)
    courant = jnp.zeros((8, NB), F32)
    for i in range(GS):
        courant = jnp.where(which == i, tab_ref[COURANT, base + i], courant)

    def block(c, carry):
        cols = pl.ds(pl.multiple_of(c * NB, NB), NB)
        got = []
        for n, first in enumerate((0, 12, 6, 18)):
            index = near_ref[n : n + 1, cols].astype(jnp.int16)
            hot = jnp.where(
                lax.broadcasted_iota(jnp.int16, (EXT, NB), 0) == index, jnp.ones((), BF), jnp.zeros((), BF)
            )
            got.append(jnp.dot(x_ref[first * 16 : first * 16 + 192, :], hot, preferred_element_type=F32))
        for k in range(ND):
            a = (k + ROLL) % ND
            x_of = got[0] if a < 12 else got[1]
            a = a % 12
            y_of = got[2] if k < 12 else got[3]
            b = k % 12
            from_x = x_of[a * 16 : a * 16 + 8] + x_of[a * 16 + 8 : a * 16 + 16]
            from_y = y_of[b * 16 : b * 16 + 8] + y_of[b * 16 + 8 : b * 16 + 16]
            spec = spec_ref[:, k, cols]
            out_ref[:, k, cols] = (
                spec - (courant * abs(COS[k])) * (spec - from_x) - (courant * abs(SIN[k])) * (spec - from_y)
            )
        return carry

    lax.fori_loop(0, PTS // NB, block, 0)


def source_kernel(tab_ref, freq_ref, moved_ref, wind_ref, diss_ref, dir_ref, out_ref):
    base = freq_ref[0] * GS + pl.program_id(0) * 2

    def block(c, carry):
        cols = pl.ds(pl.multiple_of(c * 128, 128), 128)
        row = lambda n: jnp.broadcast_to(wind_ref[pl.ds(n * 16 + c, 1), :], (8, 128))
        east, north, density, speed, friction = (row(n) for n in range(5))
        loss = jnp.broadcast_to(diss_ref[pl.ds(c, 1), :], (8, 128))
        share = 0.25 * (density / WATER_DENSITY)
        pull = 28.0 * friction / speed
        for g in range(3):
            push = pull * (east * dir_ref[0, 8 * g : 8 * g + 8, :] + north * dir_ref[1, 8 * g : 8 * g + 8, :])
            for i in range(2):
                excess = jnp.maximum(push * tab_ref[INV_C, base + i] - 1.0, 0.0)
                growth = share * excess * tab_ref[OMEGA, base + i] - loss * tab_ref[WAVENUM, base + i]
                out_ref[i, 8 * g : 8 * g + 8, cols] = moved_ref[i, 8 * g : 8 * g + 8, cols] * jnp.exp(DT_SRC * growth)
        return carry

    lax.fori_loop(0, PTS // 128, block, 0)


SMEM = pl.BlockSpec(memory_space=pltpu.SMEM)
VMEM = pl.BlockSpec(memory_space=pltpu.VMEM)


def params(mib):
    return pltpu.CompilerParams(vmem_limit_bytes=mib * 2**20)


def shape(*dims):
    return jax.ShapeDtypeStruct(dims, F32)


def on_device(spectrum, forcing, send_rows, point_slot, remap_weight, neighbours, halo_send):
    table = jnp.asarray(frequency_table())
    dirs = jnp.asarray(direction_tiles())
    freq = lax.axis_index("freq").astype(I32).reshape(1)

    outgoing = pl.pallas_call(
        outgoing_kernel, out_shape=shape(TILES, 8, 128), name="outgoing", compiler_params=params(16)
    )(forcing, send_rows)
    arrived = lax.all_to_all(outgoing, "tile", split_axis=0, concat_axis=0, tiled=True)

    to_before, to_after = pl.pallas_call(
        rim_kernel, out_shape=(shape(GS, ND, RIM), shape(GS, ND, RIM)), name="rims", compiler_params=params(16)
    )(spectrum, halo_send.reshape(2, RIM))
    up = [(d, d + 1) for d in range(TILES - 1)]
    low_rim = lax.ppermute(to_after, "tile", up)
    high_rim = lax.ppermute(to_before, "tile", [(b, a) for a, b in up])

    moved = pl.pallas_call(
        move_kernel,
        out_shape=shape(GS, ND, PTS),
        in_specs=[SMEM, SMEM, VMEM, VMEM, VMEM, VMEM],
        scratch_shapes=[pltpu.VMEM((KCOPIES * 16, EXT), BF)],
        name="move",
        compiler_params=params(48),
    )(table, freq, spectrum, low_rim, high_rim, neighbours)

    wind, moments = pl.pallas_call(
        wind_kernel,
        out_shape=(shape(80, 128), shape(80, 128)),
        in_specs=[SMEM, SMEM] + [VMEM] * 5,
        scratch_shapes=[pltpu.VMEM((256, 6 * 256), BF)],
        name="wind",
        compiler_params=params(32),
    )(table, freq, arrived, point_slot, remap_weight, spectrum, dirs)
    others = [lax.ppermute(moments, "freq", [(i, (i + n) % 4) for i in range(4)]) for n in (1, 2, 3)]

    diss, slot_sums = pl.pallas_call(
        field_kernel,
        out_shape=(shape(16, 128), shape(TILES, 2, 128)),
        in_specs=[SMEM] + [VMEM] * 7,
        scratch_shapes=[pltpu.VMEM((16, 128), F32)],
        name="fields",
        compiler_params=params(32),
    )(freq, moments, *others, wind, point_slot, remap_weight)
    arrived_sums = lax.all_to_all(slot_sums, "tile", split_axis=0, concat_axis=0, tiled=True)

    whole = lambda s: (0, 0)
    new_spectrum = pl.pallas_call(
        source_kernel,
        out_shape=shape(GS, ND, PTS),
        grid=(GS // 2,),
        in_specs=[
            SMEM,
            SMEM,
            pl.BlockSpec((2, ND, PTS), lambda s: (s, 0, 0)),
            pl.BlockSpec((80, 128), whole),
            pl.BlockSpec((16, 128), whole),
            pl.BlockSpec((2, ND, 128), lambda s: (0, 0, 0)),
        ],
        out_specs=pl.BlockSpec((2, ND, PTS), lambda s: (s, 0, 0)),
        name="source",
        compiler_params=params(16),
    )(table, freq, moved, wind, diss, dirs)

    returned = pl.pallas_call(
        band_kernel, out_shape=shape(16, 128), name="band", compiler_params=params(32)
    )(arrived_sums, send_rows)
    return (new_spectrum, returned.reshape(1, PTS))


def solution(mesh):
    placed = (
        P("freq", None, "tile"),
        P(None, "tile"),
        P("tile", None),
        P(None, "tile"),
        P(None, "tile"),
        P(None, "tile"),
        P("tile"),
    )
    return jax.shard_map(
        on_device,
        mesh=mesh,
        in_specs=placed,
        out_specs=(P("freq", None, "tile"), P("freq", "tile")),
        check_vma=False,
    )
```

```python
import math

import jax
import jax.numpy as jnp
import numpy as np
from jax import lax
from jax.experimental import pallas as pl
from jax.experimental.pallas import tpu as pltpu
from jax.sharding import PartitionSpec as P

G_ACC = 9.81
WATER_DENSITY = 1025.0
FREQ_LOW = 0.03453
FREQ_RATIO = 1.1
E_UNIT = 0.001
DT_SRC = 120.0
COURANT_MAX = 0.7
DISSIP_COEF = 2.33e-05
STEEP_PM = 0.00302
TOP_EXPONENT = 31.0

NF = 32
ND = 24
GS = 8
PTS = 2048
TILES = 64
CAP = 256
RIM = 128
EXT = PTS + 2 * RIM

F32 = jnp.float32
BF = jnp.bfloat16
I32 = jnp.int32

THETA = [(k + 0.5) * 2.0 * math.pi / ND for k in range(ND)]
COS = [math.cos(t) for t in THETA]
SIN = [math.sin(t) for t in THETA]

OMEGA, INV_C, WAVENUM, COURANT, INV_OMEGA, INV_ROOT, OMEGA_C = range(7)


def frequency_table():
    e = np.arange(NF, dtype=np.float64) * (TOP_EXPONENT / (NF - 1))
    omega = 2.0 * math.pi * FREQ_LOW * FREQ_RATIO**e
    speed = G_ACC / omega
    wavenum = omega * omega / G_ACC
    courant = COURANT_MAX * FREQ_RATIO ** (-e)
    rows = [omega, 1 / speed, wavenum, courant, 1 / omega, 1 / np.sqrt(wavenum), omega / speed]
    return np.stack(rows).astype(np.float32)


def direction_tiles():
    both = np.stack([np.array(COS), np.array(SIN)]).astype(np.float32)
    return np.broadcast_to(both[:, :, None], (2, ND, 128)).copy()


def lane_gather(block, index):
    return jnp.take_along_axis(block, index, axis=1, mode="promise_in_bounds")


def parts2(x):
    first = x.astype(BF)
    return first, (x - first.astype(F32)).astype(BF)


def parts3(x):
    first = x.astype(BF)
    rest = x - first.astype(F32)
    second = rest.astype(BF)
    return first, second, (rest - second.astype(F32)).astype(BF)


def outgoing_kernel(forcing_ref, rows_ref, out_ref):
    def eight_tiles(q, carry):
        d = pl.ds(pl.multiple_of(q * 8, 8), 8)
        for half in range(2):
            index = rows_ref[d, half * 128 : half * 128 + 128]
            low, high = index & 127, index >> 7
            for i in range(4):
                got = None
                for h in range(16):
                    block = jnp.broadcast_to(forcing_ref[i : i + 1, h * 128 : h * 128 + 128], (8, 128))
                    piece = lane_gather(block, low)
                    got = piece if h == 0 else jnp.where(high == h, piece, got)
                out_ref[d, 2 * i + half, :] = got
        return carry

    lax.fori_loop(0, TILES // 8, eight_tiles, 0)


def rim_kernel(spec_ref, list_ref, before_ref, after_ref):
    for side, out_ref in ((0, before_ref), (1, after_ref)):
        index = jnp.broadcast_to(list_ref[side : side + 1, :], (8, 128))
        low, high = index & 127, index >> 7

        def one_freq(i, carry):
            for g in range(3):
                got = None
                for h in range(16):
                    piece = lane_gather(spec_ref[i, 8 * g : 8 * g + 8, h * 128 : h * 128 + 128], low)
                    got = piece if h == 0 else jnp.where(high == h, piece, got)
                out_ref[i, 8 * g : 8 * g + 8, :] = got
            return carry

        lax.fori_loop(0, GS, one_freq, 0)


def weight_matrix(slot_ref, weight_ref, cols, width):
    slots = lax.broadcasted_iota(I32, (CAP, width), 0)
    total = None
    for j in range(4):
        index = slot_ref[j : j + 1, cols] & (CAP - 1)
        term = jnp.where(slots == index, weight_ref[j : j + 1, cols], 0.0)
        total = term if j == 0 else total + term
    return total, slot_ref[0:1, cols] >> 8


WB = 256


def wind_kernel(tab_ref, freq_ref, arrived_ref, slot_ref, weight_ref, spec_ref, dir_ref, wind_ref, mom_ref, left_ref):
    base = freq_ref[0] * GS
    for i in range(4):
        for half in range(2):
            p0, p1, p2 = parts3(arrived_ref[:, 2 * i + half, :])
            for n, part in enumerate((p0, p1, p2, p0, p1, p0)):
                left_ref[i * 64 : i * 64 + 64, n * 256 + half * 128 : n * 256 + half * 128 + 128] = part

    def block(c, carry):
        cols = pl.ds(pl.multiple_of(c * WB, WB), WB)
        weights, band = weight_matrix(slot_ref, weight_ref, cols, WB)
        w0, w1, w2 = parts3(weights)
        right = jnp.concatenate([w0, w0, w0, w1, w1, w2], axis=0)
        mixed = jnp.dot(left_ref[...], right, preferred_element_type=F32)
        mine = lax.broadcasted_iota(I32, (TILES, WB), 0) == band
        east, north, density, gust = (
            jnp.sum(jnp.where(mine, mixed[i * 64 : i * 64 + 64], 0.0), axis=0, keepdims=True) for i in range(4)
        )
        speed = jnp.sqrt(east * east + north * north + 1.0)
        friction = jnp.sqrt(0.001 * (0.8 + 0.065 * speed)) * speed * (1.0 + 0.15 * gust)
        pull = 28.0 * friction
        share = 0.25 * (density / WATER_DENSITY)
        spread = lambda v: jnp.broadcast_to(v, (8, WB))
        east8, north8, speed8, pull8 = spread(east), spread(north), spread(speed), spread(pull)
        m0 = jnp.zeros((8, WB), F32)
        ms, mk, sx, sy = m0, m0, m0, m0
        for g in range(3):
            cos8 = jnp.concatenate([dir_ref[0, 8 * g : 8 * g + 8, :]] * (WB // 128), axis=1)
            sin8 = jnp.concatenate([dir_ref[1, 8 * g : 8 * g + 8, :]] * (WB // 128), axis=1)
            push = pull8 * ((east8 * cos8 + north8 * sin8) / speed8)
            stress = jnp.zeros((8, WB), F32)
            for i in range(GS):
                spec = spec_ref[i, 8 * g : 8 * g + 8, cols]
                m0 = m0 + spec
                ms = ms + spec * tab_ref[INV_OMEGA, base + i]
                mk = mk + spec * tab_ref[INV_ROOT, base + i]
                excess = jnp.maximum(push * tab_ref[INV_C, base + i] - 1.0, 0.0)
                stress = stress + (excess * tab_ref[OMEGA_C, base + i]) * spec
            sx = sx + stress * cos8
            sy = sy + stress * sin8
        down = lambda v: jnp.sum(v, axis=0, keepdims=True)
        for n, row in enumerate((down(m0), down(ms), down(mk), down(sx) * share, down(sy) * share)):
            for half in range(WB // 128):
                mom_ref[pl.ds(n * 16 + c * (WB // 128) + half, 1), :] = row[:, half * 128 : half * 128 + 128]
        for n, row in enumerate((east, north, density, speed, friction)):
            for half in range(WB // 128):
                wind_ref[pl.ds(n * 16 + c * (WB // 128) + half, 1), :] = row[:, half * 128 : half * 128 + 128]
        return carry

    lax.fori_loop(0, PTS // WB, block, 0)


def field_kernel(freq_ref, m0_ref, m1_ref, m2_ref, m3_ref, wind_ref, slot_ref, weight_ref, diss_ref, sums_ref, own_ref):
    moments = m0_ref[...] + m1_ref[...] + m2_ref[...] + m3_ref[...]
    total, inv_sigma, inv_root, stress_e, stress_n = (moments[16 * n : 16 * n + 16] for n in range(5))
    east, north, density, speed, friction = (wind_ref[16 * n : 16 * n + 16, :] for n in range(5))
    mean_sigma = total / inv_sigma
    mean_wavenum = jnp.square(total / inv_root)
    steepness = mean_wavenum * mean_wavenum * total * E_UNIT
    diss_ref[...] = DISSIP_COEF * mean_sigma * jnp.square(steepness / STEEP_PM) / mean_wavenum
    scale = WATER_DENSITY / density * G_ACC * E_UNIT
    friction_sq = friction * friction
    east_ratio = scale * stress_e / friction_sq
    north_ratio = scale * stress_n / friction_sq
    aligned = (east_ratio * east + north_ratio * north) / speed
    charnock = 1.0 / jnp.sqrt(1.0 - 0.9 * aligned / (1.0 + jnp.abs(aligned)))
    height = 4.0 * jnp.sqrt(E_UNIT * total)
    f = freq_ref[0]
    own_ref[...] = jnp.where(f == 0, east_ratio, jnp.where(f == 1, north_ratio, jnp.where(f == 2, charnock, height)))

    def block(c, acc):
        cols = pl.ds(pl.multiple_of(c * WB, WB), WB)
        weights, band = weight_matrix(slot_ref, weight_ref, cols, WB)
        w0, w1 = parts2(weights)
        field = jnp.concatenate([own_ref[pl.ds(c * (WB // 128) + half, 1), :] for half in range(WB // 128)], axis=1)
        spread = jnp.where(lax.broadcasted_iota(I32, (TILES, WB), 0) == band, field, 0.0)
        f0, f1 = parts2(spread)
        left = jnp.concatenate([f0, f1, f0], axis=1)
        right = jnp.concatenate([w0, w0, w1], axis=1)
        return acc + lax.dot_general(left, right, (((1,), (1,)), ((), ())), preferred_element_type=F32)

    acc = lax.fori_loop(0, PTS // WB, block, jnp.zeros((TILES, CAP), F32))
    for half in range(2):
        sums_ref[:, half, :] = acc[:, half * 128 : half * 128 + 128]


def band_kernel(arrived_ref, rows_ref, out_ref):
    def eight_tiles(q, acc):
        ones, values = [], []
        for t in range(8):
            index = rows_ref[pl.ds(q * 8 + t, 1), :]
            tile = arrived_ref[q * 8 + t]
            row = jnp.concatenate([tile[0:1, :], tile[1:2, :]], axis=1)
            v0, v1 = parts2(row)
            high = lax.broadcasted_iota(I32, (16, CAP), 0) == (index >> 7)
            v0, v1 = v0.astype(F32), v1.astype(F32)
            values.append(jnp.concatenate([jnp.where(high, v0, 0.0), jnp.where(high, v1, 0.0)], axis=0).astype(BF))
            ones.append((lax.broadcasted_iota(I32, (128, CAP), 0) == (index & 127)).astype(F32).astype(BF))
        left = jnp.concatenate(ones, axis=1)
        right = jnp.concatenate(values, axis=1)
        return acc + lax.dot_general(left, right, (((1,), (1,)), ((), ())), preferred_element_type=F32)

    acc = lax.fori_loop(0, TILES // 8, eight_tiles, jnp.zeros((128, 32), F32))
    out_ref[...] = jnp.transpose(acc[:, :16] + acc[:, 16:])


ROLL = 6
KCOPIES = 30
NB = 512
HALF = PTS // 2


def put_parts(ref, source, x_ref, target):
    for kp in range(KCOPIES):
        v = ref[:, (kp + ND - ROLL) % ND, source]
        p0 = v.astype(BF).astype(F32)
        x_ref[kp * 16 : kp * 16 + 16, target] = jnp.concatenate([p0, v - p0], axis=0).astype(BF)


def operand_kernel(spec_ref, x_ref):
    def put_block(h, carry):
        cols = pl.ds(pl.multiple_of(h * 128, 128), 128)
        put_parts(spec_ref, cols, x_ref, cols)
        return carry

    lax.fori_loop(0, PTS // 128, put_block, 0)


def move_kernel(start, tab_ref, freq_ref, spec_ref, x_ref, low_ref, high_ref, near_ref, out_ref, rim_ref):
    base = freq_ref[0] * GS
    put_parts(low_ref, slice(0, RIM), rim_ref, slice(0, RIM))
    put_parts(high_ref, slice(0, RIM), rim_ref, slice(RIM, 2 * RIM))
    which = lax.broadcasted_iota(I32, (8, NB), 0)
    courant = jnp.zeros((8, NB), F32)
    for i in range(GS):
        courant = jnp.where(which == i, tab_ref[COURANT, base + i], courant)

    def hot(rows, index):
        match = lax.broadcasted_iota(jnp.int16, (rows, NB), 0) == index
        return jnp.where(match, jnp.ones((), BF), jnp.zeros((), BF))

    def block(c, carry):
        cols = pl.ds(pl.multiple_of(start + c * NB, NB), NB)
        outs = pl.ds(pl.multiple_of(c * NB, NB), NB)
        got = []
        for n, first in enumerate((0, 12, 6, 18)):
            index = near_ref[n : n + 1, cols]
            rim_index = jnp.where(index < RIM, index, jnp.where(index < RIM + PTS, 2 * RIM, index - PTS))
            rows = slice(first * 16, first * 16 + 192)
            own = jnp.dot(x_ref[rows, :], hot(PTS, (index - RIM).astype(jnp.int16)), preferred_element_type=F32)
            rim = jnp.dot(rim_ref[rows, :], hot(2 * RIM, rim_index.astype(jnp.int16)), preferred_element_type=F32)
            got.append(own + rim)
        for k in range(ND):
            a = (k + ROLL) % ND
            x_of = got[0] if a < 12 else got[1]
            a = a % 12
            y_of = got[2] if k < 12 else got[3]
            b = k % 12
            from_x = x_of[a * 16 : a * 16 + 8] + x_of[a * 16 + 8 : a * 16 + 16]
            from_y = y_of[b * 16 : b * 16 + 8] + y_of[b * 16 + 8 : b * 16 + 16]
            spec = spec_ref[:, k, cols]
            out_ref[:, k, outs] = (
                spec - (courant * abs(COS[k])) * (spec - from_x) - (courant * abs(SIN[k])) * (spec - from_y)
            )
        return carry

    lax.fori_loop(0, HALF // NB, block, 0)


def source_kernel(tab_ref, freq_ref, moved0_ref, moved1_ref, wind_ref, diss_ref, dir_ref, out_ref, new_ref, sems):
    base = freq_ref[0] * GS
    copies = [pltpu.make_async_copy(new_ref.at[i], out_ref.at[i], sems.at[i]) for i in range(GS)]
    for i in range(GS):

        def block(c, carry):
            cols = pl.ds(pl.multiple_of(c * 128, 128), 128)
            for part, moved_ref in ((0, moved0_ref), (1, moved1_ref)):
                at = c + part * (HALF // 128)
                row = lambda n: jnp.broadcast_to(wind_ref[pl.ds(n * 16 + at, 1), :], (8, 128))
                east, north, density, speed, friction = (row(n) for n in range(5))
                loss = jnp.broadcast_to(diss_ref[pl.ds(at, 1), :], (8, 128))
                share = 0.25 * (density / WATER_DENSITY)
                pull = 28.0 * friction / speed
                to = pl.ds(pl.multiple_of(part * HALF + c * 128, 128), 128)
                for g in range(3):
                    rows = slice(8 * g, 8 * g + 8)
                    push = pull * (east * dir_ref[0, rows, :] + north * dir_ref[1, rows, :])
                    excess = jnp.maximum(push * tab_ref[INV_C, base + i] - 1.0, 0.0)
                    growth = share * excess * tab_ref[OMEGA, base + i] - loss * tab_ref[WAVENUM, base + i]
                    new_ref[i, rows, to] = moved_ref[i, rows, cols] * jnp.exp(DT_SRC * growth)
            return carry

        lax.fori_loop(0, HALF // 128, block, 0)
        copies[i].start()
    for copy in copies:
        copy.wait()


SMEM = pl.BlockSpec(memory_space=pltpu.SMEM)
VMEM = pl.BlockSpec(memory_space=pltpu.VMEM)
ANY = pl.BlockSpec(memory_space=pl.ANY)


def array(*dims, dtype=F32):
    return jax.ShapeDtypeStruct(dims, dtype)


def call(body, name, out, specs, scratch=(), mib=16, microseconds=1.0, out_specs=None, behind=False, mark=False):
    out = list(out)
    out_specs = [VMEM] * len(out) if out_specs is None else list(out_specs)
    specs = [*specs, VMEM] if behind else specs
    inputs = len(specs) - behind
    outputs = len(out)
    if mark:
        out.append(array(8, 128))
        out_specs.append(VMEM)

    def kernel(*refs):
        results = inputs + behind
        if mark:
            refs[results + outputs][...] = jnp.zeros((8, 128), F32)
        body(*refs[:inputs], *refs[results : results + outputs], *refs[results + outputs + mark :])

    cost = pl.CostEstimate(flops=0, bytes_accessed=int(microseconds * 3.0e6), transcendentals=0)
    return pl.pallas_call(
        kernel,
        out_shape=out,
        in_specs=specs,
        out_specs=out_specs,
        scratch_shapes=list(scratch),
        name=name,
        cost_estimate=cost,
        compiler_params=pltpu.CompilerParams(vmem_limit_bytes=mib * 2**20),
    )


def on_device(spectrum, forcing, send_rows, point_slot, remap_weight, neighbours, halo_send):
    table = jnp.asarray(frequency_table())
    dirs = jnp.asarray(direction_tiles())
    freq = lax.axis_index("freq").astype(I32).reshape(1)

    outgoing, mark = call(
        outgoing_kernel, "outgoing", [array(TILES, 8, 128)], [VMEM] * 2, microseconds=2.4, mark=True
    )(forcing, send_rows)
    arrived = lax.all_to_all(outgoing, "tile", split_axis=0, concat_axis=0, tiled=True)

    to_before, to_after, mark = call(
        rim_kernel, "rims", [array(GS, ND, RIM)] * 2, [VMEM] * 2, microseconds=1.9, behind=True, mark=True
    )(spectrum, halo_send.reshape(2, RIM), mark)
    up = [(d, d + 1) for d in range(TILES - 1)]
    low_rim = lax.ppermute(to_after, "tile", up)
    high_rim = lax.ppermute(to_before, "tile", [(b, a) for a, b in up])
    operand, mark = call(
        operand_kernel,
        "operand",
        [array(KCOPIES * 16, PTS, dtype=BF)],
        [VMEM],
        microseconds=3.0,
        behind=True,
        mark=True,
    )(spectrum, mark)

    def move(half, mark):
        return call(
            lambda *refs: move_kernel(half * HALF, *refs),
            f"move{half}",
            [array(GS, ND, HALF)],
            [SMEM, SMEM] + [VMEM] * 5,
            [pltpu.VMEM((KCOPIES * 16, 2 * RIM), BF)],
            mib=24,
            microseconds=5.0,
            behind=True,
            mark=True,
        )(table, freq, spectrum, operand, low_rim, high_rim, neighbours, mark)

    moved0, mark = move(0, mark)
    wind, moments, mark = call(
        wind_kernel,
        "wind",
        [array(80, 128), array(80, 128)],
        [SMEM, SMEM] + [VMEM] * 5,
        [pltpu.VMEM((256, 6 * 256), BF)],
        mib=16,
        microseconds=6.0,
        behind=True,
        mark=True,
    )(table, freq, arrived, point_slot, remap_weight, spectrum, dirs, mark)
    others = [lax.ppermute(moments, "freq", [(i, (i + n) % 4) for i in range(4)]) for n in (1, 2, 3)]
    moved1, mark = move(1, mark)

    diss, slot_sums = call(
        field_kernel,
        "fields",
        [array(16, 128), array(TILES, 2, 128)],
        [SMEM] + [VMEM] * 7,
        [pltpu.VMEM((16, 128), F32)],
        mib=16,
        microseconds=3.0,
        behind=True,
    )(freq, moments, *others, wind, point_slot, remap_weight, mark)
    arrived_sums = lax.all_to_all(slot_sums, "tile", split_axis=0, concat_axis=0, tiled=True)

    new_spectrum, mark = call(
        source_kernel,
        "source",
        [array(GS, ND, PTS)],
        [SMEM, SMEM] + [VMEM] * 5,
        [pltpu.VMEM((GS, ND, PTS), F32), pltpu.SemaphoreType.DMA((GS,))],
        microseconds=3.0,
        out_specs=[ANY],
        mark=True,
    )(table, freq, moved0, moved1, wind, diss, dirs)

    (returned,) = call(
        band_kernel, "band", [array(16, 128)], [VMEM] * 2, mib=16, microseconds=2.5, behind=True
    )(arrived_sums, send_rows, mark)
    return (new_spectrum, returned.reshape(1, PTS))


def solution(mesh):
    placed = (
        P("freq", None, "tile"),
        P(None, "tile"),
        P("tile", None),
        P(None, "tile"),
        P(None, "tile"),
        P(None, "tile"),
        P("tile"),
    )
    return jax.shard_map(
        on_device,
        mesh=mesh,
        in_specs=placed,
        out_specs=(P("freq", None, "tile"), P("freq", "tile")),
        check_vma=False,
    )
```

```python
import functools
import math

import jax
import jax.numpy as jnp
from jax import lax
from jax.experimental import pallas as pl
from jax.experimental.pallas import tpu as pltpu
from jax.sharding import PartitionSpec as P

G_ACC = 9.81
WATER_DENSITY = 1025.0
FREQ_LOW = 0.03453
FREQ_RATIO = 1.1
E_UNIT = 0.001
DT_SRC = 120.0
COURANT_MAX = 0.7
DISSIP_COEF = 2.33e-05
STEEP_PM = 0.00302
TOP_EXPONENT = 31.0

NF = 32
ND = 24
GS = 8
PTS = 2048
TILES = 64
CAP = 256
RIM = 128
EXT = PTS + 2 * RIM

F32 = jnp.float32
BF = jnp.bfloat16
I32 = jnp.int32

THETA = [(k + 0.5) * 2.0 * math.pi / ND for k in range(ND)]
COS = [math.cos(t) for t in THETA]
SIN = [math.sin(t) for t in THETA]

OMEGA = [2.0 * math.pi * FREQ_LOW * FREQ_RATIO**i for i in range(GS)]
COURANT = [COURANT_MAX * FREQ_RATIO ** (-i) for i in range(GS)]


def group_scale():
    f = lax.axis_index("freq")
    pick = lambda v: jnp.where(f == 0, v[0], jnp.where(f == 1, v[1], jnp.where(f == 2, v[2], v[3]))).astype(F32)
    return pick([FREQ_RATIO ** (GS * n) for n in range(4)]), pick([FREQ_RATIO ** (-GS * n) for n in range(4)])


def by_sublane(values):
    which = lax.broadcasted_iota(I32, (8, 128), 0)
    tile = jnp.full((8, 128), values[7], F32)
    for n in range(7):
        tile = jnp.where(which == n, values[n], tile)
    return tile


def direction_tiles(values):
    return [by_sublane(values[8 * g : 8 * g + 8]) for g in range(3)]


def lane_gather(block, index):
    return jnp.take_along_axis(block, index, axis=1, mode="promise_in_bounds")


def parts2(x):
    first = x.astype(BF)
    return first, (x - first.astype(F32)).astype(BF)


def parts3(x):
    first = x.astype(BF)
    rest = x - first.astype(F32)
    second = rest.astype(BF)
    return first, second, (rest - second.astype(F32)).astype(BF)


ROLL = 6
KCOPIES = 30
NB = 512
HALF = PTS // 2
MOVE_SEMS = 10


def put_parts(ref, source, x_ref, target):
    for kp in range(KCOPIES):
        v = ref[:, (kp + ND - ROLL) % ND, source]
        p0 = v.astype(BF).astype(F32)
        x_ref[kp * 16 : kp * 16 + 16, target] = jnp.concatenate([p0, v - p0], axis=0).astype(BF)


def first_kernel(
    forcing_hbm, rows_hbm, list_hbm, spec_hbm, out_hbm, before_ref, after_ref, x_ref,
    forcing_ref, rows_ref, list_ref, spec_ref, out_ref, sems, out_sems,
):
    pairs = ((rows_hbm, rows_ref), (forcing_hbm, forcing_ref), (list_hbm, list_ref), (spec_hbm, spec_ref))
    copies = [pltpu.make_async_copy(src, dst, sems.at[n]) for n, (src, dst) in enumerate(pairs)]
    for copy in copies:
        copy.start()
    for copy in copies:
        copy.wait()
    rims = []
    for side, rim_ref in ((0, before_ref), (1, after_ref)):
        index = jnp.broadcast_to(list_ref[side : side + 1, :], (8, 128))
        rims.append((index & 127, index >> 7, rim_ref))

    def step(q, carry):
        d = pl.ds(pl.multiple_of(q * 8, 8), 8)
        for half in range(2):
            index = rows_ref[d, half * 128 : half * 128 + 128]
            low, high = index & 127, index >> 7
            for i in range(4):
                got = None
                for h in range(16):
                    block = jnp.broadcast_to(forcing_ref[i : i + 1, h * 128 : h * 128 + 128], (8, 128))
                    piece = lane_gather(block, low)
                    got = piece if h == 0 else jnp.where(high == h, piece, got)
                out_ref[d, 2 * i + half, :] = got
        pltpu.make_async_copy(out_ref.at[d], out_hbm.at[d], out_sems.at[q]).start()
        for low, high, rim_ref in rims:
            for g in range(3):
                rows = slice(8 * g, 8 * g + 8)
                got = None
                for h in range(16):
                    piece = lane_gather(spec_ref[q, rows, h * 128 : h * 128 + 128], low)
                    got = piece if h == 0 else jnp.where(high == h, piece, got)
                rim_ref[q, rows, :] = got
        for half in range(2):
            cols = pl.ds(pl.multiple_of(q * 256 + half * 128, 128), 128)
            put_parts(spec_ref, cols, x_ref, cols)
        return carry

    lax.fori_loop(0, TILES // 8, step, 0)
    for q in range(TILES // 8):
        d = pl.ds(q * 8, 8)
        pltpu.make_async_copy(out_ref.at[d], out_hbm.at[d], out_sems.at[q]).wait()


def weight_matrix(slot_ref, weight_ref, cols, width):
    slots = lax.broadcasted_iota(I32, (CAP, width), 0)
    total = None
    for j in range(4):
        index = slot_ref[j : j + 1, cols] & (CAP - 1)
        term = jnp.where(slots == index, weight_ref[j : j + 1, cols], 0.0)
        total = term if j == 0 else total + term
    return total, slot_ref[0:1, cols] >> 8


WB = 256


def wind_kernel(
    arrived_ref, slot_hbm, weight_hbm, spec_ref, wind_ref, mom_ref, left_ref, slot_ref, weight_ref, sems
):
    copies = [
        pltpu.make_async_copy(slot_hbm, slot_ref, sems.at[0]),
        pltpu.make_async_copy(weight_hbm, weight_ref, sems.at[1]),
    ]
    for copy in copies:
        copy.start()
    up, down_scale = group_scale()
    inv_c = [w / G_ACC * up for w in OMEGA]
    inv_omega = [1.0 / w * down_scale for w in OMEGA]
    inv_root = [math.sqrt(G_ACC) / w * down_scale for w in OMEGA]
    omega_c = [w * w / G_ACC * (up * up) for w in OMEGA]
    cos_tiles = [jnp.concatenate([t] * (WB // 128), axis=1) for t in direction_tiles(COS)]
    sin_tiles = [jnp.concatenate([t] * (WB // 128), axis=1) for t in direction_tiles(SIN)]
    for i in range(4):
        for half in range(2):
            p0, p1, p2 = parts3(arrived_ref[:, 2 * i + half, :])
            for n, part in enumerate((p0, p1, p2, p0, p1, p0)):
                left_ref[i * 64 : i * 64 + 64, n * 256 + half * 128 : n * 256 + half * 128 + 128] = part

    for copy in copies:
        copy.wait()

    def block(c, carry):
        cols = pl.ds(pl.multiple_of(c * WB, WB), WB)
        weights, band = weight_matrix(slot_ref, weight_ref, cols, WB)
        w0, w1, w2 = parts3(weights)
        right = jnp.concatenate([w0, w0, w0, w1, w1, w2], axis=0)
        mixed = jnp.dot(left_ref[...], right, preferred_element_type=F32)
        mine = lax.broadcasted_iota(I32, (TILES, WB), 0) == band
        east, north, density, gust = (
            jnp.sum(jnp.where(mine, mixed[i * 64 : i * 64 + 64], 0.0), axis=0, keepdims=True) for i in range(4)
        )
        speed = jnp.sqrt(east * east + north * north + 1.0)
        friction = jnp.sqrt(0.001 * (0.8 + 0.065 * speed)) * speed * (1.0 + 0.15 * gust)
        pull = 28.0 * friction
        share = 0.25 * (density / WATER_DENSITY)
        spread = lambda v: jnp.broadcast_to(v, (8, WB))
        east8, north8, speed8, pull8 = spread(east), spread(north), spread(speed), spread(pull)
        m0 = jnp.zeros((8, WB), F32)
        ms, mk, sx, sy = m0, m0, m0, m0
        for g in range(3):
            cos8, sin8 = cos_tiles[g], sin_tiles[g]
            push = pull8 * ((east8 * cos8 + north8 * sin8) / speed8)
            stress = jnp.zeros((8, WB), F32)
            for i in range(GS):
                spec = spec_ref[i, 8 * g : 8 * g + 8, cols]
                m0 = m0 + spec
                ms = ms + spec * inv_omega[i]
                mk = mk + spec * inv_root[i]
                excess = jnp.maximum(push * inv_c[i] - 1.0, 0.0)
                stress = stress + (excess * omega_c[i]) * spec
            sx = sx + stress * cos8
            sy = sy + stress * sin8
        down = lambda v: jnp.sum(v, axis=0, keepdims=True)
        for n, row in enumerate((down(m0), down(ms), down(mk), down(sx) * share, down(sy) * share)):
            for half in range(WB // 128):
                mom_ref[pl.ds(n * 16 + c * (WB // 128) + half, 1), :] = row[:, half * 128 : half * 128 + 128]
        for n, row in enumerate((east, north, density, speed, friction)):
            for half in range(WB // 128):
                wind_ref[pl.ds(n * 16 + c * (WB // 128) + half, 1), :] = row[:, half * 128 : half * 128 + 128]
        return carry

    lax.fori_loop(0, PTS // WB, block, 0)


def field_kernel(m0_ref, m1_ref, m2_ref, m3_ref, wind_ref, slot_ref, weight_ref, diss_ref, sums_ref, own_ref):
    moments = m0_ref[...] + m1_ref[...] + m2_ref[...] + m3_ref[...]
    total, inv_sigma, inv_root, stress_e, stress_n = (moments[16 * n : 16 * n + 16] for n in range(5))
    east, north, density, speed, friction = (wind_ref[16 * n : 16 * n + 16, :] for n in range(5))
    mean_sigma = total / inv_sigma
    mean_wavenum = jnp.square(total / inv_root)
    steepness = mean_wavenum * mean_wavenum * total * E_UNIT
    diss_ref[...] = DISSIP_COEF * mean_sigma * jnp.square(steepness / STEEP_PM) / mean_wavenum
    scale = WATER_DENSITY / density * G_ACC * E_UNIT
    friction_sq = friction * friction
    east_ratio = scale * stress_e / friction_sq
    north_ratio = scale * stress_n / friction_sq
    aligned = (east_ratio * east + north_ratio * north) / speed
    charnock = 1.0 / jnp.sqrt(1.0 - 0.9 * aligned / (1.0 + jnp.abs(aligned)))
    height = 4.0 * jnp.sqrt(E_UNIT * total)
    f = lax.axis_index("freq")
    own_ref[...] = jnp.where(f == 0, east_ratio, jnp.where(f == 1, north_ratio, jnp.where(f == 2, charnock, height)))

    def block(c, acc):
        cols = pl.ds(pl.multiple_of(c * WB, WB), WB)
        weights, band = weight_matrix(slot_ref, weight_ref, cols, WB)
        w0, w1 = parts2(weights)
        field = jnp.concatenate([own_ref[pl.ds(c * (WB // 128) + half, 1), :] for half in range(WB // 128)], axis=1)
        spread = jnp.where(lax.broadcasted_iota(I32, (TILES, WB), 0) == band, field, 0.0)
        f0, f1 = parts2(spread)
        left = jnp.concatenate([f0, f1, f0], axis=1)
        right = jnp.concatenate([w0, w0, w1], axis=1)
        return acc + lax.dot_general(left, right, (((1,), (1,)), ((), ())), preferred_element_type=F32)

    acc = lax.fori_loop(0, PTS // WB, block, jnp.zeros((TILES, CAP), F32))
    for half in range(2):
        sums_ref[:, half, :] = acc[:, half * 128 : half * 128 + 128]


def band_kernel(arrived_ref, rows_ref, out_ref):
    def eight_tiles(q, acc):
        ones, values = [], []
        for t in range(8):
            index = rows_ref[pl.ds(q * 8 + t, 1), :]
            tile = arrived_ref[q * 8 + t]
            row = jnp.concatenate([tile[0:1, :], tile[1:2, :]], axis=1)
            v0, v1 = parts2(row)
            high = lax.broadcasted_iota(I32, (16, CAP), 0) == (index >> 7)
            v0, v1 = v0.astype(F32), v1.astype(F32)
            values.append(jnp.concatenate([jnp.where(high, v0, 0.0), jnp.where(high, v1, 0.0)], axis=0).astype(BF))
            ones.append((lax.broadcasted_iota(I32, (128, CAP), 0) == (index & 127)).astype(F32).astype(BF))
        left = jnp.concatenate(ones, axis=1)
        right = jnp.concatenate(values, axis=1)
        return acc + lax.dot_general(left, right, (((1,), (1,)), ((), ())), preferred_element_type=F32)

    acc = lax.fori_loop(0, TILES // 8, eight_tiles, jnp.zeros((128, 32), F32))
    out_ref[...] = jnp.transpose(acc[:, :16] + acc[:, 16:])


def move_kernel(half, spec_hbm, x_hbm, low_hbm, high_hbm, near_hbm, *refs):
    if half == 0:
        out_hbm, rim_hbm, *refs = refs
    else:
        out_hbm, *refs = refs
    x_ref, spec_ref, rim_ref, near_ref, low_ref, high_ref, out_ref, sems = refs
    start = half * HALF
    here = pl.ds(start, HALF)
    copies = []

    def load(source, target):
        copies.append(pltpu.make_async_copy(source, target, sems.at[len(copies)]))
        copies[-1].start()
        return copies[-1]

    near_load = load(near_hbm.at[:, here], near_ref)
    if half == 0:
        rim_loads = [load(low_hbm, low_ref), load(high_hbm, high_ref)]
    else:
        rim_loads = [load(low_hbm, rim_ref)]
    piece = KCOPIES * 16 // 5
    x_loads = [load(x_hbm.at[pl.ds(n * piece, piece)], x_ref.at[pl.ds(n * piece, piece)]) for n in range(5)]
    spec_load = load(spec_hbm.at[:, :, here], spec_ref)
    for copy in rim_loads:
        copy.wait()
    if half == 0:
        put_parts(low_ref, slice(0, RIM), rim_ref, slice(0, RIM))
        put_parts(high_ref, slice(0, RIM), rim_ref, slice(RIM, 2 * RIM))
        load(rim_ref, rim_hbm)
    scale = group_scale()[1]
    courant = jnp.concatenate([by_sublane(COURANT) * scale] * (NB // 128), axis=1)
    near_load.wait()
    for copy in x_loads:
        copy.wait()
    spec_load.wait()

    def hot(rows, index):
        match = lax.broadcasted_iota(jnp.int16, (rows, NB), 0) == index
        return jnp.where(match, jnp.ones((), BF), jnp.zeros((), BF))

    def block(c, carry):
        outs = pl.ds(pl.multiple_of(c * NB, NB), NB)
        got = []
        for n, first in enumerate((0, 12, 6, 18)):
            index = near_ref[n : n + 1, outs]
            rim_index = jnp.where(index < RIM, index, jnp.where(index < RIM + PTS, 2 * RIM, index - PTS))
            rows = slice(first * 16, first * 16 + 192)
            own = jnp.dot(x_ref[rows, :], hot(PTS, (index - RIM).astype(jnp.int16)), preferred_element_type=F32)
            rim = jnp.dot(rim_ref[rows, :], hot(2 * RIM, rim_index.astype(jnp.int16)), preferred_element_type=F32)
            got.append(own + rim)
        for k in range(ND):
            a = (k + ROLL) % ND
            x_of = got[0] if a < 12 else got[1]
            a = a % 12
            y_of = got[2] if k < 12 else got[3]
            b = k % 12
            from_x = x_of[a * 16 : a * 16 + 8] + x_of[a * 16 + 8 : a * 16 + 16]
            from_y = y_of[b * 16 : b * 16 + 8] + y_of[b * 16 + 8 : b * 16 + 16]
            spec = spec_ref[:, k, outs]
            out_ref[:, k, outs] = (
                spec - (courant * abs(COS[k])) * (spec - from_x) - (courant * abs(SIN[k])) * (spec - from_y)
            )
        pltpu.make_async_copy(out_ref.at[:, :, outs], out_hbm.at[:, :, outs], sems.at[MOVE_SEMS + c]).start()
        return carry

    lax.fori_loop(0, HALF // NB, block, 0)
    for c in range(HALF // NB):
        outs = pl.ds(c * NB, NB)
        pltpu.make_async_copy(out_ref.at[:, :, outs], out_hbm.at[:, :, outs], sems.at[MOVE_SEMS + c]).wait()
    if half == 0:
        copies[-1].wait()


def source_kernel(moved0_hbm, moved1_hbm, wind_ref, diss_ref, out_hbm, moved_ref, push_ref, new_ref, loads, stores):
    copies = []
    for i in range(GS):
        for half, moved_hbm in ((0, moved0_hbm), (1, moved1_hbm)):
            target = moved_ref.at[i, :, half * HALF : half * HALF + HALF]
            copies.append(pltpu.make_async_copy(moved_hbm.at[i], target, loads.at[2 * i + half]))
    for copy in copies:
        copy.start()
    up = group_scale()[0]
    cos_tiles, sin_tiles = direction_tiles(COS), direction_tiles(SIN)

    def spread(c):
        row = lambda n: jnp.broadcast_to(wind_ref[pl.ds(n * 16 + c, 1), :], (8, 128))
        return [row(n) for n in range(5)]

    def prepare(c, carry):
        east, north, density, speed, friction = spread(c)
        pull = 28.0 * friction / speed
        for g in range(3):
            push_ref[c, 8 * g : 8 * g + 8, :] = pull * (east * cos_tiles[g] + north * sin_tiles[g])
        push_ref[c, 24:32, :] = (0.25 * DT_SRC) * (density / WATER_DENSITY)
        push_ref[c, 32:40, :] = DT_SRC * jnp.broadcast_to(diss_ref[pl.ds(c, 1), :], (8, 128))
        return carry

    lax.fori_loop(0, PTS // 128, prepare, 0)
    for i in range(GS):
        inv_c, omega, wavenum = OMEGA[i] / G_ACC * up, OMEGA[i] * up, OMEGA[i] ** 2 / G_ACC * (up * up)
        copies[2 * i].wait()
        copies[2 * i + 1].wait()

        def block(c, carry):
            cols = pl.ds(pl.multiple_of(c * 128, 128), 128)
            share, loss = push_ref[c, 24:32, :] * omega, push_ref[c, 32:40, :] * wavenum
            for g in range(3):
                rows = slice(8 * g, 8 * g + 8)
                excess = jnp.maximum(push_ref[c, rows, :] * inv_c - 1.0, 0.0)
                new_ref[i, rows, cols] = moved_ref[i, rows, cols] * jnp.exp(share * excess - loss)
            return carry

        lax.fori_loop(0, PTS // 128, block, 0, unroll=4)
        pltpu.make_async_copy(new_ref.at[i], out_hbm.at[i], stores.at[i]).start()
    for i in range(GS):
        pltpu.make_async_copy(new_ref.at[i], out_hbm.at[i], stores.at[i]).wait()


VMEM = pl.BlockSpec(memory_space=pltpu.VMEM)
HBM = pl.BlockSpec(memory_space=pltpu.HBM)


def array(*dims, dtype=F32):
    return jax.ShapeDtypeStruct(dims, dtype)


def call(body, name, out, specs, scratch=(), mib=64, microseconds=1.0, out_specs=None, behind=False, mark=False):
    out = list(out)
    out_specs = [VMEM] * len(out) if out_specs is None else list(out_specs)
    specs = [*specs, VMEM] if behind else specs
    inputs = len(specs) - behind
    outputs = len(out)
    if mark:
        out.append(array(8, 128))
        out_specs.append(VMEM)

    def kernel(*refs):
        results = inputs + behind
        if mark:
            refs[results + outputs][...] = jnp.zeros((8, 128), F32)
        body(*refs[:inputs], *refs[results : results + outputs], *refs[results + outputs + mark :])

    cost = pl.CostEstimate(flops=0, bytes_accessed=int(microseconds * 3.0e6), transcendentals=0)
    return pl.pallas_call(
        kernel,
        out_shape=out,
        in_specs=specs,
        out_specs=out_specs,
        scratch_shapes=list(scratch),
        name=name,
        cost_estimate=cost,
        compiler_params=pltpu.CompilerParams(vmem_limit_bytes=mib * 2**20),
    )


def on_device(spectrum, forcing, send_rows, point_slot, remap_weight, neighbours, halo_send):
    dma = pltpu.SemaphoreType.DMA
    outgoing, to_before, to_after, operand, mark = call(
        first_kernel,
        "first",
        [array(TILES, 8, 128), array(GS, ND, RIM), array(GS, ND, RIM), array(KCOPIES * 16, PTS, dtype=BF)],
        [HBM] * 4,
        [
            pltpu.VMEM((4, PTS), F32),
            pltpu.VMEM((TILES, CAP), I32),
            pltpu.VMEM((2, RIM), I32),
            pltpu.VMEM((GS, ND, PTS), F32),
            pltpu.VMEM((TILES, 8, 128), F32),
            dma((4,)),
            dma((TILES // 8,)),
        ],
        microseconds=5.0,
        out_specs=[HBM, VMEM, VMEM, VMEM],
        mark=True,
    )(forcing, send_rows, halo_send.reshape(2, RIM), spectrum)
    arrived = lax.all_to_all(outgoing, "tile", split_axis=0, concat_axis=0, tiled=True)

    up = [(d, d + 1) for d in range(TILES - 1)]
    low_rim = lax.ppermute(to_after, "tile", up)
    high_rim = lax.ppermute(to_before, "tile", [(b, a) for a, b in up])

    blocks = HALF // NB
    scratch = [
        pltpu.VMEM((KCOPIES * 16, PTS), BF),
        pltpu.VMEM((GS, ND, HALF), F32),
        pltpu.VMEM((KCOPIES * 16, 2 * RIM), BF),
        pltpu.VMEM((4, HALF), I32),
        pltpu.VMEM((GS, ND, RIM), F32),
        pltpu.VMEM((GS, ND, RIM), F32),
        pltpu.VMEM((GS, ND, HALF), F32),
        dma((MOVE_SEMS + blocks,)),
    ]
    moved0, rims, mark = call(
        functools.partial(move_kernel, 0),
        "move0",
        [array(GS, ND, HALF), array(KCOPIES * 16, 2 * RIM, dtype=BF)],
        [HBM] * 5,
        scratch,
        microseconds=5.5,
        out_specs=[HBM, HBM],
        behind=True,
        mark=True,
    )(spectrum, operand, low_rim, high_rim, neighbours, mark)
    wind, moments, mark = call(
        wind_kernel,
        "wind",
        [array(80, 128), array(80, 128)],
        [VMEM, HBM, HBM, VMEM],
        [
            pltpu.VMEM((256, 6 * 256), BF),
            pltpu.VMEM((4, PTS), I32),
            pltpu.VMEM((4, PTS), F32),
            dma((2,)),
        ],
        microseconds=6.0,
        behind=True,
        mark=True,
    )(arrived, point_slot, remap_weight, spectrum, mark)
    others = [lax.ppermute(moments, "freq", [(i, (i + n) % 4) for i in range(4)]) for n in (1, 2, 3)]
    moved1, mark = call(
        lambda spec, x, rim, near, *refs: move_kernel(1, spec, x, rim, None, near, *refs),
        "move1",
        [array(GS, ND, HALF)],
        [HBM] * 4,
        scratch,
        microseconds=5.0,
        out_specs=[HBM],
        behind=True,
        mark=True,
    )(spectrum, operand, rims, neighbours, mark)

    diss, slot_sums = call(
        field_kernel,
        "fields",
        [array(16, 128), array(TILES, 2, 128)],
        [VMEM] * 7,
        [pltpu.VMEM((16, 128), F32)],
        microseconds=3.0,
        behind=True,
    )(moments, *others, wind, point_slot, remap_weight, mark)
    arrived_sums = lax.all_to_all(slot_sums, "tile", split_axis=0, concat_axis=0, tiled=True)

    new_spectrum, mark = call(
        source_kernel,
        "source",
        [array(GS, ND, PTS)],
        [HBM, HBM, VMEM, VMEM],
        [
            pltpu.VMEM((GS, ND, PTS), F32),
            pltpu.VMEM((PTS // 128, 40, 128), F32),
            pltpu.VMEM((GS, ND, PTS), F32),
            dma((2 * GS,)),
            dma((GS,)),
        ],
        microseconds=3.0,
        out_specs=[HBM],
        mark=True,
    )(moved0, moved1, wind, diss)

    (returned,) = call(band_kernel, "band", [array(16, 128)], [VMEM] * 2, microseconds=2.5, behind=True)(
        arrived_sums, send_rows, mark
    )
    return (new_spectrum, returned.reshape(1, PTS))


def solution(mesh):
    placed = (
        P("freq", None, "tile"),
        P(None, "tile"),
        P("tile", None),
        P(None, "tile"),
        P(None, "tile"),
        P(None, "tile"),
        P("tile"),
    )
    return jax.shard_map(
        on_device,
        mesh=mesh,
        in_specs=placed,
        out_specs=(P("freq", None, "tile"), P("freq", "tile")),
        check_vma=False,
    )
```

```python
import functools
import math

import jax
import jax.numpy as jnp
from jax import lax
from jax.experimental import pallas as pl
from jax.experimental.pallas import tpu as pltpu
from jax.sharding import PartitionSpec as P

G_ACC = 9.81
WATER_DENSITY = 1025.0
FREQ_LOW = 0.03453
FREQ_RATIO = 1.1
E_UNIT = 0.001
DT_SRC = 120.0
COURANT_MAX = 0.7
DISSIP_COEF = 2.33e-05
STEEP_PM = 0.00302
TOP_EXPONENT = 31.0

NF = 32
ND = 24
GS = 8
PTS = 2048
TILES = 64
CAP = 256
RIM = 128
EXT = PTS + 2 * RIM

F32 = jnp.float32
BF = jnp.bfloat16
I32 = jnp.int32

THETA = [(k + 0.5) * 2.0 * math.pi / ND for k in range(ND)]
COS = [math.cos(t) for t in THETA]
SIN = [math.sin(t) for t in THETA]

OMEGA = [2.0 * math.pi * FREQ_LOW * FREQ_RATIO**i for i in range(GS)]
COURANT = [COURANT_MAX * FREQ_RATIO ** (-i) for i in range(GS)]


def group_scale():
    f = lax.axis_index("freq")
    pick = lambda v: jnp.where(f == 0, v[0], jnp.where(f == 1, v[1], jnp.where(f == 2, v[2], v[3]))).astype(F32)
    return pick([FREQ_RATIO ** (GS * n) for n in range(4)]), pick([FREQ_RATIO ** (-GS * n) for n in range(4)])


def by_sublane(values):
    which = lax.broadcasted_iota(I32, (8, 128), 0)
    tile = jnp.full((8, 128), values[7], F32)
    for n in range(7):
        tile = jnp.where(which == n, values[n], tile)
    return tile


def direction_tiles(values):
    return [by_sublane(values[8 * g : 8 * g + 8]) for g in range(3)]


def lane_gather(block, index):
    return jnp.take_along_axis(block, index, axis=1, mode="promise_in_bounds")


def parts2(x):
    first = x.astype(BF)
    return first, (x - first.astype(F32)).astype(BF)


def parts3(x):
    first = x.astype(BF)
    rest = x - first.astype(F32)
    second = rest.astype(BF)
    return first, second, (rest - second.astype(F32)).astype(BF)


ROLL = 6
KCOPIES = 30
NB = 512
HALF = PTS // 2


def put_parts(ref, source, x_ref, target):
    for kp in range(KCOPIES):
        v = ref[:, (kp + ND - ROLL) % ND, source]
        p0 = v.astype(BF).astype(F32)
        x_ref[kp * 16 : kp * 16 + 16, target] = jnp.concatenate([p0, v - p0], axis=0).astype(BF)


def start_copies(pairs, sems, first=0):
    copies = [pltpu.make_async_copy(src, dst, sems.at[first + n]) for n, (src, dst) in enumerate(pairs)]
    for copy in copies:
        copy.start()
    return copies


def wait_copies(copies):
    for copy in copies:
        copy.wait()


def start_copies(pairs, sems, first=0):
    copies = [pltpu.make_async_copy(src, dst, sems.at[first + n]) for n, (src, dst) in enumerate(pairs)]
    for copy in copies:
        copy.start()
    return copies


def wait_copies(copies):
    for copy in copies:
        copy.wait()


def first_kernel(
    rows_hbm, forcing_hbm, list_hbm, spec_hbm, out_hbm, before_hbm, after_hbm, x_ref, spec_ref,
    rows_ref, forcing_ref, list_ref, out_ref, before_ref, after_ref, sems, out_sems,
):
    sources = ((rows_hbm, rows_ref), (forcing_hbm, forcing_ref), (list_hbm, list_ref), (spec_hbm, spec_ref))
    wait_copies(start_copies(sources, sems))
    rims = []
    for side, rim_ref in ((0, before_ref), (1, after_ref)):
        index = jnp.broadcast_to(list_ref[side : side + 1, :], (8, 128))
        rims.append((index & 127, index >> 7, rim_ref))

    def step(q, carry):
        d = pl.ds(pl.multiple_of(q * 8, 8), 8)
        for half in range(2):
            index = rows_ref[d, half * 128 : half * 128 + 128]
            low, high = index & 127, index >> 7
            for i in range(4):
                got = None
                for h in range(16):
                    block = jnp.broadcast_to(forcing_ref[i : i + 1, h * 128 : h * 128 + 128], (8, 128))
                    piece = lane_gather(block, low)
                    got = piece if h == 0 else jnp.where(high == h, piece, got)
                out_ref[d, 2 * i + half, :] = got
        pltpu.make_async_copy(out_ref.at[d], out_hbm.at[d], out_sems.at[q]).start()
        for low, high, rim_ref in rims:
            for g in range(3):
                rows = slice(8 * g, 8 * g + 8)
                got = None
                for h in range(16):
                    piece = lane_gather(spec_ref[q, rows, h * 128 : h * 128 + 128], low)
                    got = piece if h == 0 else jnp.where(high == h, piece, got)
                rim_ref[q, rows, :] = got
        for half in range(2):
            cols = pl.ds(pl.multiple_of(q * 256 + half * 128, 128), 128)
            put_parts(spec_ref, cols, x_ref, cols)
        return carry

    lax.fori_loop(0, TILES // 8, step, 0)
    stores = start_copies(((before_ref, before_hbm), (after_ref, after_hbm)), sems)
    for q in range(TILES // 8):
        d = pl.ds(q * 8, 8)
        pltpu.make_async_copy(out_ref.at[d], out_hbm.at[d], out_sems.at[q]).wait()
    wait_copies(stores)


def weight_matrix(slot_ref, weight_ref, cols, width):
    slots = lax.broadcasted_iota(I32, (CAP, width), 0)
    total = None
    for j in range(4):
        index = slot_ref[j : j + 1, cols] & (CAP - 1)
        term = jnp.where(slots == index, weight_ref[j : j + 1, cols], 0.0)
        total = term if j == 0 else total + term
    return total, slot_ref[0:1, cols] >> 8


WB = 256


def wind_kernel(
    arrived_hbm, slot_hbm, weight_hbm, spec_ref, wind_ref, mom_ref, left_ref, arrived_ref, slot_ref, weight_ref, sems
):
    copies = start_copies(((arrived_hbm, arrived_ref), (slot_hbm, slot_ref), (weight_hbm, weight_ref)), sems)
    up, down_scale = group_scale()
    inv_c = [w / G_ACC * up for w in OMEGA]
    inv_omega = [1.0 / w * down_scale for w in OMEGA]
    inv_root = [math.sqrt(G_ACC) / w * down_scale for w in OMEGA]
    omega_c = [w * w / G_ACC * (up * up) for w in OMEGA]
    cos_tiles = [jnp.concatenate([t] * (WB // 128), axis=1) for t in direction_tiles(COS)]
    sin_tiles = [jnp.concatenate([t] * (WB // 128), axis=1) for t in direction_tiles(SIN)]
    wait_copies(copies)
    for i in range(4):
        for half in range(2):
            p0, p1, p2 = parts3(arrived_ref[:, 2 * i + half, :])
            for n, part in enumerate((p0, p1, p2, p0, p1, p0)):
                left_ref[i * 64 : i * 64 + 64, n * 256 + half * 128 : n * 256 + half * 128 + 128] = part

    def block(c, carry):
        cols = pl.ds(pl.multiple_of(c * WB, WB), WB)
        weights, band = weight_matrix(slot_ref, weight_ref, cols, WB)
        w0, w1, w2 = parts3(weights)
        right = jnp.concatenate([w0, w0, w0, w1, w1, w2], axis=0)
        mixed = jnp.dot(left_ref[...], right, preferred_element_type=F32)
        mine = lax.broadcasted_iota(I32, (TILES, WB), 0) == band
        east, north, density, gust = (
            jnp.sum(jnp.where(mine, mixed[i * 64 : i * 64 + 64], 0.0), axis=0, keepdims=True) for i in range(4)
        )
        speed = jnp.sqrt(east * east + north * north + 1.0)
        friction = jnp.sqrt(0.001 * (0.8 + 0.065 * speed)) * speed * (1.0 + 0.15 * gust)
        pull = 28.0 * friction
        share = 0.25 * (density / WATER_DENSITY)
        spread = lambda v: jnp.broadcast_to(v, (8, WB))
        east8, north8, speed8, pull8 = spread(east), spread(north), spread(speed), spread(pull)
        m0 = jnp.zeros((8, WB), F32)
        ms, mk, sx, sy = m0, m0, m0, m0
        for g in range(3):
            cos8, sin8 = cos_tiles[g], sin_tiles[g]
            push = pull8 * ((east8 * cos8 + north8 * sin8) / speed8)
            stress = jnp.zeros((8, WB), F32)
            for i in range(GS):
                spec = spec_ref[i, 8 * g : 8 * g + 8, cols]
                m0 = m0 + spec
                ms = ms + spec * inv_omega[i]
                mk = mk + spec * inv_root[i]
                excess = jnp.maximum(push * inv_c[i] - 1.0, 0.0)
                stress = stress + (excess * omega_c[i]) * spec
            sx = sx + stress * cos8
            sy = sy + stress * sin8
        down = lambda v: jnp.sum(v, axis=0, keepdims=True)
        for n, row in enumerate((down(m0), down(ms), down(mk), down(sx) * share, down(sy) * share)):
            for half in range(WB // 128):
                mom_ref[pl.ds(n * 16 + c * (WB // 128) + half, 1), :] = row[:, half * 128 : half * 128 + 128]
        for n, row in enumerate((east, north, density, speed, friction)):
            for half in range(WB // 128):
                wind_ref[pl.ds(n * 16 + c * (WB // 128) + half, 1), :] = row[:, half * 128 : half * 128 + 128]
        return carry

    lax.fori_loop(0, PTS // WB, block, 0)


def field_kernel(
    m0_ref, m1_ref, m2_ref, m3_ref, wind_ref, slot_hbm, weight_hbm, diss_ref, sums_ref, own_ref, slot_ref, weight_ref, sems
):
    copies = start_copies(((slot_hbm, slot_ref), (weight_hbm, weight_ref)), sems)
    moments = m0_ref[...] + m1_ref[...] + m2_ref[...] + m3_ref[...]
    total, inv_sigma, inv_root, stress_e, stress_n = (moments[16 * n : 16 * n + 16] for n in range(5))
    east, north, density, speed, friction = (wind_ref[16 * n : 16 * n + 16, :] for n in range(5))
    mean_sigma = total / inv_sigma
    mean_wavenum = jnp.square(total / inv_root)
    steepness = mean_wavenum * mean_wavenum * total * E_UNIT
    diss_ref[80:96, :] = DISSIP_COEF * mean_sigma * jnp.square(steepness / STEEP_PM) / mean_wavenum
    diss_ref[0:80, :] = wind_ref[...]
    scale = WATER_DENSITY / density * G_ACC * E_UNIT
    friction_sq = friction * friction
    east_ratio = scale * stress_e / friction_sq
    north_ratio = scale * stress_n / friction_sq
    aligned = (east_ratio * east + north_ratio * north) / speed
    charnock = 1.0 / jnp.sqrt(1.0 - 0.9 * aligned / (1.0 + jnp.abs(aligned)))
    height = 4.0 * jnp.sqrt(E_UNIT * total)
    f = lax.axis_index("freq")
    own_ref[...] = jnp.where(f == 0, east_ratio, jnp.where(f == 1, north_ratio, jnp.where(f == 2, charnock, height)))

    wait_copies(copies)

    def block(c, acc):
        cols = pl.ds(pl.multiple_of(c * WB, WB), WB)
        weights, band = weight_matrix(slot_ref, weight_ref, cols, WB)
        w0, w1 = parts2(weights)
        field = jnp.concatenate([own_ref[pl.ds(c * (WB // 128) + half, 1), :] for half in range(WB // 128)], axis=1)
        spread = jnp.where(lax.broadcasted_iota(I32, (TILES, WB), 0) == band, field, 0.0)
        f0, f1 = parts2(spread)
        left = jnp.concatenate([f0, f1, f0], axis=1)
        right = jnp.concatenate([w0, w0, w1], axis=1)
        return acc + lax.dot_general(left, right, (((1,), (1,)), ((), ())), preferred_element_type=F32)

    acc = lax.fori_loop(0, PTS // WB, block, jnp.zeros((TILES, CAP), F32))
    for half in range(2):
        sums_ref[:, half, :] = acc[:, half * 128 : half * 128 + 128]


def band_kernel(arrived_ref, rows_hbm, out_ref, rows_ref, sems):
    wait_copies(start_copies(((rows_hbm, rows_ref),), sems))

    def eight_tiles(q, acc):
        ones, values = [], []
        for t in range(8):
            index = rows_ref[pl.ds(q * 8 + t, 1), :]
            tile = arrived_ref[q * 8 + t]
            row = jnp.concatenate([tile[0:1, :], tile[1:2, :]], axis=1)
            v0, v1 = parts2(row)
            high = lax.broadcasted_iota(I32, (16, CAP), 0) == (index >> 7)
            v0, v1 = v0.astype(F32), v1.astype(F32)
            values.append(jnp.concatenate([jnp.where(high, v0, 0.0), jnp.where(high, v1, 0.0)], axis=0).astype(BF))
            ones.append((lax.broadcasted_iota(I32, (128, CAP), 0) == (index & 127)).astype(F32).astype(BF))
        left = jnp.concatenate(ones, axis=1)
        right = jnp.concatenate(values, axis=1)
        return acc + lax.dot_general(left, right, (((1,), (1,)), ((), ())), preferred_element_type=F32)

    acc = lax.fori_loop(0, TILES // 8, eight_tiles, jnp.zeros((128, 32), F32))
    out_ref[...] = jnp.transpose(acc[:, :16] + acc[:, 16:])


def move_kernel(half, spec_ref, x_ref, low_ref, high_ref, near_hbm, *refs):
    start = half * HALF
    if half == 0:
        out_hbm, rim_hbm, near_ref, rim_ref, out_ref, sems = refs
        copies = start_copies(((near_hbm, near_ref),), sems)
        put_parts(low_ref, slice(0, RIM), rim_ref, slice(0, RIM))
        put_parts(high_ref, slice(0, RIM), rim_ref, slice(RIM, 2 * RIM))
        stores = start_copies(((rim_ref, rim_hbm),), sems, 1)
    else:
        out_hbm, near_ref, rim_ref, out_ref, sems = refs
        copies = start_copies(((near_hbm, near_ref), (low_ref, rim_ref)), sems)
        stores = []
    wait_copies(copies)
    scale = group_scale()[1]
    courant = jnp.concatenate([by_sublane(COURANT) * scale] * (NB // 128), axis=1)

    def hot(rows, index):
        match = lax.broadcasted_iota(jnp.int16, (rows, NB), 0) == index
        return jnp.where(match, jnp.ones((), BF), jnp.zeros((), BF))

    def block(c, carry):
        outs = pl.ds(pl.multiple_of(c * NB, NB), NB)
        cols = pl.ds(pl.multiple_of(start + c * NB, NB), NB)
        got = []
        for n, first in enumerate((0, 12, 6, 18)):
            index = near_ref[n : n + 1, cols]
            rim_index = jnp.where(index < RIM, index, jnp.where(index < RIM + PTS, 2 * RIM, index - PTS))
            rows = slice(first * 16, first * 16 + 192)
            own = jnp.dot(x_ref[rows, :], hot(PTS, (index - RIM).astype(jnp.int16)), preferred_element_type=F32)
            rim = jnp.dot(rim_ref[rows, :], hot(2 * RIM, rim_index.astype(jnp.int16)), preferred_element_type=F32)
            got.append(own + rim)
        for k in range(ND):
            a = (k + ROLL) % ND
            x_of = got[0] if a < 12 else got[1]
            a = a % 12
            y_of = got[2] if k < 12 else got[3]
            b = k % 12
            from_x = x_of[a * 16 : a * 16 + 8] + x_of[a * 16 + 8 : a * 16 + 16]
            from_y = y_of[b * 16 : b * 16 + 8] + y_of[b * 16 + 8 : b * 16 + 16]
            spec = spec_ref[:, k, cols]
            out_ref[:, k, outs] = (
                spec - (courant * abs(COS[k])) * (spec - from_x) - (courant * abs(SIN[k])) * (spec - from_y)
            )
        pltpu.make_async_copy(out_ref.at[:, :, outs], out_hbm.at[:, :, outs], sems.at[2 + c]).start()
        return carry

    lax.fori_loop(0, HALF // NB, block, 0)
    for c in range(HALF // NB):
        outs = pl.ds(c * NB, NB)
        pltpu.make_async_copy(out_ref.at[:, :, outs], out_hbm.at[:, :, outs], sems.at[2 + c]).wait()
    wait_copies(stores)


def source_kernel(moved0_hbm, moved1_hbm, wind_ref, out_hbm, push_ref, new_ref, moved0_ref, moved1_ref, loads, stores):
    pairs = []
    for i in range(GS):
        pairs += [(moved0_hbm.at[i], moved0_ref.at[i]), (moved1_hbm.at[i], moved1_ref.at[i])]
    copies = start_copies(pairs, loads)
    up = group_scale()[0]
    cos_tiles, sin_tiles = direction_tiles(COS), direction_tiles(SIN)

    def spread(c):
        row = lambda n: jnp.broadcast_to(wind_ref[pl.ds(n * 16 + c, 1), :], (8, 128))
        return [row(n) for n in range(5)]

    def prepare(c, carry):
        east, north, density, speed, friction = spread(c)
        pull = 28.0 * friction / speed
        for g in range(3):
            push_ref[c, 8 * g : 8 * g + 8, :] = pull * (east * cos_tiles[g] + north * sin_tiles[g])
        push_ref[c, 24:32, :] = (0.25 * DT_SRC) * (density / WATER_DENSITY)
        push_ref[c, 32:40, :] = DT_SRC * jnp.broadcast_to(wind_ref[pl.ds(80 + c, 1), :], (8, 128))
        return carry

    lax.fori_loop(0, PTS // 128, prepare, 0)
    for i in range(GS):
        inv_c, omega, wavenum = OMEGA[i] / G_ACC * up, OMEGA[i] * up, OMEGA[i] ** 2 / G_ACC * (up * up)
        wait_copies(copies[2 * i : 2 * i + 2])
        for half, moved_ref in ((0, moved0_ref), (1, moved1_ref)):

            def block(c, carry):
                at = c + half * (HALF // 128)
                cols = pl.ds(pl.multiple_of(c * 128, 128), 128)
                outs = pl.ds(pl.multiple_of(at * 128, 128), 128)
                share, loss = push_ref[at, 24:32, :] * omega, push_ref[at, 32:40, :] * wavenum
                for g in range(3):
                    rows = slice(8 * g, 8 * g + 8)
                    excess = jnp.maximum(push_ref[at, rows, :] * inv_c - 1.0, 0.0)
                    new_ref[i, rows, outs] = moved_ref[i, rows, cols] * jnp.exp(share * excess - loss)
                return carry

            lax.fori_loop(0, HALF // 128, block, 0, unroll=4)
        pltpu.make_async_copy(new_ref.at[i], out_hbm.at[i], stores.at[i]).start()
    for i in range(GS):
        pltpu.make_async_copy(new_ref.at[i], out_hbm.at[i], stores.at[i]).wait()


VMEM = pl.BlockSpec(memory_space=pltpu.VMEM)
HBM = pl.BlockSpec(memory_space=pltpu.HBM)


def array(*dims, dtype=F32):
    return jax.ShapeDtypeStruct(dims, dtype)


def resident(*dims, dtype=F32):
    return pltpu.VMEM(dims, dtype)


def distant(*dims, dtype=F32):
    return pltpu.HBM(dims, dtype)


def in_hbm(x):
    return pltpu.with_memory_space_constraint(x, pltpu.HBM)


def call(body, name, out, specs, scratch=(), mib=24, microseconds=1.0, out_specs=None, behind=False, mark=False):
    out = list(out)
    out_specs = [VMEM] * len(out) if out_specs is None else list(out_specs)
    specs = [*specs, VMEM] if behind else specs
    inputs = len(specs) - behind
    outputs = len(out)
    if mark:
        out.append(resident(8, 128))
        out_specs.append(VMEM)

    def kernel(*refs):
        results = inputs + behind
        if mark:
            refs[results + outputs][...] = jnp.zeros((8, 128), F32)
        body(*refs[:inputs], *refs[results : results + outputs], *refs[results + outputs + mark :])

    cost = pl.CostEstimate(flops=0, bytes_accessed=int(microseconds * 3.0e6), transcendentals=0)
    return pl.pallas_call(
        kernel,
        out_shape=out,
        in_specs=specs,
        out_specs=out_specs,
        scratch_shapes=list(scratch),
        name=name,
        cost_estimate=cost,
        compiler_params=pltpu.CompilerParams(vmem_limit_bytes=mib * 2**20),
    )


def on_device(spectrum, forcing, send_rows, point_slot, remap_weight, neighbours, halo_send):
    dma = pltpu.SemaphoreType.DMA
    outgoing, to_before, to_after, operand, spec, mark = call(
        first_kernel,
        "first",
        [
            distant(TILES, 8, 128),
            distant(GS, ND, RIM),
            distant(GS, ND, RIM),
            resident(KCOPIES * 16, PTS, dtype=BF),
            resident(GS, ND, PTS),
        ],
        [HBM] * 4,
        [
            pltpu.VMEM((TILES, CAP), I32),
            pltpu.VMEM((4, PTS), F32),
            pltpu.VMEM((2, RIM), I32),
            pltpu.VMEM((TILES, 8, 128), F32),
            pltpu.VMEM((GS, ND, RIM), F32),
            pltpu.VMEM((GS, ND, RIM), F32),
            dma((4,)),
            dma((TILES // 8,)),
        ],
        microseconds=5.0,
        out_specs=[HBM, HBM, HBM, VMEM, VMEM],
        mark=True,
    )(*map(in_hbm, (send_rows, forcing, halo_send.reshape(2, RIM), spectrum)))
    arrived = lax.all_to_all(outgoing, "tile", split_axis=0, concat_axis=0, tiled=True)

    up = [(d, d + 1) for d in range(TILES - 1)]
    low_rim = lax.ppermute(to_after, "tile", up)
    high_rim = lax.ppermute(to_before, "tile", [(b, a) for a, b in up])

    blocks = HALF // NB
    scratch = [
        pltpu.VMEM((4, PTS), I32),
        pltpu.VMEM((KCOPIES * 16, 2 * RIM), BF),
        pltpu.VMEM((GS, ND, HALF), F32),
        dma((2 + blocks,)),
    ]
    moved0, rims, mark = call(
        functools.partial(move_kernel, 0),
        "move0",
        [distant(GS, ND, HALF), distant(KCOPIES * 16, 2 * RIM, dtype=BF)],
        [VMEM] * 4 + [HBM],
        scratch,
        microseconds=5.5,
        out_specs=[HBM, HBM],
        behind=True,
        mark=True,
    )(spec, operand, low_rim, high_rim, in_hbm(neighbours), mark)
    wind, moments, mark = call(
        wind_kernel,
        "wind",
        [array(80, 128), array(80, 128)],
        [HBM, HBM, HBM, VMEM],
        [
            pltpu.VMEM((256, 6 * 256), BF),
            pltpu.VMEM((TILES, 8, 128), F32),
            pltpu.VMEM((4, PTS), I32),
            pltpu.VMEM((4, PTS), F32),
            dma((3,)),
        ],
        microseconds=6.0,
        behind=True,
        mark=True,
    )(in_hbm(arrived), in_hbm(point_slot), in_hbm(remap_weight), spec, mark)
    others = [lax.ppermute(moments, "freq", [(i, (i + n) % 4) for i in range(4)]) for n in (1, 2, 3)]
    moved1, mark = call(
        lambda spec_ref, x_ref, rim_ref, near_ref, *refs: move_kernel(1, spec_ref, x_ref, rim_ref, None, near_ref, *refs),
        "move1",
        [distant(GS, ND, HALF)],
        [VMEM] * 2 + [HBM] * 2,
        scratch,
        microseconds=5.0,
        out_specs=[HBM],
        behind=True,
        mark=True,
    )(spec, operand, rims, in_hbm(neighbours), mark)

    state, slot_sums = call(
        field_kernel,
        "fields",
        [resident(96, 128), array(TILES, 2, 128)],
        [VMEM] * 5 + [HBM] * 2,
        [pltpu.VMEM((16, 128), F32), pltpu.VMEM((4, PTS), I32), pltpu.VMEM((4, PTS), F32), dma((2,))],
        microseconds=3.0,
        behind=True,
    )(moments, *others, wind, in_hbm(point_slot), in_hbm(remap_weight), mark)
    arrived_sums = lax.all_to_all(slot_sums, "tile", split_axis=0, concat_axis=0, tiled=True)

    new_spectrum, mark = call(
        source_kernel,
        "source",
        [array(GS, ND, PTS)],
        [HBM, HBM, VMEM],
        [
            pltpu.VMEM((PTS // 128, 40, 128), F32),
            pltpu.VMEM((GS, ND, PTS), F32),
            pltpu.VMEM((GS, ND, HALF), F32),
            pltpu.VMEM((GS, ND, HALF), F32),
            dma((2 * GS,)),
            dma((GS,)),
        ],
        microseconds=3.0,
        out_specs=[HBM],
        mark=True,
    )(in_hbm(moved0), in_hbm(moved1), state)

    (returned,) = call(
        band_kernel,
        "band",
        [array(16, 128)],
        [VMEM, HBM],
        [pltpu.VMEM((TILES, CAP), I32), dma((1,))],
        microseconds=2.5,
        behind=True,
    )(arrived_sums, in_hbm(send_rows), mark)
    return (new_spectrum, returned.reshape(1, PTS))


def solution(mesh):
    placed = (
        P("freq", None, "tile"),
        P(None, "tile"),
        P("tile", None),
        P(None, "tile"),
        P(None, "tile"),
        P(None, "tile"),
        P("tile"),
    )
    return jax.shard_map(
        on_device,
        mesh=mesh,
        in_specs=placed,
        out_specs=(P("freq", None, "tile"), P("freq", "tile")),
        check_vma=False,
    )
```

```python
import functools
import math

import jax
import jax.numpy as jnp
from jax import lax
from jax.experimental import pallas as pl
from jax.experimental.pallas import tpu as pltpu
from jax.sharding import PartitionSpec as P

G_ACC = 9.81
WATER_DENSITY = 1025.0
FREQ_LOW = 0.03453
FREQ_RATIO = 1.1
E_UNIT = 0.001
DT_SRC = 120.0
COURANT_MAX = 0.7
DISSIP_COEF = 2.33e-05
STEEP_PM = 0.00302
TOP_EXPONENT = 31.0

NF = 32
ND = 24
GS = 8
PTS = 2048
TILES = 64
CAP = 256
RIM = 128
EXT = PTS + 2 * RIM

F32 = jnp.float32
BF = jnp.bfloat16
I32 = jnp.int32

THETA = [(k + 0.5) * 2.0 * math.pi / ND for k in range(ND)]
COS = [math.cos(t) for t in THETA]
SIN = [math.sin(t) for t in THETA]

OMEGA = [2.0 * math.pi * FREQ_LOW * FREQ_RATIO**i for i in range(GS)]
COURANT = [COURANT_MAX * FREQ_RATIO ** (-i) for i in range(GS)]


def group_scale():
    f = lax.axis_index("freq")
    pick = lambda v: jnp.where(f == 0, v[0], jnp.where(f == 1, v[1], jnp.where(f == 2, v[2], v[3]))).astype(F32)
    return pick([FREQ_RATIO ** (GS * n) for n in range(4)]), pick([FREQ_RATIO ** (-GS * n) for n in range(4)])


def by_sublane(values):
    which = lax.broadcasted_iota(I32, (8, 128), 0)
    tile = jnp.full((8, 128), values[7], F32)
    for n in range(7):
        tile = jnp.where(which == n, values[n], tile)
    return tile


def direction_tiles(values):
    return [by_sublane(values[8 * g : 8 * g + 8]) for g in range(3)]


def lane_gather(block, index):
    return jnp.take_along_axis(block, index, axis=1, mode="promise_in_bounds")


def parts2(x):
    first = x.astype(BF)
    return first, (x - first.astype(F32)).astype(BF)


def parts3(x):
    first = x.astype(BF)
    rest = x - first.astype(F32)
    second = rest.astype(BF)
    return first, second, (rest - second.astype(F32)).astype(BF)


ROLL = 6
KCOPIES = 30
NB = 512
HALF = PTS // 2


def put_parts(ref, source, x_ref, target):
    for kp in range(KCOPIES):
        v = ref[:, (kp + ND - ROLL) % ND, source]
        p0 = v.astype(BF).astype(F32)
        x_ref[kp * 16 : kp * 16 + 16, target] = jnp.concatenate([p0, v - p0], axis=0).astype(BF)


def start_copies(pairs, sems, first=0):
    copies = [pltpu.make_async_copy(src, dst, sems.at[first + n]) for n, (src, dst) in enumerate(pairs)]
    for copy in copies:
        copy.start()
    return copies


def wait_copies(copies):
    for copy in copies:
        copy.wait()


def start_copies(pairs, sems, first=0):
    copies = [pltpu.make_async_copy(src, dst, sems.at[first + n]) for n, (src, dst) in enumerate(pairs)]
    for copy in copies:
        copy.start()
    return copies


def wait_copies(copies):
    for copy in copies:
        copy.wait()


def start_copies(pairs, sems, first=0):
    copies = [pltpu.make_async_copy(src, dst, sems.at[first + n]) for n, (src, dst) in enumerate(pairs)]
    for copy in copies:
        copy.start()
    return copies


def wait_copies(copies):
    for copy in copies:
        copy.wait()


def rim_kernel(list_hbm, spec_hbm, before_hbm, after_hbm, spec_ref, list_ref, before_ref, after_ref, sems):
    wait_copies(start_copies(((list_hbm, list_ref), (spec_hbm, spec_ref)), sems))
    rims = []
    for side, rim_ref in ((0, before_ref), (1, after_ref)):
        index = jnp.broadcast_to(list_ref[side : side + 1, :], (8, 128))
        rims.append((index & 127, index >> 7, rim_ref))

    def step(i, carry):
        for low, high, rim_ref in rims:
            for g in range(3):
                rows = slice(8 * g, 8 * g + 8)
                got = None
                for h in range(16):
                    piece = lane_gather(spec_ref[i, rows, h * 128 : h * 128 + 128], low)
                    got = piece if h == 0 else jnp.where(high == h, piece, got)
                rim_ref[i, rows, :] = got
        return carry

    lax.fori_loop(0, GS, step, 0)
    wait_copies(start_copies(((before_ref, before_hbm), (after_ref, after_hbm)), sems))


def outgoing_kernel(rows_hbm, forcing_hbm, out_hbm, rows_ref, forcing_ref, out_ref, sems, out_sems):
    wait_copies(start_copies(((rows_hbm, rows_ref), (forcing_hbm, forcing_ref)), sems))

    def step(q, carry):
        d = pl.ds(pl.multiple_of(q * 8, 8), 8)
        for half in range(2):
            index = rows_ref[d, half * 128 : half * 128 + 128]
            low, high = index & 127, index >> 7
            for i in range(4):
                got = None
                for h in range(16):
                    block = jnp.broadcast_to(forcing_ref[i : i + 1, h * 128 : h * 128 + 128], (8, 128))
                    piece = lane_gather(block, low)
                    got = piece if h == 0 else jnp.where(high == h, piece, got)
                out_ref[d, 2 * i + half, :] = got
        pltpu.make_async_copy(out_ref.at[d], out_hbm.at[d], out_sems.at[q]).start()
        return carry

    lax.fori_loop(0, TILES // 8, step, 0)
    for q in range(TILES // 8):
        d = pl.ds(q * 8, 8)
        pltpu.make_async_copy(out_ref.at[d], out_hbm.at[d], out_sems.at[q]).wait()


def weight_matrix(slot_ref, weight_ref, cols, width):
    slots = lax.broadcasted_iota(I32, (CAP, width), 0)
    total = None
    for j in range(4):
        index = slot_ref[j : j + 1, cols] & (CAP - 1)
        term = jnp.where(slots == index, weight_ref[j : j + 1, cols], 0.0)
        total = term if j == 0 else total + term
    return total, slot_ref[0:1, cols] >> 8


WB = 256


def wind_kernel(
    arrived_hbm, slot_hbm, weight_hbm, spec_ref, wind_ref, mom_ref, left_ref, arrived_ref, slot_ref, weight_ref, sems
):
    copies = start_copies(((arrived_hbm, arrived_ref), (slot_hbm, slot_ref), (weight_hbm, weight_ref)), sems)
    up, down_scale = group_scale()
    inv_c = [w / G_ACC * up for w in OMEGA]
    inv_omega = [1.0 / w * down_scale for w in OMEGA]
    inv_root = [math.sqrt(G_ACC) / w * down_scale for w in OMEGA]
    omega_c = [w * w / G_ACC * (up * up) for w in OMEGA]
    cos_tiles = [jnp.concatenate([t] * (WB // 128), axis=1) for t in direction_tiles(COS)]
    sin_tiles = [jnp.concatenate([t] * (WB // 128), axis=1) for t in direction_tiles(SIN)]
    wait_copies(copies)
    for i in range(4):
        for half in range(2):
            p0, p1, p2 = parts3(arrived_ref[:, 2 * i + half, :])
            for n, part in enumerate((p0, p1, p2, p0, p1, p0)):
                left_ref[i * 64 : i * 64 + 64, n * 256 + half * 128 : n * 256 + half * 128 + 128] = part

    def block(c, carry):
        cols = pl.ds(pl.multiple_of(c * WB, WB), WB)
        weights, band = weight_matrix(slot_ref, weight_ref, cols, WB)
        w0, w1, w2 = parts3(weights)
        right = jnp.concatenate([w0, w0, w0, w1, w1, w2], axis=0)
        mixed = jnp.dot(left_ref[...], right, preferred_element_type=F32)
        mine = lax.broadcasted_iota(I32, (TILES, WB), 0) == band
        east, north, density, gust = (
            jnp.sum(jnp.where(mine, mixed[i * 64 : i * 64 + 64], 0.0), axis=0, keepdims=True) for i in range(4)
        )
        speed = jnp.sqrt(east * east + north * north + 1.0)
        friction = jnp.sqrt(0.001 * (0.8 + 0.065 * speed)) * speed * (1.0 + 0.15 * gust)
        pull = 28.0 * friction
        share = 0.25 * (density / WATER_DENSITY)
        spread = lambda v: jnp.broadcast_to(v, (8, WB))
        east8, north8, speed8, pull8 = spread(east), spread(north), spread(speed), spread(pull)
        m0 = jnp.zeros((8, WB), F32)
        ms, mk, sx, sy = m0, m0, m0, m0
        for g in range(3):
            cos8, sin8 = cos_tiles[g], sin_tiles[g]
            push = pull8 * ((east8 * cos8 + north8 * sin8) / speed8)
            stress = jnp.zeros((8, WB), F32)
            for i in range(GS):
                spec = spec_ref[i, 8 * g : 8 * g + 8, cols]
                m0 = m0 + spec
                ms = ms + spec * inv_omega[i]
                mk = mk + spec * inv_root[i]
                excess = jnp.maximum(push * inv_c[i] - 1.0, 0.0)
                stress = stress + (excess * omega_c[i]) * spec
            sx = sx + stress * cos8
            sy = sy + stress * sin8
        down = lambda v: jnp.sum(v, axis=0, keepdims=True)
        for n, row in enumerate((down(m0), down(ms), down(mk), down(sx) * share, down(sy) * share)):
            for half in range(WB // 128):
                mom_ref[pl.ds(n * 16 + c * (WB // 128) + half, 1), :] = row[:, half * 128 : half * 128 + 128]
        for n, row in enumerate((east, north, density, speed, friction)):
            for half in range(WB // 128):
                wind_ref[pl.ds(n * 16 + c * (WB // 128) + half, 1), :] = row[:, half * 128 : half * 128 + 128]
        return carry

    lax.fori_loop(0, PTS // WB, block, 0, unroll=8)


def field_kernel(
    m0_ref, m1_ref, m2_ref, m3_ref, wind_ref, slot_hbm, weight_hbm, diss_ref, sums_ref, own_ref, slot_ref, weight_ref, sems
):
    copies = start_copies(((slot_hbm, slot_ref), (weight_hbm, weight_ref)), sems)
    moments = m0_ref[...] + m1_ref[...] + m2_ref[...] + m3_ref[...]
    total, inv_sigma, inv_root, stress_e, stress_n = (moments[16 * n : 16 * n + 16] for n in range(5))
    east, north, density, speed, friction = (wind_ref[16 * n : 16 * n + 16, :] for n in range(5))
    mean_sigma = total / inv_sigma
    mean_wavenum = jnp.square(total / inv_root)
    steepness = mean_wavenum * mean_wavenum * total * E_UNIT
    diss_ref[80:96, :] = DISSIP_COEF * mean_sigma * jnp.square(steepness / STEEP_PM) / mean_wavenum
    diss_ref[0:80, :] = wind_ref[...]
    scale = WATER_DENSITY / density * G_ACC * E_UNIT
    friction_sq = friction * friction
    east_ratio = scale * stress_e / friction_sq
    north_ratio = scale * stress_n / friction_sq
    aligned = (east_ratio * east + north_ratio * north) / speed
    charnock = 1.0 / jnp.sqrt(1.0 - 0.9 * aligned / (1.0 + jnp.abs(aligned)))
    height = 4.0 * jnp.sqrt(E_UNIT * total)
    f = lax.axis_index("freq")
    own_ref[...] = jnp.where(f == 0, east_ratio, jnp.where(f == 1, north_ratio, jnp.where(f == 2, charnock, height)))

    wait_copies(copies)

    def block(c, acc):
        cols = pl.ds(pl.multiple_of(c * WB, WB), WB)
        weights, band = weight_matrix(slot_ref, weight_ref, cols, WB)
        w0, w1 = parts2(weights)
        field = jnp.concatenate([own_ref[pl.ds(c * (WB // 128) + half, 1), :] for half in range(WB // 128)], axis=1)
        spread = jnp.where(lax.broadcasted_iota(I32, (TILES, WB), 0) == band, field, 0.0)
        f0, f1 = parts2(spread)
        left = jnp.concatenate([f0, f1, f0], axis=1)
        right = jnp.concatenate([w0, w0, w1], axis=1)
        return acc + lax.dot_general(left, right, (((1,), (1,)), ((), ())), preferred_element_type=F32)

    acc = lax.fori_loop(0, PTS // WB, block, jnp.zeros((TILES, CAP), F32), unroll=8)
    for half in range(2):
        sums_ref[:, half, :] = acc[:, half * 128 : half * 128 + 128]


def band_kernel(arrived_ref, rows_hbm, out_ref, rows_ref, sems):
    wait_copies(start_copies(((rows_hbm, rows_ref),), sems))

    def eight_tiles(q, acc):
        ones, values = [], []
        for t in range(8):
            index = rows_ref[pl.ds(q * 8 + t, 1), :]
            tile = arrived_ref[q * 8 + t]
            row = jnp.concatenate([tile[0:1, :], tile[1:2, :]], axis=1)
            v0, v1 = parts2(row)
            high = lax.broadcasted_iota(I32, (16, CAP), 0) == (index >> 7)
            v0, v1 = v0.astype(F32), v1.astype(F32)
            values.append(jnp.concatenate([jnp.where(high, v0, 0.0), jnp.where(high, v1, 0.0)], axis=0).astype(BF))
            match = lax.broadcasted_iota(jnp.int16, (128, CAP), 0) == (index & 127).astype(jnp.int16)
            ones.append(jnp.where(match, jnp.ones((), BF), jnp.zeros((), BF)))
        left = jnp.concatenate(ones, axis=1)
        right = jnp.concatenate(values, axis=1)
        return acc + lax.dot_general(left, right, (((1,), (1,)), ((), ())), preferred_element_type=F32)

    acc = lax.fori_loop(0, TILES // 8, eight_tiles, jnp.zeros((128, 32), F32), unroll=8)
    out_ref[...] = jnp.transpose(acc[:, :16] + acc[:, 16:])


def move_kernel(half, spec_ref, low_ref, high_ref, near_hbm, *refs):
    start = half * HALF
    if half == 0:
        out_hbm, rim_hbm, x_ref, near_ref, rim_ref, out_ref, sems, low_v, high_v, rim_sems = refs
        copies = start_copies(((near_hbm, near_ref),), sems)
        rim_loads = start_copies(((low_ref, low_v), (high_ref, high_v)), rim_sems)

        def put_block(h, carry):
            cols = pl.ds(pl.multiple_of(h * 128, 128), 128)
            put_parts(spec_ref, cols, x_ref, cols)
            return carry

        lax.fori_loop(0, PTS // 128, put_block, 0)
        wait_copies(rim_loads)
        put_parts(low_v, slice(0, RIM), rim_ref, slice(0, RIM))
        put_parts(high_v, slice(0, RIM), rim_ref, slice(RIM, 2 * RIM))
        stores = start_copies(((rim_ref, rim_hbm),), sems, 1)
    else:
        x_ref = high_ref
        out_hbm, near_ref, rim_ref, out_ref, sems = refs
        copies = start_copies(((near_hbm, near_ref), (low_ref, rim_ref)), sems)
        stores = []
    wait_copies(copies)
    scale = group_scale()[1]
    courant = jnp.concatenate([by_sublane(COURANT) * scale] * (NB // 128), axis=1)

    def hot(rows, index):
        match = lax.broadcasted_iota(jnp.int16, (rows, NB), 0) == index
        return jnp.where(match, jnp.ones((), BF), jnp.zeros((), BF))

    def block(c, carry):
        outs = pl.ds(pl.multiple_of(c * NB, NB), NB)
        cols = pl.ds(pl.multiple_of(start + c * NB, NB), NB)
        got = []
        for n, first in enumerate((0, 12, 6, 18)):
            index = near_ref[n : n + 1, cols]
            rim_index = jnp.where(index < RIM, index, jnp.where(index < RIM + PTS, 2 * RIM, index - PTS))
            rows = slice(first * 16, first * 16 + 192)
            own = jnp.dot(x_ref[rows, :], hot(PTS, (index - RIM).astype(jnp.int16)), preferred_element_type=F32)
            rim = jnp.dot(rim_ref[rows, :], hot(2 * RIM, rim_index.astype(jnp.int16)), preferred_element_type=F32)
            got.append(own + rim)
        for k in range(ND):
            a = (k + ROLL) % ND
            x_of = got[0] if a < 12 else got[1]
            a = a % 12
            y_of = got[2] if k < 12 else got[3]
            b = k % 12
            from_x = x_of[a * 16 : a * 16 + 8] + x_of[a * 16 + 8 : a * 16 + 16]
            from_y = y_of[b * 16 : b * 16 + 8] + y_of[b * 16 + 8 : b * 16 + 16]
            spec = spec_ref[:, k, cols]
            out_ref[:, k, outs] = (
                spec - (courant * abs(COS[k])) * (spec - from_x) - (courant * abs(SIN[k])) * (spec - from_y)
            )
        pltpu.make_async_copy(out_ref.at[:, :, outs], out_hbm.at[:, :, outs], sems.at[2 + c]).start()
        return carry

    lax.fori_loop(0, HALF // NB, block, 0)
    for c in range(HALF // NB):
        outs = pl.ds(c * NB, NB)
        pltpu.make_async_copy(out_ref.at[:, :, outs], out_hbm.at[:, :, outs], sems.at[2 + c]).wait()
    wait_copies(stores)


def source_kernel(moved0_hbm, moved1_hbm, wind_ref, out_hbm, push_ref, new_ref, moved0_ref, moved1_ref, loads, stores):
    pairs = []
    for i in range(GS):
        pairs += [(moved0_hbm.at[i], moved0_ref.at[i]), (moved1_hbm.at[i], moved1_ref.at[i])]
    copies = start_copies(pairs, loads)
    up = group_scale()[0]
    cos_tiles, sin_tiles = direction_tiles(COS), direction_tiles(SIN)

    def spread(c):
        row = lambda n: jnp.broadcast_to(wind_ref[pl.ds(n * 16 + c, 1), :], (8, 128))
        return [row(n) for n in range(5)]

    def prepare(c, carry):
        east, north, density, speed, friction = spread(c)
        pull = 28.0 * friction / speed
        for g in range(3):
            push_ref[c, 8 * g : 8 * g + 8, :] = pull * (east * cos_tiles[g] + north * sin_tiles[g])
        push_ref[c, 24:32, :] = (0.25 * DT_SRC) * (density / WATER_DENSITY)
        push_ref[c, 32:40, :] = DT_SRC * jnp.broadcast_to(wind_ref[pl.ds(80 + c, 1), :], (8, 128))
        return carry

    lax.fori_loop(0, PTS // 128, prepare, 0)
    for i in range(GS):
        inv_c, omega, wavenum = OMEGA[i] / G_ACC * up, OMEGA[i] * up, OMEGA[i] ** 2 / G_ACC * (up * up)
        wait_copies(copies[2 * i : 2 * i + 2])
        for half, moved_ref in ((0, moved0_ref), (1, moved1_ref)):

            def block(c, carry):
                at = c + half * (HALF // 128)
                cols = pl.ds(pl.multiple_of(c * 128, 128), 128)
                outs = pl.ds(pl.multiple_of(at * 128, 128), 128)
                share, loss = push_ref[at, 24:32, :] * omega, push_ref[at, 32:40, :] * wavenum
                for g in range(3):
                    rows = slice(8 * g, 8 * g + 8)
                    excess = jnp.maximum(push_ref[at, rows, :] * inv_c - 1.0, 0.0)
                    new_ref[i, rows, outs] = moved_ref[i, rows, cols] * jnp.exp(share * excess - loss)
                return carry

            lax.fori_loop(0, HALF // 128, block, 0, unroll=4)
        pltpu.make_async_copy(new_ref.at[i], out_hbm.at[i], stores.at[i]).start()
    for i in range(GS):
        pltpu.make_async_copy(new_ref.at[i], out_hbm.at[i], stores.at[i]).wait()


VMEM = pl.BlockSpec(memory_space=pltpu.VMEM)
HBM = pl.BlockSpec(memory_space=pltpu.HBM)


def array(*dims, dtype=F32):
    return jax.ShapeDtypeStruct(dims, dtype)


def resident(*dims, dtype=F32):
    return pltpu.VMEM(dims, dtype)


def distant(*dims, dtype=F32):
    return pltpu.HBM(dims, dtype)


def in_hbm(x):
    return pltpu.with_memory_space_constraint(x, pltpu.HBM)


def call(body, name, out, specs, scratch=(), mib=24, microseconds=1.0, out_specs=None, behind=False, mark=False):
    out = list(out)
    out_specs = [VMEM] * len(out) if out_specs is None else list(out_specs)
    specs = [*specs, VMEM] if behind else specs
    inputs = len(specs) - behind
    outputs = len(out)
    if mark:
        out.append(resident(8, 128))
        out_specs.append(VMEM)

    def kernel(*refs):
        results = inputs + behind
        if mark:
            refs[results + outputs][...] = jnp.zeros((8, 128), F32)
        body(*refs[:inputs], *refs[results : results + outputs], *refs[results + outputs + mark :])

    cost = pl.CostEstimate(flops=0, bytes_accessed=int(microseconds * 3.0e6), transcendentals=0)
    return pl.pallas_call(
        kernel,
        out_shape=out,
        in_specs=specs,
        out_specs=out_specs,
        scratch_shapes=list(scratch),
        name=name,
        cost_estimate=cost,
        compiler_params=pltpu.CompilerParams(vmem_limit_bytes=mib * 2**20),
    )


def on_device(spectrum, forcing, send_rows, point_slot, remap_weight, neighbours, halo_send):
    dma = pltpu.SemaphoreType.DMA
    to_before, to_after, spec, mark = call(
        rim_kernel,
        "rims",
        [distant(GS, ND, RIM), distant(GS, ND, RIM), resident(GS, ND, PTS)],
        [HBM] * 2,
        [
            pltpu.VMEM((2, RIM), I32),
            pltpu.VMEM((GS, ND, RIM), F32),
            pltpu.VMEM((GS, ND, RIM), F32),
            dma((2,)),
        ],
        microseconds=3.0,
        out_specs=[HBM, HBM, VMEM],
        mark=True,
    )(in_hbm(halo_send.reshape(2, RIM)), in_hbm(spectrum))
    up = [(d, d + 1) for d in range(TILES - 1)]
    low_rim = lax.ppermute(to_after, "tile", up)
    high_rim = lax.ppermute(to_before, "tile", [(b, a) for a, b in up])

    outgoing, mark = call(
        outgoing_kernel,
        "outgoing",
        [distant(TILES, 8, 128)],
        [HBM] * 2,
        [
            pltpu.VMEM((TILES, CAP), I32),
            pltpu.VMEM((4, PTS), F32),
            pltpu.VMEM((TILES, 8, 128), F32),
            dma((2,)),
            dma((TILES // 8,)),
        ],
        microseconds=3.0,
        out_specs=[HBM],
        behind=True,
        mark=True,
    )(in_hbm(send_rows), in_hbm(forcing), mark)
    outgoing, low_rim, high_rim = lax.optimization_barrier((outgoing, low_rim, high_rim))
    arrived = lax.all_to_all(outgoing, "tile", split_axis=0, concat_axis=0, tiled=True)

    blocks = HALF // NB
    scratch = [
        pltpu.VMEM((4, PTS), I32),
        pltpu.VMEM((KCOPIES * 16, 2 * RIM), BF),
        pltpu.VMEM((GS, ND, HALF), F32),
        dma((2 + blocks,)),
    ]
    moved0, rims, operand, mark = call(
        functools.partial(move_kernel, 0),
        "move0",
        [
            distant(GS, ND, HALF),
            distant(KCOPIES * 16, 2 * RIM, dtype=BF),
            resident(KCOPIES * 16, PTS, dtype=BF),
        ],
        [VMEM] + [HBM] * 3,
        scratch + [pltpu.VMEM((GS, ND, RIM), F32), pltpu.VMEM((GS, ND, RIM), F32), dma((2,))],
        microseconds=7.5,
        out_specs=[HBM, HBM, VMEM],
        behind=True,
        mark=True,
    )(spec, in_hbm(low_rim), in_hbm(high_rim), in_hbm(neighbours), mark)
    wind, moments, mark = call(
        wind_kernel,
        "wind",
        [array(80, 128), array(80, 128)],
        [HBM, HBM, HBM, VMEM],
        [
            pltpu.VMEM((256, 6 * 256), BF),
            pltpu.VMEM((TILES, 8, 128), F32),
            pltpu.VMEM((4, PTS), I32),
            pltpu.VMEM((4, PTS), F32),
            dma((3,)),
        ],
        microseconds=6.0,
        behind=True,
        mark=True,
    )(in_hbm(arrived), in_hbm(point_slot), in_hbm(remap_weight), spec, mark)
    others = [lax.ppermute(moments, "freq", [(i, (i + n) % 4) for i in range(4)]) for n in (1, 2, 3)]
    moved1, mark = call(
        functools.partial(move_kernel, 1),
        "move1",
        [distant(GS, ND, HALF)],
        [VMEM, HBM, VMEM, HBM],
        scratch,
        microseconds=5.0,
        out_specs=[HBM],
        behind=True,
        mark=True,
    )(spec, rims, operand, in_hbm(neighbours), mark)

    state, slot_sums = call(
        field_kernel,
        "fields",
        [resident(96, 128), array(TILES, 2, 128)],
        [VMEM] * 5 + [HBM] * 2,
        [pltpu.VMEM((16, 128), F32), pltpu.VMEM((4, PTS), I32), pltpu.VMEM((4, PTS), F32), dma((2,))],
        microseconds=3.0,
        behind=True,
    )(moments, *others, wind, in_hbm(point_slot), in_hbm(remap_weight), mark)
    arrived_sums = lax.all_to_all(slot_sums, "tile", split_axis=0, concat_axis=0, tiled=True)

    new_spectrum, mark = call(
        source_kernel,
        "source",
        [array(GS, ND, PTS)],
        [HBM, HBM, VMEM],
        [
            pltpu.VMEM((PTS // 128, 40, 128), F32),
            pltpu.VMEM((GS, ND, PTS), F32),
            pltpu.VMEM((GS, ND, HALF), F32),
            pltpu.VMEM((GS, ND, HALF), F32),
            dma((2 * GS,)),
            dma((GS,)),
        ],
        microseconds=3.0,
        out_specs=[HBM],
        mark=True,
    )(in_hbm(moved0), in_hbm(moved1), state)

    (returned,) = call(
        band_kernel,
        "band",
        [array(16, 128)],
        [VMEM, HBM],
        [pltpu.VMEM((TILES, CAP), I32), dma((1,))],
        microseconds=2.5,
        behind=True,
    )(arrived_sums, in_hbm(send_rows), mark)
    return (new_spectrum, returned.reshape(1, PTS))


def solution(mesh):
    placed = (
        P("freq", None, "tile"),
        P(None, "tile"),
        P("tile", None),
        P(None, "tile"),
        P(None, "tile"),
        P(None, "tile"),
        P("tile"),
    )
    return jax.shard_map(
        on_device,
        mesh=mesh,
        in_specs=placed,
        out_specs=(P("freq", None, "tile"), P("freq", "tile")),
        check_vma=False,
    )
```

```python
import functools
import math

import jax
import jax.numpy as jnp
from jax import lax
from jax.experimental import pallas as pl
from jax.experimental.pallas import tpu as pltpu
from jax.sharding import PartitionSpec as P

G_ACC = 9.81
WATER_DENSITY = 1025.0
FREQ_LOW = 0.03453
FREQ_RATIO = 1.1
E_UNIT = 0.001
DT_SRC = 120.0
COURANT_MAX = 0.7
DISSIP_COEF = 2.33e-05
STEEP_PM = 0.00302
TOP_EXPONENT = 31.0

NF = 32
ND = 24
GS = 8
PTS = 2048
TILES = 64
CAP = 256
RIM = 128
EXT = PTS + 2 * RIM

F32 = jnp.float32
BF = jnp.bfloat16
I32 = jnp.int32

THETA = [(k + 0.5) * 2.0 * math.pi / ND for k in range(ND)]
COS = [math.cos(t) for t in THETA]
SIN = [math.sin(t) for t in THETA]

OMEGA = [2.0 * math.pi * FREQ_LOW * FREQ_RATIO**i for i in range(GS)]
COURANT = [COURANT_MAX * FREQ_RATIO ** (-i) for i in range(GS)]


def group_scale():
    f = lax.axis_index("freq")
    pick = lambda v: jnp.where(f == 0, v[0], jnp.where(f == 1, v[1], jnp.where(f == 2, v[2], v[3]))).astype(F32)
    return pick([FREQ_RATIO ** (GS * n) for n in range(4)]), pick([FREQ_RATIO ** (-GS * n) for n in range(4)])


def by_sublane(values):
    which = lax.broadcasted_iota(I32, (8, 128), 0)
    tile = jnp.full((8, 128), values[7], F32)
    for n in range(7):
        tile = jnp.where(which == n, values[n], tile)
    return tile


def direction_tiles(values):
    return [by_sublane(values[8 * g : 8 * g + 8]) for g in range(3)]


def lane_gather(block, index):
    return jnp.take_along_axis(block, index, axis=1, mode="promise_in_bounds")


def parts2(x):
    first = x.astype(BF)
    return first, (x - first.astype(F32)).astype(BF)


def parts3(x):
    first = x.astype(BF)
    rest = x - first.astype(F32)
    second = rest.astype(BF)
    return first, second, (rest - second.astype(F32)).astype(BF)


ROLL = 6
NB = 512
HALF = PTS // 2


def put_parts(ref, source, x_ref, target):
    for kp in range(ND):
        v = ref[:, (kp + ND - ROLL) % ND, source]
        p0 = v.astype(BF).astype(F32)
        x_ref[kp * 16 : kp * 16 + 16, target] = jnp.concatenate([p0, v - p0], axis=0).astype(BF)


def start_copies(pairs, sems, first=0):
    copies = [pltpu.make_async_copy(src, dst, sems.at[first + n]) for n, (src, dst) in enumerate(pairs)]
    for copy in copies:
        copy.start()
    return copies


def wait_copies(copies):
    for copy in copies:
        copy.wait()


def start_copies(pairs, sems, first=0):
    copies = [pltpu.make_async_copy(src, dst, sems.at[first + n]) for n, (src, dst) in enumerate(pairs)]
    for copy in copies:
        copy.start()
    return copies


def wait_copies(copies):
    for copy in copies:
        copy.wait()


def start_copies(pairs, sems, first=0):
    copies = [pltpu.make_async_copy(src, dst, sems.at[first + n]) for n, (src, dst) in enumerate(pairs)]
    for copy in copies:
        copy.start()
    return copies


def wait_copies(copies):
    for copy in copies:
        copy.wait()


def rim_kernel(
    list_hbm, spec_hbm, near_hbm, slot_hbm, weight_hbm, before_hbm, after_hbm, spec_ref,
    near_ref, slot_ref, weight_ref, list_ref, before_ref, after_ref, sems,
):
    pairs = ((list_hbm, list_ref), (spec_hbm, spec_ref))
    first = start_copies(pairs + ((near_hbm, near_ref), (slot_hbm, slot_ref), (weight_hbm, weight_ref)), sems)
    wait_copies(first[:2])
    rims = []
    for side, rim_ref in ((0, before_ref), (1, after_ref)):
        index = jnp.broadcast_to(list_ref[side : side + 1, :], (8, 128))
        rims.append((index & 127, index >> 7, rim_ref))

    def step(i, carry):
        for low, high, rim_ref in rims:
            for g in range(3):
                rows = slice(8 * g, 8 * g + 8)
                got = None
                for h in range(16):
                    piece = lane_gather(spec_ref[i, rows, h * 128 : h * 128 + 128], low)
                    got = piece if h == 0 else jnp.where(high == h, piece, got)
                rim_ref[i, rows, :] = got
        return carry

    lax.fori_loop(0, GS, step, 0)
    last = start_copies(((before_ref, before_hbm), (after_ref, after_hbm)), sems)
    wait_copies(first[2:])
    wait_copies(last)


def outgoing_kernel(rows_hbm, forcing_hbm, out_hbm, rows_ref, forcing_ref, out_ref, sems, out_sems):
    wait_copies(start_copies(((rows_hbm, rows_ref), (forcing_hbm, forcing_ref)), sems))

    def step(q, carry):
        d = pl.ds(pl.multiple_of(q * 8, 8), 8)
        for half in range(2):
            index = rows_ref[d, half * 128 : half * 128 + 128]
            low, high = index & 127, index >> 7
            for i in range(4):
                got = None
                for h in range(16):
                    block = jnp.broadcast_to(forcing_ref[i : i + 1, h * 128 : h * 128 + 128], (8, 128))
                    piece = lane_gather(block, low)
                    got = piece if h == 0 else jnp.where(high == h, piece, got)
                out_ref[d, 2 * i + half, :] = got
        pltpu.make_async_copy(out_ref.at[d], out_hbm.at[d], out_sems.at[q]).start()
        return carry

    lax.fori_loop(0, TILES // 8, step, 0, unroll=2)
    for q in range(TILES // 8):
        d = pl.ds(q * 8, 8)
        pltpu.make_async_copy(out_ref.at[d], out_hbm.at[d], out_sems.at[q]).wait()


def weight_matrix(slot_ref, weight_ref, cols, width):
    slots = lax.broadcasted_iota(I32, (CAP, width), 0)
    total = None
    for j in range(4):
        place = slot_ref[j : j + 1, cols]
        term = jnp.where(slots == (place & (CAP - 1)), weight_ref[j : j + 1, cols], 0.0)
        total = term if j == 0 else total + term
    return total, place >> 8


WB = 256


def wind_kernel(
    x_in_ref, arrived_ref, spec_hbm, low_ref, high_ref, slot_ref, weight_ref, x_ref, wind_ref, mom_ref,
    left_ref, spec_ref, sems,
):
    copies = start_copies(((spec_hbm, spec_ref),), sems)
    up, down_scale = group_scale()
    inv_c = [w / G_ACC * up for w in OMEGA]
    inv_omega = [1.0 / w * down_scale for w in OMEGA]
    inv_root = [math.sqrt(G_ACC) / w * down_scale for w in OMEGA]
    omega_c = [w * w / G_ACC * (up * up) for w in OMEGA]
    cos_tiles = [jnp.concatenate([t] * (WB // 128), axis=1) for t in direction_tiles(COS)]
    sin_tiles = [jnp.concatenate([t] * (WB // 128), axis=1) for t in direction_tiles(SIN)]
    put_parts(low_ref, slice(0, RIM), x_ref, slice(0, RIM))
    put_parts(high_ref, slice(0, RIM), x_ref, slice(EXT - RIM, EXT))
    for i in range(4):
        for half in range(2):
            p0, p1, p2 = parts3(arrived_ref[:, 2 * i + half, :])
            for n, part in enumerate((p0, p1, p2, p0, p1, p0)):
                left_ref[i * 64 : i * 64 + 64, n * 256 + half * 128 : n * 256 + half * 128 + 128] = part

    wait_copies(copies)

    def block(c, carry):
        cols = pl.ds(pl.multiple_of(c * WB, WB), WB)
        weights, band = weight_matrix(slot_ref, weight_ref, cols, WB)
        w0, w1, w2 = parts3(weights)
        right = jnp.concatenate([w0, w0, w0, w1, w1, w2], axis=0)
        mixed = jnp.dot(left_ref[...], right, preferred_element_type=F32)
        mine = lax.broadcasted_iota(I32, (TILES, WB), 0) == band
        east, north, density, gust = (
            jnp.sum(jnp.where(mine, mixed[i * 64 : i * 64 + 64], 0.0), axis=0, keepdims=True) for i in range(4)
        )
        speed = jnp.sqrt(east * east + north * north + 1.0)
        friction = jnp.sqrt(0.001 * (0.8 + 0.065 * speed)) * speed * (1.0 + 0.15 * gust)
        pull = 28.0 * friction
        share = 0.25 * (density / WATER_DENSITY)
        spread = lambda v: jnp.broadcast_to(v, (8, WB))
        east8, north8, speed8, pull8 = spread(east), spread(north), spread(speed), spread(pull)
        m0 = jnp.zeros((8, WB), F32)
        ms, mk, sx, sy = m0, m0, m0, m0
        for g in range(3):
            cos8, sin8 = cos_tiles[g], sin_tiles[g]
            push = pull8 * ((east8 * cos8 + north8 * sin8) / speed8)
            stress = jnp.zeros((8, WB), F32)
            for i in range(GS):
                spec = spec_ref[i, 8 * g : 8 * g + 8, cols]
                m0 = m0 + spec
                ms = ms + spec * inv_omega[i]
                mk = mk + spec * inv_root[i]
                excess = jnp.maximum(push * inv_c[i] - 1.0, 0.0)
                stress = stress + (excess * omega_c[i]) * spec
            sx = sx + stress * cos8
            sy = sy + stress * sin8
        down = lambda v: jnp.sum(v, axis=0, keepdims=True)
        for n, row in enumerate((down(m0), down(ms), down(mk), down(sx) * share, down(sy) * share)):
            for half in range(WB // 128):
                mom_ref[pl.ds(n * 16 + c * (WB // 128) + half, 1), :] = row[:, half * 128 : half * 128 + 128]
        for n, row in enumerate((east, north, density, speed, friction)):
            for half in range(WB // 128):
                wind_ref[pl.ds(n * 16 + c * (WB // 128) + half, 1), :] = row[:, half * 128 : half * 128 + 128]
        return carry

    lax.fori_loop(0, PTS // WB, block, 0, unroll=8)


def field_kernel(
    m0_ref, m1_ref, m2_ref, m3_ref, wind_ref, slot_ref, weight_ref, diss_ref, sums_hbm,
    own_ref, sums_ref, sems,
):
    moments = m0_ref[...] + m1_ref[...] + m2_ref[...] + m3_ref[...]
    total, inv_sigma, inv_root, stress_e, stress_n = (moments[16 * n : 16 * n + 16] for n in range(5))
    east, north, density, speed, friction = (wind_ref[16 * n : 16 * n + 16, :] for n in range(5))
    mean_sigma = total / inv_sigma
    mean_wavenum = jnp.square(total / inv_root)
    steepness = mean_wavenum * mean_wavenum * total * E_UNIT
    diss_ref[80:96, :] = DISSIP_COEF * mean_sigma * jnp.square(steepness / STEEP_PM) / mean_wavenum
    diss_ref[0:80, :] = wind_ref[...]
    scale = WATER_DENSITY / density * G_ACC * E_UNIT
    friction_sq = friction * friction
    east_ratio = scale * stress_e / friction_sq
    north_ratio = scale * stress_n / friction_sq
    aligned = (east_ratio * east + north_ratio * north) / speed
    charnock = 1.0 / jnp.sqrt(1.0 - 0.9 * aligned / (1.0 + jnp.abs(aligned)))
    height = 4.0 * jnp.sqrt(E_UNIT * total)
    f = lax.axis_index("freq")
    own_ref[...] = jnp.where(f == 0, east_ratio, jnp.where(f == 1, north_ratio, jnp.where(f == 2, charnock, height)))


    def block(c, acc):
        cols = pl.ds(pl.multiple_of(c * WB, WB), WB)
        weights, band = weight_matrix(slot_ref, weight_ref, cols, WB)
        w0, w1 = parts2(weights)
        field = jnp.concatenate([own_ref[pl.ds(c * (WB // 128) + half, 1), :] for half in range(WB // 128)], axis=1)
        spread = jnp.where(lax.broadcasted_iota(I32, (TILES, WB), 0) == band, field, 0.0)
        f0, f1 = parts2(spread)
        left = jnp.concatenate([f0, f1, f0], axis=1)
        right = jnp.concatenate([w0, w0, w1], axis=1)
        return acc + lax.dot_general(left, right, (((1,), (1,)), ((), ())), preferred_element_type=F32)

    acc = lax.fori_loop(0, PTS // WB, block, jnp.zeros((TILES, CAP), F32), unroll=8)
    for half in range(2):
        sums_ref[:, half, :] = acc[:, half * 128 : half * 128 + 128]
    wait_copies(start_copies(((sums_ref, sums_hbm),), sems))


def band_kernel(arrived_ref, rows_ref, out_ref):
    def eight_tiles(q, acc):
        ones, values = [], []
        for t in range(8):
            index = rows_ref[pl.ds(q * 8 + t, 1), :]
            tile = arrived_ref[q * 8 + t]
            row = jnp.concatenate([tile[0:1, :], tile[1:2, :]], axis=1)
            v0, v1 = parts2(row)
            high = lax.broadcasted_iota(I32, (16, CAP), 0) == (index >> 7)
            v0, v1 = v0.astype(F32), v1.astype(F32)
            values.append(jnp.concatenate([jnp.where(high, v0, 0.0), jnp.where(high, v1, 0.0)], axis=0).astype(BF))
            match = lax.broadcasted_iota(jnp.int16, (128, CAP), 0) == (index & 127).astype(jnp.int16)
            ones.append(jnp.where(match, jnp.ones((), BF), jnp.zeros((), BF)))
        left = jnp.concatenate(ones, axis=1)
        right = jnp.concatenate(values, axis=1)
        return acc + lax.dot_general(left, right, (((1,), (1,)), ((), ())), preferred_element_type=F32)

    acc = lax.fori_loop(0, TILES // 8, eight_tiles, jnp.zeros((128, 32), F32), unroll=8)
    out_ref[...] = jnp.transpose(acc[:, :16] + acc[:, 16:])


def operand_kernel(spec_ref, x_ref):
    def put_block(h, carry):
        cols = pl.ds(pl.multiple_of(h * 128, 128), 128)
        put_parts(spec_ref, cols, x_ref, pl.ds(pl.multiple_of(h * 128 + RIM, 128), 128))
        return carry

    lax.fori_loop(0, PTS // 128, put_block, 0)


def move_kernel(half, near_ref, x_ref, out_ref):
    start = half * HALF
    scale = group_scale()[1]
    courant = jnp.concatenate([by_sublane(COURANT) * scale] * (NB // 128), axis=1)

    def hot(index):
        match = lax.broadcasted_iota(jnp.int16, (EXT, NB), 0) == index.astype(jnp.int16)
        return jnp.where(match, jnp.ones((), BF), jnp.zeros((), BF))

    def block(c, carry):
        outs = pl.ds(pl.multiple_of(c * NB, NB), NB)
        cols = pl.ds(pl.multiple_of(start + c * NB, NB), NB)
        own = pl.ds(pl.multiple_of(start + c * NB + RIM, RIM), NB)
        got = []
        for n, first in enumerate((0, 12, 6, 18)):
            index = near_ref[n : n + 1, cols]
            if first + 12 <= ND:
                left = x_ref[first * 16 : first * 16 + 192, :]
            else:
                left = jnp.concatenate([x_ref[first * 16 :, :], x_ref[: (first - 12) * 16, :]], axis=0)
            got.append(jnp.dot(left, hot(index), preferred_element_type=F32))
        for k in range(ND):
            kp = (k + ROLL) % ND
            x_of = got[0] if kp < 12 else got[1]
            a = kp % 12
            y_of = got[2] if k < 12 else got[3]
            b = k % 12
            from_x = x_of[a * 16 : a * 16 + 8] + x_of[a * 16 + 8 : a * 16 + 16]
            from_y = y_of[b * 16 : b * 16 + 8] + y_of[b * 16 + 8 : b * 16 + 16]
            both = x_ref[kp * 16 : kp * 16 + 16, own].astype(F32)
            spec = both[:8] + both[8:]
            out_ref[:, k, outs] = (
                spec - (courant * abs(COS[k])) * (spec - from_x) - (courant * abs(SIN[k])) * (spec - from_y)
            )
        return carry

    lax.fori_loop(0, HALF // NB, block, 0)


def source_kernel(moved0_ref, moved1_ref, wind_ref, out_hbm, push_ref, new_ref, stores):
    up = group_scale()[0]
    cos_tiles, sin_tiles = direction_tiles(COS), direction_tiles(SIN)

    def spread(c):
        row = lambda n: jnp.broadcast_to(wind_ref[pl.ds(n * 16 + c, 1), :], (8, 128))
        return [row(n) for n in range(5)]

    def prepare(c, carry):
        east, north, density, speed, friction = spread(c)
        pull = 28.0 * friction / speed
        for g in range(3):
            push_ref[c, 8 * g : 8 * g + 8, :] = pull * (east * cos_tiles[g] + north * sin_tiles[g])
        push_ref[c, 24:32, :] = (0.25 * DT_SRC) * (density / WATER_DENSITY)
        push_ref[c, 32:40, :] = DT_SRC * jnp.broadcast_to(wind_ref[pl.ds(80 + c, 1), :], (8, 128))
        return carry

    lax.fori_loop(0, PTS // 128, prepare, 0)
    for i in range(GS):
        inv_c, omega, wavenum = OMEGA[i] / G_ACC * up, OMEGA[i] * up, OMEGA[i] ** 2 / G_ACC * (up * up)

        for half, moved_ref in ((0, moved0_ref), (1, moved1_ref)):

            def block(c, carry):
                at = c + half * (HALF // 128)
                cols = pl.ds(pl.multiple_of(c * 128, 128), 128)
                outs = pl.ds(pl.multiple_of(at * 128, 128), 128)
                share, loss = push_ref[at, 24:32, :] * omega, push_ref[at, 32:40, :] * wavenum
                for g in range(3):
                    rows = slice(8 * g, 8 * g + 8)
                    excess = jnp.maximum(push_ref[at, rows, :] * inv_c - 1.0, 0.0)
                    new_ref[i, rows, outs] = moved_ref[i, rows, cols] * jnp.exp(share * excess - loss)
                return carry

            lax.fori_loop(0, HALF // 128, block, 0, unroll=4)
        pltpu.make_async_copy(new_ref.at[i], out_hbm.at[i], stores.at[i]).start()
    for i in range(GS):
        pltpu.make_async_copy(new_ref.at[i], out_hbm.at[i], stores.at[i]).wait()


VMEM = pl.BlockSpec(memory_space=pltpu.VMEM)
HBM = pl.BlockSpec(memory_space=pltpu.HBM)


def array(*dims, dtype=F32):
    return jax.ShapeDtypeStruct(dims, dtype)


def resident(*dims, dtype=F32):
    return pltpu.VMEM(dims, dtype)


def distant(*dims, dtype=F32):
    return pltpu.HBM(dims, dtype)


def in_hbm(x):
    return pltpu.with_memory_space_constraint(x, pltpu.HBM)


def call(body, name, out, specs, scratch=(), mib=24, microseconds=1.0, out_specs=None, behind=False, mark=False, aliases={}):
    out = list(out)
    out_specs = [VMEM] * len(out) if out_specs is None else list(out_specs)
    specs = [*specs, VMEM] if behind else specs
    inputs = len(specs) - behind
    outputs = len(out)
    if mark:
        out.append(resident(8, 128))
        out_specs.append(VMEM)

    def kernel(*refs):
        results = inputs + behind
        if mark:
            refs[results + outputs][...] = jnp.zeros((8, 128), F32)
        body(*refs[:inputs], *refs[results : results + outputs], *refs[results + outputs + mark :])

    cost = pl.CostEstimate(flops=0, bytes_accessed=int(microseconds * 3.0e6), transcendentals=0)
    return pl.pallas_call(
        kernel,
        out_shape=out,
        in_specs=specs,
        out_specs=out_specs,
        scratch_shapes=list(scratch),
        name=name,
        input_output_aliases=aliases,
        cost_estimate=cost,
        compiler_params=pltpu.CompilerParams(vmem_limit_bytes=int(mib * 2**20)),
    )


def on_device(spectrum, forcing, send_rows, point_slot, remap_weight, neighbours, halo_send):
    dma = pltpu.SemaphoreType.DMA
    outgoing, rows, mark = call(
        outgoing_kernel,
        "outgoing",
        [distant(TILES, 8, 128), resident(TILES, CAP, dtype=I32)],
        [HBM] * 2,
        [
            pltpu.VMEM((4, PTS), F32),
            pltpu.VMEM((TILES, 8, 128), F32),
            dma((2,)),
            dma((TILES // 8,)),
        ],
        microseconds=3.0,
        out_specs=[HBM, VMEM],
        mark=True,
    )(in_hbm(send_rows), in_hbm(forcing))
    arrived = lax.all_to_all(outgoing, "tile", split_axis=0, concat_axis=0, tiled=True)

    to_before, to_after, spec, near, slot, weight, mark = call(
        rim_kernel,
        "rims",
        [distant(GS, ND, RIM), distant(GS, ND, RIM), resident(GS, ND, PTS)]
        + [resident(4, PTS, dtype=I32), resident(4, PTS, dtype=I32), resident(4, PTS)],
        [HBM] * 5,
        [
            pltpu.VMEM((2, RIM), I32),
            pltpu.VMEM((GS, ND, RIM), F32),
            pltpu.VMEM((GS, ND, RIM), F32),
            dma((5,)),
        ],
        microseconds=3.0,
        out_specs=[HBM, HBM] + [VMEM] * 4,
        behind=True,
        mark=True,
    )(*map(in_hbm, (halo_send.reshape(2, RIM), spectrum, neighbours, point_slot, remap_weight)), mark)
    up = [(d, d + 1) for d in range(TILES - 1)]
    low_rim = lax.ppermute(to_after, "tile", up)
    high_rim = lax.ppermute(to_before, "tile", [(b, a) for a, b in up])
    operand, mark = call(
        operand_kernel,
        "operand",
        [resident(ND * 16, EXT, dtype=BF)],
        [VMEM],
        microseconds=3.0,
        behind=True,
        mark=True,
    )(spec, mark)

    operand, wind, moments, mark = call(
        wind_kernel,
        "wind",
        [resident(ND * 16, EXT, dtype=BF), array(80, 128), array(80, 128)],
        [VMEM, VMEM, HBM] + [VMEM] * 4,
        [pltpu.VMEM((256, 6 * 256), BF), pltpu.VMEM((GS, ND, PTS), F32), dma((1,))],
        microseconds=6.0,
        behind=True,
        mark=True,
        aliases={0: 0},
    )(operand, arrived, in_hbm(spectrum), low_rim, high_rim, slot, weight, mark)
    others = [lax.ppermute(moments, "freq", [(i, (i + n) % 4) for i in range(4)]) for n in (1, 2, 3)]

    def move(half, mark):
        return call(
            functools.partial(move_kernel, half),
            f"move{half}",
            [resident(GS, ND, HALF)],
            [VMEM] * 2,
            microseconds=5.5,
            behind=True,
            mark=True,
        )(near, operand, mark)

    moved0, mark = move(0, mark)
    state, slot_sums, mark = call(
        field_kernel,
        "fields",
        [resident(96, 128), distant(TILES, 2, 128)],
        [VMEM] * 7,
        [
            pltpu.VMEM((16, 128), F32),
            pltpu.VMEM((TILES, 2, 128), F32),
            dma((1,)),
        ],
        microseconds=3.0,
        out_specs=[VMEM, HBM],
        behind=True,
        mark=True,
    )(moments, *others, wind, slot, weight, mark)
    arrived_sums = lax.all_to_all(slot_sums, "tile", split_axis=0, concat_axis=0, tiled=True)

    moved1, mark = move(1, mark)
    new_spectrum, mark = call(
        source_kernel,
        "source",
        [array(GS, ND, PTS)],
        [VMEM] * 3,
        [pltpu.VMEM((PTS // 128, 40, 128), F32), pltpu.VMEM((GS, ND, PTS), F32), dma((GS,))],
        microseconds=3.0,
        out_specs=[HBM],
        behind=True,
        mark=True,
    )(moved0, moved1, state, mark)

    (returned,) = call(
        band_kernel,
        "band",
        [array(16, 128)],
        [VMEM] * 2,
        microseconds=2.5,
        behind=True,
    )(arrived_sums, rows, mark)
    return (new_spectrum, returned.reshape(1, PTS))


def solution(mesh):
    placed = (
        P("freq", None, "tile"),
        P(None, "tile"),
        P("tile", None),
        P(None, "tile"),
        P(None, "tile"),
        P(None, "tile"),
        P("tile"),
    )
    return jax.shard_map(
        on_device,
        mesh=mesh,
        in_specs=placed,
        out_specs=(P("freq", None, "tile"), P("freq", "tile")),
        check_vma=False,
    )
```

```python
import functools
import math

import jax
import jax.numpy as jnp
from jax import lax
from jax.experimental import pallas as pl
from jax.experimental.pallas import tpu as pltpu
from jax.sharding import PartitionSpec as P

G_ACC = 9.81
WATER_DENSITY = 1025.0
FREQ_LOW = 0.03453
FREQ_RATIO = 1.1
E_UNIT = 0.001
DT_SRC = 120.0
COURANT_MAX = 0.7
DISSIP_COEF = 2.33e-05
STEEP_PM = 0.00302
TOP_EXPONENT = 31.0

NF = 32
ND = 24
GS = 8
PTS = 2048
TILES = 64
CAP = 256
RIM = 128
EXT = PTS + 2 * RIM

F32 = jnp.float32
BF = jnp.bfloat16
I32 = jnp.int32

THETA = [(k + 0.5) * 2.0 * math.pi / ND for k in range(ND)]
COS = [math.cos(t) for t in THETA]
SIN = [math.sin(t) for t in THETA]

OMEGA = [2.0 * math.pi * FREQ_LOW * FREQ_RATIO**i for i in range(GS)]
COURANT = [COURANT_MAX * FREQ_RATIO ** (-i) for i in range(GS)]


def group_scale():
    f = lax.axis_index("freq")
    pick = lambda v: jnp.where(f == 0, v[0], jnp.where(f == 1, v[1], jnp.where(f == 2, v[2], v[3]))).astype(F32)
    return pick([FREQ_RATIO ** (GS * n) for n in range(4)]), pick([FREQ_RATIO ** (-GS * n) for n in range(4)])


def by_sublane(values):
    which = lax.broadcasted_iota(I32, (8, 128), 0)
    tile = jnp.full((8, 128), values[7], F32)
    for n in range(7):
        tile = jnp.where(which == n, values[n], tile)
    return tile


def direction_tiles(values):
    return [by_sublane(values[8 * g : 8 * g + 8]) for g in range(3)]


def lane_gather(block, index):
    return jnp.take_along_axis(block, index, axis=1, mode="promise_in_bounds")


def parts2(x):
    first = x.astype(BF)
    return first, (x - first.astype(F32)).astype(BF)


def parts3(x):
    first = x.astype(BF)
    rest = x - first.astype(F32)
    second = rest.astype(BF)
    return first, second, (rest - second.astype(F32)).astype(BF)


ROLL = 6
NB = 512
PARTS = ((0, 1024), (1024, PTS - 1024))


def put_parts(ref, source, x_ref, target):
    for kp in range(ND):
        v = ref[:, (kp + ND - ROLL) % ND, source]
        p0 = v.astype(BF).astype(F32)
        x_ref[kp * 16 : kp * 16 + 16, target] = jnp.concatenate([p0, v - p0], axis=0).astype(BF)


def start_copies(pairs, sems, first=0):
    copies = [pltpu.make_async_copy(src, dst, sems.at[first + n]) for n, (src, dst) in enumerate(pairs)]
    for copy in copies:
        copy.start()
    return copies


def wait_copies(copies):
    for copy in copies:
        copy.wait()


def start_copies(pairs, sems, first=0):
    copies = [pltpu.make_async_copy(src, dst, sems.at[first + n]) for n, (src, dst) in enumerate(pairs)]
    for copy in copies:
        copy.start()
    return copies


def wait_copies(copies):
    for copy in copies:
        copy.wait()


def start_copies(pairs, sems, first=0):
    copies = [pltpu.make_async_copy(src, dst, sems.at[first + n]) for n, (src, dst) in enumerate(pairs)]
    for copy in copies:
        copy.start()
    return copies


def wait_copies(copies):
    for copy in copies:
        copy.wait()


def rim_kernel(
    list_hbm, spec_hbm, near_hbm, slot_hbm, weight_hbm, before_hbm, after_hbm, spec_ref,
    near_ref, slot_ref, weight_ref, list_ref, before_ref, after_ref, sems,
):
    pairs = ((list_hbm, list_ref), (spec_hbm, spec_ref))
    first = start_copies(pairs + ((near_hbm, near_ref), (slot_hbm, slot_ref), (weight_hbm, weight_ref)), sems)
    wait_copies(first[:2])
    rims = []
    for side, rim_ref in ((0, before_ref), (1, after_ref)):
        index = jnp.broadcast_to(list_ref[side : side + 1, :], (8, 128))
        rims.append((index & 127, index >> 7, rim_ref))

    def step(i, carry):
        for low, high, rim_ref in rims:
            for g in range(3):
                rows = slice(8 * g, 8 * g + 8)
                got = None
                for h in range(16):
                    piece = lane_gather(spec_ref[i, rows, h * 128 : h * 128 + 128], low)
                    got = piece if h == 0 else jnp.where(high == h, piece, got)
                rim_ref[i, rows, :] = got
        return carry

    lax.fori_loop(0, GS, step, 0, unroll=2)
    last = start_copies(((before_ref, before_hbm), (after_ref, after_hbm)), sems)
    wait_copies(first[2:])
    wait_copies(last)


def outgoing_kernel(rows_hbm, forcing_hbm, out_hbm, rows_ref, forcing_ref, out_ref, sems, out_sems):
    wait_copies(start_copies(((rows_hbm, rows_ref), (forcing_hbm, forcing_ref)), sems))

    def step(q, carry):
        d = pl.ds(pl.multiple_of(q * 8, 8), 8)
        for half in range(2):
            index = rows_ref[d, half * 128 : half * 128 + 128]
            low, high = index & 127, index >> 7
            for i in range(4):
                got = None
                for h in range(16):
                    block = jnp.broadcast_to(forcing_ref[i : i + 1, h * 128 : h * 128 + 128], (8, 128))
                    piece = lane_gather(block, low)
                    got = piece if h == 0 else jnp.where(high == h, piece, got)
                out_ref[d, 2 * i + half, :] = got
        pltpu.make_async_copy(out_ref.at[d], out_hbm.at[d], out_sems.at[q]).start()
        return carry

    lax.fori_loop(0, TILES // 8, step, 0, unroll=4)
    for q in range(TILES // 8):
        d = pl.ds(q * 8, 8)
        pltpu.make_async_copy(out_ref.at[d], out_hbm.at[d], out_sems.at[q]).wait()


def weight_parts(slot_ref, weight_ref, cols, width, count):
    place = [slot_ref[j : j + 1, cols] for j in range(4)]
    slot = [p & (CAP - 1) for p in place]
    weight = [weight_ref[j : j + 1, cols] for j in range(4)]
    for j in range(1, 4):
        for i in range(j):
            same = slot[j] == slot[i]
            weight[i] = weight[i] + jnp.where(same, weight[j], 0.0)
            weight[j] = jnp.where(same, 0.0, weight[j])
    slots = lax.broadcasted_iota(jnp.int16, (CAP, width), 0)
    total = [jnp.zeros((CAP, width), BF)] * count
    for j in (3, 2, 1, 0):
        match = slots == slot[j].astype(jnp.int16)
        split = parts3(weight[j]) if count == 3 else parts2(weight[j])
        total = [jnp.where(match, part, rest) for part, rest in zip(split, total)]
    return total, place[0] >> 8


WB = 256


def wind_kernel(
    x_in_ref, arrived_ref, low_ref, high_ref, slot_ref, weight_ref, x_ref, wind_ref, mom_ref, left_ref
):
    up, down_scale = group_scale()
    wide = lambda values: jnp.concatenate([by_sublane(values)] * (WB // 128), axis=1)
    inv_c = wide([w / G_ACC for w in OMEGA]) * up
    inv_omega = wide([1.0 / w for w in OMEGA]) * down_scale
    inv_root = wide([math.sqrt(G_ACC) / w for w in OMEGA]) * down_scale
    omega_c = wide([w * w / G_ACC for w in OMEGA]) * (up * up)
    put_parts(low_ref, slice(0, RIM), x_ref, slice(0, RIM))
    put_parts(high_ref, slice(0, RIM), x_ref, slice(EXT - RIM, EXT))
    for i in range(4):
        for half in range(2):
            p0, p1, p2 = parts3(arrived_ref[:, 2 * i + half, :])
            for n, part in enumerate((p0, p1, p2, p0, p1, p0)):
                left_ref[i * 64 : i * 64 + 64, n * 256 + half * 128 : n * 256 + half * 128 + 128] = part

    def block(c, carry):
        cols = pl.ds(pl.multiple_of(c * WB, WB), WB)
        own = pl.ds(pl.multiple_of(c * WB + RIM, RIM), WB)
        (w0, w1, w2), band = weight_parts(slot_ref, weight_ref, cols, WB, 3)
        right = jnp.concatenate([w0, w0, w0, w1, w1, w2], axis=0)
        mixed = jnp.dot(left_ref[...], right, preferred_element_type=F32)
        mine = lax.broadcasted_iota(I32, (TILES, WB), 0) == band
        east, north, density, gust = (
            jnp.sum(jnp.where(mine, mixed[i * 64 : i * 64 + 64], 0.0), axis=0, keepdims=True) for i in range(4)
        )
        speed = jnp.sqrt(east * east + north * north + 1.0)
        friction = jnp.sqrt(0.001 * (0.8 + 0.065 * speed)) * speed * (1.0 + 0.15 * gust)
        pull = 28.0 * friction
        share = 0.25 * (density / WATER_DENSITY)
        spread = lambda v: jnp.broadcast_to(v, (8, WB))
        push_east, push_north = spread(pull * east / speed), spread(pull * north / speed)
        m0 = jnp.zeros((8, WB), F32)
        sx, sy = m0, m0

        def energy(k):
            kp = (k + ROLL) % ND
            both = x_ref[kp * 16 : kp * 16 + 16, own].astype(F32)
            return both[:8] + both[8:]

        for k in range(ND // 2):
            one, other = energy(k), energy(k + ND // 2)
            m0 = m0 + (one + other)
            push = (push_east * COS[k] + push_north * SIN[k]) * inv_c
            stress = jnp.maximum(push - 1.0, 0.0) * one - jnp.maximum(-push - 1.0, 0.0) * other
            sx = sx + stress * COS[k]
            sy = sy + stress * SIN[k]
        down = lambda v: jnp.sum(v, axis=0, keepdims=True)
        ms, mk, sx, sy = m0 * inv_omega, m0 * inv_root, sx * omega_c, sy * omega_c
        for n, row in enumerate((down(m0), down(ms), down(mk), down(sx) * share, down(sy) * share)):
            for half in range(WB // 128):
                mom_ref[pl.ds(n * 16 + c * (WB // 128) + half, 1), :] = row[:, half * 128 : half * 128 + 128]
        for n, row in enumerate((east, north, density, speed, friction)):
            for half in range(WB // 128):
                wind_ref[pl.ds(n * 16 + c * (WB // 128) + half, 1), :] = row[:, half * 128 : half * 128 + 128]
        return carry

    lax.fori_loop(0, PTS // WB, block, 0, unroll=8)


def field_kernel(
    m0_ref, m1_ref, m2_ref, m3_ref, wind_ref, slot_ref, weight_ref, diss_ref, sums_hbm,
    own_ref, sums_ref, sems,
):
    moments = m0_ref[...] + m1_ref[...] + m2_ref[...] + m3_ref[...]
    total, inv_sigma, inv_root, stress_e, stress_n = (moments[16 * n : 16 * n + 16] for n in range(5))
    east, north, density, speed, friction = (wind_ref[16 * n : 16 * n + 16, :] for n in range(5))
    mean_sigma = total / inv_sigma
    mean_wavenum = jnp.square(total / inv_root)
    steepness = mean_wavenum * mean_wavenum * total * E_UNIT
    diss_ref[80:96, :] = DISSIP_COEF * mean_sigma * jnp.square(steepness / STEEP_PM) / mean_wavenum
    diss_ref[0:80, :] = wind_ref[...]
    scale = WATER_DENSITY / density * G_ACC * E_UNIT
    friction_sq = friction * friction
    east_ratio = scale * stress_e / friction_sq
    north_ratio = scale * stress_n / friction_sq
    aligned = (east_ratio * east + north_ratio * north) / speed
    charnock = 1.0 / jnp.sqrt(1.0 - 0.9 * aligned / (1.0 + jnp.abs(aligned)))
    height = 4.0 * jnp.sqrt(E_UNIT * total)
    f = lax.axis_index("freq")
    own_ref[...] = jnp.where(f == 0, east_ratio, jnp.where(f == 1, north_ratio, jnp.where(f == 2, charnock, height)))


    def block(c, acc):
        cols = pl.ds(pl.multiple_of(c * WB, WB), WB)
        (w0, w1), band = weight_parts(slot_ref, weight_ref, cols, WB, 2)
        field = jnp.concatenate([own_ref[pl.ds(c * (WB // 128) + half, 1), :] for half in range(WB // 128)], axis=1)
        spread = jnp.where(lax.broadcasted_iota(I32, (TILES, WB), 0) == band, field, 0.0)
        f0, f1 = parts2(spread)
        left = jnp.concatenate([f0, f1, f0], axis=1)
        right = jnp.concatenate([w0, w0, w1], axis=1)
        return acc + lax.dot_general(left, right, (((1,), (1,)), ((), ())), preferred_element_type=F32)

    acc = lax.fori_loop(0, PTS // WB, block, jnp.zeros((TILES, CAP), F32), unroll=8)
    for half in range(2):
        sums_ref[:, half, :] = acc[:, half * 128 : half * 128 + 128]
    wait_copies(start_copies(((sums_ref, sums_hbm),), sems))


def band_kernel(arrived_ref, rows_ref, out_ref):
    def eight_tiles(q, acc):
        ones, values = [], []
        for t in range(8):
            index = rows_ref[pl.ds(q * 8 + t, 1), :]
            tile = arrived_ref[q * 8 + t]
            row = jnp.concatenate([tile[0:1, :], tile[1:2, :]], axis=1)
            v0, v1 = parts2(row)
            high = lax.broadcasted_iota(I32, (16, CAP), 0) == (index >> 7)
            v0, v1 = v0.astype(F32), v1.astype(F32)
            values.append(jnp.concatenate([jnp.where(high, v0, 0.0), jnp.where(high, v1, 0.0)], axis=0).astype(BF))
            match = lax.broadcasted_iota(jnp.int16, (128, CAP), 0) == (index & 127).astype(jnp.int16)
            ones.append(jnp.where(match, jnp.ones((), BF), jnp.zeros((), BF)))
        left = jnp.concatenate(ones, axis=1)
        right = jnp.concatenate(values, axis=1)
        return acc + lax.dot_general(left, right, (((1,), (1,)), ((), ())), preferred_element_type=F32)

    acc = lax.fori_loop(0, TILES // 8, eight_tiles, jnp.zeros((128, 32), F32), unroll=8)
    out_ref[...] = jnp.transpose(acc[:, :16] + acc[:, 16:])


def operand_kernel(spec_ref, x_ref):
    def put_block(h, carry):
        cols = pl.ds(pl.multiple_of(h * 128, 128), 128)
        put_parts(spec_ref, cols, x_ref, pl.ds(pl.multiple_of(h * 128 + RIM, 128), 128))
        return carry

    lax.fori_loop(0, PTS // 128, put_block, 0, unroll=2)


def move_kernel(half, near_ref, x_ref, out_ref):
    start, count = PARTS[half]
    scale = group_scale()[1]
    courant = jnp.concatenate([by_sublane(COURANT) * scale] * (NB // 128), axis=1)

    def hot(index):
        match = lax.broadcasted_iota(jnp.int16, (EXT, NB), 0) == index.astype(jnp.int16)
        return jnp.where(match, jnp.ones((), BF), jnp.zeros((), BF))

    def block(c, carry):
        outs = pl.ds(pl.multiple_of(c * NB, NB), NB)
        cols = pl.ds(pl.multiple_of(start + c * NB, NB), NB)
        own = pl.ds(pl.multiple_of(start + c * NB + RIM, RIM), NB)
        got = []
        for n, first in enumerate((0, 12, 6, 18)):
            index = near_ref[n : n + 1, cols]
            if first + 12 <= ND:
                left = x_ref[first * 16 : first * 16 + 192, :]
            else:
                left = jnp.concatenate([x_ref[first * 16 :, :], x_ref[: (first - 12) * 16, :]], axis=0)
            got.append(jnp.dot(left, hot(index), preferred_element_type=F32))
        for k in range(ND):
            kp = (k + ROLL) % ND
            x_of = got[0] if kp < 12 else got[1]
            a = kp % 12
            y_of = got[2] if k < 12 else got[3]
            b = k % 12
            from_x = x_of[a * 16 : a * 16 + 8] + x_of[a * 16 + 8 : a * 16 + 16]
            from_y = y_of[b * 16 : b * 16 + 8] + y_of[b * 16 + 8 : b * 16 + 16]
            both = x_ref[kp * 16 : kp * 16 + 16, own].astype(F32)
            spec = both[:8] + both[8:]
            out_ref[:, k, outs] = (
                spec - (courant * abs(COS[k])) * (spec - from_x) - (courant * abs(SIN[k])) * (spec - from_y)
            )
        return carry

    lax.fori_loop(0, count // NB, block, 0)


def source_kernel(moved0_ref, moved1_ref, wind_ref, out_hbm, push_ref, new_ref, stores):
    up = group_scale()[0]
    cos_tiles, sin_tiles = direction_tiles(COS), direction_tiles(SIN)

    def spread(c):
        row = lambda n: jnp.broadcast_to(wind_ref[pl.ds(n * 16 + c, 1), :], (8, 128))
        return [row(n) for n in range(5)]

    def prepare(c, carry):
        east, north, density, speed, friction = spread(c)
        pull = 28.0 * friction / speed
        for g in range(3):
            push_ref[c, 8 * g : 8 * g + 8, :] = pull * (east * cos_tiles[g] + north * sin_tiles[g])
        push_ref[c, 24:32, :] = (0.25 * DT_SRC) * (density / WATER_DENSITY)
        push_ref[c, 32:40, :] = DT_SRC * jnp.broadcast_to(wind_ref[pl.ds(80 + c, 1), :], (8, 128))
        return carry

    lax.fori_loop(0, PTS // 128, prepare, 0)
    for i in range(GS):
        inv_c, omega, wavenum = OMEGA[i] / G_ACC * up, OMEGA[i] * up, OMEGA[i] ** 2 / G_ACC * (up * up)

        for (start, count), moved_ref in zip(PARTS, (moved0_ref, moved1_ref)):

            def block(c, carry):
                at = c + start // 128
                cols = pl.ds(pl.multiple_of(c * 128, 128), 128)
                outs = pl.ds(pl.multiple_of(at * 128, 128), 128)
                share, loss = push_ref[at, 24:32, :] * omega, push_ref[at, 32:40, :] * wavenum
                for g in range(3):
                    rows = slice(8 * g, 8 * g + 8)
                    excess = jnp.maximum(push_ref[at, rows, :] * inv_c - 1.0, 0.0)
                    new_ref[i, rows, outs] = moved_ref[i, rows, cols] * jnp.exp(share * excess - loss)
                return carry

            lax.fori_loop(0, count // 128, block, 0, unroll=4)
        pltpu.make_async_copy(new_ref.at[i], out_hbm.at[i], stores.at[i]).start()
    for i in range(GS):
        pltpu.make_async_copy(new_ref.at[i], out_hbm.at[i], stores.at[i]).wait()


VMEM = pl.BlockSpec(memory_space=pltpu.VMEM)
HBM = pl.BlockSpec(memory_space=pltpu.HBM)


def array(*dims, dtype=F32):
    return jax.ShapeDtypeStruct(dims, dtype)


def resident(*dims, dtype=F32):
    return pltpu.VMEM(dims, dtype)


def distant(*dims, dtype=F32):
    return pltpu.HBM(dims, dtype)


def in_hbm(x):
    return pltpu.with_memory_space_constraint(x, pltpu.HBM)


def call(body, name, out, specs, scratch=(), mib=24, microseconds=1.0, out_specs=None, behind=False, mark=False, aliases={}):
    out = list(out)
    out_specs = [VMEM] * len(out) if out_specs is None else list(out_specs)
    specs = [*specs, VMEM] if behind else specs
    inputs = len(specs) - behind
    outputs = len(out)
    if mark:
        out.append(resident(8, 128))
        out_specs.append(VMEM)

    def kernel(*refs):
        results = inputs + behind
        if mark:
            refs[results + outputs][...] = jnp.zeros((8, 128), F32)
        body(*refs[:inputs], *refs[results : results + outputs], *refs[results + outputs + mark :])

    cost = pl.CostEstimate(flops=0, bytes_accessed=int(microseconds * 3.0e6), transcendentals=0)
    return pl.pallas_call(
        kernel,
        out_shape=out,
        in_specs=specs,
        out_specs=out_specs,
        scratch_shapes=list(scratch),
        name=name,
        input_output_aliases=aliases,
        cost_estimate=cost,
        compiler_params=pltpu.CompilerParams(vmem_limit_bytes=int(mib * 2**20)),
    )


def on_device(spectrum, forcing, send_rows, point_slot, remap_weight, neighbours, halo_send):
    dma = pltpu.SemaphoreType.DMA
    outgoing, rows, mark = call(
        outgoing_kernel,
        "outgoing",
        [distant(TILES, 8, 128), resident(TILES, CAP, dtype=I32)],
        [HBM] * 2,
        [
            pltpu.VMEM((4, PTS), F32),
            pltpu.VMEM((TILES, 8, 128), F32),
            dma((2,)),
            dma((TILES // 8,)),
        ],
        microseconds=3.0,
        out_specs=[HBM, VMEM],
        mark=True,
    )(in_hbm(send_rows), in_hbm(forcing))
    arrived = lax.all_to_all(outgoing, "tile", split_axis=0, concat_axis=0, tiled=True)

    to_before, to_after, spec, near, slot, weight, mark = call(
        rim_kernel,
        "rims",
        [distant(GS, ND, RIM), distant(GS, ND, RIM), resident(GS, ND, PTS)]
        + [resident(4, PTS, dtype=I32), resident(4, PTS, dtype=I32), resident(4, PTS)],
        [HBM] * 5,
        [
            pltpu.VMEM((2, RIM), I32),
            pltpu.VMEM((GS, ND, RIM), F32),
            pltpu.VMEM((GS, ND, RIM), F32),
            dma((5,)),
        ],
        microseconds=3.0,
        out_specs=[HBM, HBM] + [VMEM] * 4,
        behind=True,
        mark=True,
    )(*map(in_hbm, (halo_send.reshape(2, RIM), spectrum, neighbours, point_slot, remap_weight)), mark)
    up = [(d, d + 1) for d in range(TILES - 1)]
    low_rim = lax.ppermute(to_after, "tile", up)
    high_rim = lax.ppermute(to_before, "tile", [(b, a) for a, b in up])
    operand, mark = call(
        operand_kernel,
        "operand",
        [resident(ND * 16, EXT, dtype=BF)],
        [VMEM],
        microseconds=3.0,
        behind=True,
        mark=True,
    )(spec, mark)

    operand, wind, moments, mark = call(
        wind_kernel,
        "wind",
        [resident(ND * 16, EXT, dtype=BF), array(80, 128), array(80, 128)],
        [VMEM] * 6,
        [pltpu.VMEM((256, 6 * 256), BF)],
        microseconds=6.0,
        behind=True,
        mark=True,
        aliases={0: 0},
    )(operand, arrived, low_rim, high_rim, slot, weight, mark)
    others = [lax.ppermute(moments, "freq", [(i, (i + n) % 4) for i in range(4)]) for n in (1, 2, 3)]

    def move(half, mark):
        return call(
            functools.partial(move_kernel, half),
            f"move{half}",
            [resident(GS, ND, PARTS[half][1])],
            [VMEM] * 2,
            microseconds=5.5,
            behind=True,
            mark=True,
        )(near, operand, mark)

    moved0, mark = move(0, mark)
    state, slot_sums, mark = call(
        field_kernel,
        "fields",
        [resident(96, 128), distant(TILES, 2, 128)],
        [VMEM] * 7,
        [
            pltpu.VMEM((16, 128), F32),
            pltpu.VMEM((TILES, 2, 128), F32),
            dma((1,)),
        ],
        microseconds=3.0,
        out_specs=[VMEM, HBM],
        behind=True,
        mark=True,
    )(moments, *others, wind, slot, weight, mark)
    arrived_sums = lax.all_to_all(slot_sums, "tile", split_axis=0, concat_axis=0, tiled=True)

    moved1, mark = move(1, mark)
    new_spectrum, mark = call(
        source_kernel,
        "source",
        [array(GS, ND, PTS)],
        [VMEM] * 3,
        [pltpu.VMEM((PTS // 128, 40, 128), F32), pltpu.VMEM((GS, ND, PTS), F32), dma((GS,))],
        microseconds=3.0,
        out_specs=[HBM],
        behind=True,
        mark=True,
    )(moved0, moved1, state, mark)

    (returned,) = call(
        band_kernel,
        "band",
        [array(16, 128)],
        [VMEM] * 2,
        microseconds=2.5,
        behind=True,
    )(arrived_sums, rows, mark)
    return (new_spectrum, returned.reshape(1, PTS))


def solution(mesh):
    placed = (
        P("freq", None, "tile"),
        P(None, "tile"),
        P("tile", None),
        P(None, "tile"),
        P(None, "tile"),
        P(None, "tile"),
        P("tile"),
    )
    return jax.shard_map(
        on_device,
        mesh=mesh,
        in_specs=placed,
        out_specs=(P("freq", None, "tile"), P("freq", "tile")),
        check_vma=False,
    )
```

```python
import functools
import math

import jax
import jax.numpy as jnp
from jax import lax
from jax.experimental import pallas as pl
from jax.experimental.pallas import tpu as pltpu
from jax.sharding import PartitionSpec as P

G_ACC = 9.81
WATER_DENSITY = 1025.0
FREQ_LOW = 0.03453
FREQ_RATIO = 1.1
E_UNIT = 0.001
DT_SRC = 120.0
COURANT_MAX = 0.7
DISSIP_COEF = 2.33e-05
STEEP_PM = 0.00302
TOP_EXPONENT = 31.0

NF = 32
ND = 24
GS = 8
PTS = 2048
TILES = 64
CAP = 256
RIM = 128
EXT = PTS + 2 * RIM

F32 = jnp.float32
BF = jnp.bfloat16
I32 = jnp.int32

THETA = [(k + 0.5) * 2.0 * math.pi / ND for k in range(ND)]
COS = [math.cos(t) for t in THETA]
SIN = [math.sin(t) for t in THETA]

OMEGA = [2.0 * math.pi * FREQ_LOW * FREQ_RATIO**i for i in range(GS)]
COURANT = [COURANT_MAX * FREQ_RATIO ** (-i) for i in range(GS)]


def group_scale():
    f = lax.axis_index("freq")
    pick = lambda v: jnp.where(f == 0, v[0], jnp.where(f == 1, v[1], jnp.where(f == 2, v[2], v[3]))).astype(F32)
    return pick([FREQ_RATIO ** (GS * n) for n in range(4)]), pick([FREQ_RATIO ** (-GS * n) for n in range(4)])


def by_sublane(values):
    which = lax.broadcasted_iota(I32, (8, 128), 0)
    tile = jnp.full((8, 128), values[7], F32)
    for n in range(7):
        tile = jnp.where(which == n, values[n], tile)
    return tile


def direction_tiles(values):
    return [by_sublane(values[8 * g : 8 * g + 8]) for g in range(3)]


def lane_gather(block, index):
    return jnp.take_along_axis(block, index, axis=1, mode="promise_in_bounds")


def parts2(x):
    first = x.astype(BF)
    return first, (x - first.astype(F32)).astype(BF)


def parts3(x):
    first = x.astype(BF)
    rest = x - first.astype(F32)
    second = rest.astype(BF)
    return first, second, (rest - second.astype(F32)).astype(BF)


ROLL = 6
NB = 512
PARTS = ((0, 1024), (1024, PTS - 1024))


def put_parts(ref, source, x_ref, target):
    for kp in range(ND):
        v = ref[:, (kp + ND - ROLL) % ND, source]
        p0 = v.astype(BF).astype(F32)
        x_ref[kp * 16 : kp * 16 + 16, target] = jnp.concatenate([p0, v - p0], axis=0).astype(BF)


def start_copies(pairs, sems, first=0):
    copies = [pltpu.make_async_copy(src, dst, sems.at[first + n]) for n, (src, dst) in enumerate(pairs)]
    for copy in copies:
        copy.start()
    return copies


def wait_copies(copies):
    for copy in copies:
        copy.wait()


def start_copies(pairs, sems, first=0):
    copies = [pltpu.make_async_copy(src, dst, sems.at[first + n]) for n, (src, dst) in enumerate(pairs)]
    for copy in copies:
        copy.start()
    return copies


def wait_copies(copies):
    for copy in copies:
        copy.wait()


def start_copies(pairs, sems, first=0):
    copies = [pltpu.make_async_copy(src, dst, sems.at[first + n]) for n, (src, dst) in enumerate(pairs)]
    for copy in copies:
        copy.start()
    return copies


def wait_copies(copies):
    for copy in copies:
        copy.wait()


def rim_kernel(
    list_hbm, spec_hbm, near_hbm, slot_hbm, weight_hbm, inner_hbm, outer_hbm, spec_ref,
    near_ref, slot_ref, weight_ref, list_ref, inner_ref, outer_ref, sems,
):
    pairs = ((list_hbm, list_ref), (spec_hbm, spec_ref))
    first = start_copies(pairs + ((near_hbm, near_ref), (slot_hbm, slot_ref), (weight_hbm, weight_ref)), sems)
    wait_copies(first[:2])
    rims = []
    even = lax.rem(lax.axis_index("tile"), 2) == 0
    to_last, to_next = list_ref[0:1, :], list_ref[1:2, :]
    lists = (jnp.where(even, to_next, to_last), jnp.where(even, to_last, to_next))
    for chosen, rim_ref in zip(lists, (inner_ref, outer_ref)):
        index = jnp.broadcast_to(chosen, (8, 128))
        rims.append((index & 127, index >> 7, rim_ref))

    def step(i, carry):
        for low, high, rim_ref in rims:
            for g in range(3):
                rows = slice(8 * g, 8 * g + 8)
                got = None
                for h in range(16):
                    piece = lane_gather(spec_ref[i, rows, h * 128 : h * 128 + 128], low)
                    got = piece if h == 0 else jnp.where(high == h, piece, got)
                rim_ref[i, rows, :] = got
        return carry

    lax.fori_loop(0, GS, step, 0, unroll=2)
    last = start_copies(((inner_ref, inner_hbm), (outer_ref, outer_hbm)), sems)
    wait_copies(first[2:])
    wait_copies(last)


def outgoing_kernel(rows_hbm, forcing_hbm, out_hbm, rows_ref, forcing_ref, out_ref, sems, out_sems):
    wait_copies(start_copies(((rows_hbm, rows_ref), (forcing_hbm, forcing_ref)), sems))

    def step(q, carry):
        d = pl.ds(pl.multiple_of(q * 8, 8), 8)
        for half in range(2):
            index = rows_ref[d, half * 128 : half * 128 + 128]
            low, high = index & 127, index >> 7
            for i in range(4):
                got = None
                for h in range(16):
                    block = jnp.broadcast_to(forcing_ref[i : i + 1, h * 128 : h * 128 + 128], (8, 128))
                    piece = lane_gather(block, low)
                    got = piece if h == 0 else jnp.where(high == h, piece, got)
                out_ref[d, 2 * i + half, :] = got
        pltpu.make_async_copy(out_ref.at[d], out_hbm.at[d], out_sems.at[q]).start()
        return carry

    lax.fori_loop(0, TILES // 8, step, 0, unroll=4)
    for q in range(TILES // 8):
        d = pl.ds(q * 8, 8)
        pltpu.make_async_copy(out_ref.at[d], out_hbm.at[d], out_sems.at[q]).wait()


def weight_parts(slot_ref, weight_ref, cols, width, count):
    place = [slot_ref[j : j + 1, cols] for j in range(4)]
    slot = [p & (CAP - 1) for p in place]
    weight = [weight_ref[j : j + 1, cols] for j in range(4)]
    for j in range(1, 4):
        for i in range(j):
            same = slot[j] == slot[i]
            weight[i] = weight[i] + jnp.where(same, weight[j], 0.0)
            weight[j] = jnp.where(same, 0.0, weight[j])
    slots = lax.broadcasted_iota(jnp.int16, (CAP, width), 0)
    total = [jnp.zeros((CAP, width), BF)] * count
    for j in (3, 2, 1, 0):
        match = slots == slot[j].astype(jnp.int16)
        split = parts3(weight[j]) if count == 3 else parts2(weight[j])
        total = [jnp.where(match, part, rest) for part, rest in zip(split, total)]
    return total, place[0] >> 8


WB = 256


def wind_kernel(
    x_in_ref, arrived_ref, low_ref, high_ref, slot_ref, weight_ref, x_ref, wind_ref, mom_ref, left_ref
):
    up, down_scale = group_scale()
    wide = lambda values: jnp.concatenate([by_sublane(values)] * (WB // 128), axis=1)
    inv_c = wide([w / G_ACC for w in OMEGA]) * up
    inv_omega = wide([1.0 / w for w in OMEGA]) * down_scale
    inv_root = wide([math.sqrt(G_ACC) / w for w in OMEGA]) * down_scale
    omega_c = wide([w * w / G_ACC for w in OMEGA]) * (up * up)
    even = lax.rem(lax.axis_index("tile"), 2) == 0
    upper, lower = jnp.where(even, EXT - RIM, 0), jnp.where(even, 0, EXT - RIM)
    put_parts(low_ref, slice(0, RIM), x_ref, pl.ds(pl.multiple_of(upper, RIM), RIM))
    put_parts(high_ref, slice(0, RIM), x_ref, pl.ds(pl.multiple_of(lower, RIM), RIM))
    for i in range(4):
        for half in range(2):
            p0, p1, p2 = parts3(arrived_ref[:, 2 * i + half, :])
            for n, part in enumerate((p0, p1, p2, p0, p1, p0)):
                left_ref[i * 64 : i * 64 + 64, n * 256 + half * 128 : n * 256 + half * 128 + 128] = part

    def block(c, carry):
        cols = pl.ds(pl.multiple_of(c * WB, WB), WB)
        own = pl.ds(pl.multiple_of(c * WB + RIM, RIM), WB)
        (w0, w1, w2), band = weight_parts(slot_ref, weight_ref, cols, WB, 3)
        right = jnp.concatenate([w0, w0, w0, w1, w1, w2], axis=0)
        mixed = jnp.dot(left_ref[...], right, preferred_element_type=F32)
        mine = lax.broadcasted_iota(I32, (TILES, WB), 0) == band
        east, north, density, gust = (
            jnp.sum(jnp.where(mine, mixed[i * 64 : i * 64 + 64], 0.0), axis=0, keepdims=True) for i in range(4)
        )
        speed = jnp.sqrt(east * east + north * north + 1.0)
        friction = jnp.sqrt(0.001 * (0.8 + 0.065 * speed)) * speed * (1.0 + 0.15 * gust)
        pull = 28.0 * friction
        share = 0.25 * (density / WATER_DENSITY)
        spread = lambda v: jnp.broadcast_to(v, (8, WB))
        push_east, push_north = spread(pull * east / speed), spread(pull * north / speed)
        m0 = jnp.zeros((8, WB), F32)
        sx, sy = m0, m0

        def energy(k):
            kp = (k + ROLL) % ND
            both = x_ref[kp * 16 : kp * 16 + 16, own].astype(F32)
            return both[:8] + both[8:]

        for k in range(ND // 2):
            one, other = energy(k), energy(k + ND // 2)
            m0 = m0 + (one + other)
            push = (push_east * COS[k] + push_north * SIN[k]) * inv_c
            stress = jnp.maximum(push - 1.0, 0.0) * one - jnp.maximum(-push - 1.0, 0.0) * other
            sx = sx + stress * COS[k]
            sy = sy + stress * SIN[k]
        down = lambda v: jnp.sum(v, axis=0, keepdims=True)
        ms, mk, sx, sy = m0 * inv_omega, m0 * inv_root, sx * omega_c, sy * omega_c
        for n, row in enumerate((down(m0), down(ms), down(mk), down(sx) * share, down(sy) * share)):
            for half in range(WB // 128):
                mom_ref[pl.ds(n * 16 + c * (WB // 128) + half, 1), :] = row[:, half * 128 : half * 128 + 128]
        for n, row in enumerate((east, north, density, speed, friction)):
            for half in range(WB // 128):
                wind_ref[pl.ds(n * 16 + c * (WB // 128) + half, 1), :] = row[:, half * 128 : half * 128 + 128]
        return carry

    lax.fori_loop(0, PTS // WB, block, 0, unroll=8)


def field_kernel(
    m0_ref, m1_ref, m2_ref, m3_ref, wind_ref, slot_ref, weight_ref, diss_ref, sums_hbm,
    own_ref, sums_ref, sems,
):
    moments = m0_ref[...] + m1_ref[...] + m2_ref[...] + m3_ref[...]
    total, inv_sigma, inv_root, stress_e, stress_n = (moments[16 * n : 16 * n + 16] for n in range(5))
    east, north, density, speed, friction = (wind_ref[16 * n : 16 * n + 16, :] for n in range(5))
    mean_sigma = total / inv_sigma
    mean_wavenum = jnp.square(total / inv_root)
    steepness = mean_wavenum * mean_wavenum * total * E_UNIT
    diss_ref[80:96, :] = DISSIP_COEF * mean_sigma * jnp.square(steepness / STEEP_PM) / mean_wavenum
    diss_ref[0:80, :] = wind_ref[...]
    scale = WATER_DENSITY / density * G_ACC * E_UNIT
    friction_sq = friction * friction
    east_ratio = scale * stress_e / friction_sq
    north_ratio = scale * stress_n / friction_sq
    aligned = (east_ratio * east + north_ratio * north) / speed
    charnock = 1.0 / jnp.sqrt(1.0 - 0.9 * aligned / (1.0 + jnp.abs(aligned)))
    height = 4.0 * jnp.sqrt(E_UNIT * total)
    f = lax.axis_index("freq")
    own_ref[...] = jnp.where(f == 0, east_ratio, jnp.where(f == 1, north_ratio, jnp.where(f == 2, charnock, height)))


    def block(c, acc):
        cols = pl.ds(pl.multiple_of(c * WB, WB), WB)
        (w0, w1), band = weight_parts(slot_ref, weight_ref, cols, WB, 2)
        field = jnp.concatenate([own_ref[pl.ds(c * (WB // 128) + half, 1), :] for half in range(WB // 128)], axis=1)
        spread = jnp.where(lax.broadcasted_iota(I32, (TILES, WB), 0) == band, field, 0.0)
        f0, f1 = parts2(spread)
        left = jnp.concatenate([f0, f1, f0], axis=1)
        right = jnp.concatenate([w0, w0, w1], axis=1)
        return acc + lax.dot_general(left, right, (((1,), (1,)), ((), ())), preferred_element_type=F32)

    acc = lax.fori_loop(0, PTS // WB, block, jnp.zeros((TILES, CAP), F32), unroll=8)
    for half in range(2):
        sums_ref[:, half, :] = acc[:, half * 128 : half * 128 + 128]
    wait_copies(start_copies(((sums_ref, sums_hbm),), sems))


def band_kernel(arrived_ref, rows_ref, out_ref):
    def eight_tiles(q, acc):
        ones, values = [], []
        for t in range(8):
            index = rows_ref[pl.ds(q * 8 + t, 1), :]
            tile = arrived_ref[q * 8 + t]
            row = jnp.concatenate([tile[0:1, :], tile[1:2, :]], axis=1)
            v0, v1 = parts2(row)
            high = lax.broadcasted_iota(I32, (16, CAP), 0) == (index >> 7)
            v0, v1 = v0.astype(F32), v1.astype(F32)
            values.append(jnp.concatenate([jnp.where(high, v0, 0.0), jnp.where(high, v1, 0.0)], axis=0).astype(BF))
            match = lax.broadcasted_iota(jnp.int16, (128, CAP), 0) == (index & 127).astype(jnp.int16)
            ones.append(jnp.where(match, jnp.ones((), BF), jnp.zeros((), BF)))
        left = jnp.concatenate(ones, axis=1)
        right = jnp.concatenate(values, axis=1)
        return acc + lax.dot_general(left, right, (((1,), (1,)), ((), ())), preferred_element_type=F32)

    acc = lax.fori_loop(0, TILES // 8, eight_tiles, jnp.zeros((128, 32), F32), unroll=8)
    out_ref[...] = jnp.transpose(acc[:, :16] + acc[:, 16:])


def operand_kernel(spec_ref, x_ref):
    def put_block(h, carry):
        cols = pl.ds(pl.multiple_of(h * 128, 128), 128)
        put_parts(spec_ref, cols, x_ref, pl.ds(pl.multiple_of(h * 128 + RIM, 128), 128))
        return carry

    lax.fori_loop(0, PTS // 128, put_block, 0, unroll=2)


def move_kernel(half, near_ref, x_ref, out_ref):
    start, count = PARTS[half]
    scale = group_scale()[1]
    courant = jnp.concatenate([by_sublane(COURANT) * scale] * (NB // 128), axis=1)

    def hot(index):
        match = lax.broadcasted_iota(jnp.int16, (EXT, NB), 0) == index.astype(jnp.int16)
        return jnp.where(match, jnp.ones((), BF), jnp.zeros((), BF))

    def block(c, carry):
        outs = pl.ds(pl.multiple_of(c * NB, NB), NB)
        cols = pl.ds(pl.multiple_of(start + c * NB, NB), NB)
        own = pl.ds(pl.multiple_of(start + c * NB + RIM, RIM), NB)
        got = []
        for n, first in enumerate((0, 12, 6, 18)):
            index = near_ref[n : n + 1, cols]
            if first + 12 <= ND:
                left = x_ref[first * 16 : first * 16 + 192, :]
            else:
                left = jnp.concatenate([x_ref[first * 16 :, :], x_ref[: (first - 12) * 16, :]], axis=0)
            got.append(jnp.dot(left, hot(index), preferred_element_type=F32))
        for k in range(ND):
            kp = (k + ROLL) % ND
            x_of = got[0] if kp < 12 else got[1]
            a = kp % 12
            y_of = got[2] if k < 12 else got[3]
            b = k % 12
            from_x = x_of[a * 16 : a * 16 + 8] + x_of[a * 16 + 8 : a * 16 + 16]
            from_y = y_of[b * 16 : b * 16 + 8] + y_of[b * 16 + 8 : b * 16 + 16]
            both = x_ref[kp * 16 : kp * 16 + 16, own].astype(F32)
            spec = both[:8] + both[8:]
            out_ref[:, k, outs] = (
                spec - (courant * abs(COS[k])) * (spec - from_x) - (courant * abs(SIN[k])) * (spec - from_y)
            )
        return carry

    lax.fori_loop(0, count // NB, block, 0)


def source_kernel(moved0_ref, moved1_ref, wind_ref, out_hbm, push_ref, new_ref, stores):
    up = group_scale()[0]
    cos_tiles, sin_tiles = direction_tiles(COS), direction_tiles(SIN)

    def spread(c):
        row = lambda n: jnp.broadcast_to(wind_ref[pl.ds(n * 16 + c, 1), :], (8, 128))
        return [row(n) for n in range(5)]

    def prepare(c, carry):
        east, north, density, speed, friction = spread(c)
        pull = 28.0 * friction / speed
        for g in range(3):
            push_ref[c, 8 * g : 8 * g + 8, :] = pull * (east * cos_tiles[g] + north * sin_tiles[g])
        push_ref[c, 24:32, :] = (0.25 * DT_SRC) * (density / WATER_DENSITY)
        push_ref[c, 32:40, :] = DT_SRC * jnp.broadcast_to(wind_ref[pl.ds(80 + c, 1), :], (8, 128))
        return carry

    lax.fori_loop(0, PTS // 128, prepare, 0)
    for i in range(GS):
        inv_c, omega, wavenum = OMEGA[i] / G_ACC * up, OMEGA[i] * up, OMEGA[i] ** 2 / G_ACC * (up * up)

        for (start, count), moved_ref in zip(PARTS, (moved0_ref, moved1_ref)):

            def block(c, carry):
                at = c + start // 128
                cols = pl.ds(pl.multiple_of(c * 128, 128), 128)
                outs = pl.ds(pl.multiple_of(at * 128, 128), 128)
                share, loss = push_ref[at, 24:32, :] * omega, push_ref[at, 32:40, :] * wavenum
                for g in range(3):
                    rows = slice(8 * g, 8 * g + 8)
                    excess = jnp.maximum(push_ref[at, rows, :] * inv_c - 1.0, 0.0)
                    new_ref[i, rows, outs] = moved_ref[i, rows, cols] * jnp.exp(share * excess - loss)
                return carry

            lax.fori_loop(0, count // 128, block, 0, unroll=4)
        pltpu.make_async_copy(new_ref.at[i], out_hbm.at[i], stores.at[i]).start()
    for i in range(GS):
        pltpu.make_async_copy(new_ref.at[i], out_hbm.at[i], stores.at[i]).wait()


VMEM = pl.BlockSpec(memory_space=pltpu.VMEM)
HBM = pl.BlockSpec(memory_space=pltpu.HBM)


def array(*dims, dtype=F32):
    return jax.ShapeDtypeStruct(dims, dtype)


def resident(*dims, dtype=F32):
    return pltpu.VMEM(dims, dtype)


def distant(*dims, dtype=F32):
    return pltpu.HBM(dims, dtype)


def in_hbm(x):
    return pltpu.with_memory_space_constraint(x, pltpu.HBM)


def call(body, name, out, specs, scratch=(), mib=24, microseconds=1.0, out_specs=None, behind=False, mark=False, aliases={}):
    out = list(out)
    out_specs = [VMEM] * len(out) if out_specs is None else list(out_specs)
    specs = [*specs, VMEM] if behind else specs
    inputs = len(specs) - behind
    outputs = len(out)
    if mark:
        out.append(resident(8, 128))
        out_specs.append(VMEM)

    def kernel(*refs):
        results = inputs + behind
        if mark:
            refs[results + outputs][...] = jnp.zeros((8, 128), F32)
        body(*refs[:inputs], *refs[results : results + outputs], *refs[results + outputs + mark :])

    cost = pl.CostEstimate(flops=0, bytes_accessed=int(microseconds * 3.0e6), transcendentals=0)
    return pl.pallas_call(
        kernel,
        out_shape=out,
        in_specs=specs,
        out_specs=out_specs,
        scratch_shapes=list(scratch),
        name=name,
        input_output_aliases=aliases,
        cost_estimate=cost,
        compiler_params=pltpu.CompilerParams(vmem_limit_bytes=int(mib * 2**20)),
    )


def on_device(spectrum, forcing, send_rows, point_slot, remap_weight, neighbours, halo_send):
    dma = pltpu.SemaphoreType.DMA
    outgoing, rows, mark = call(
        outgoing_kernel,
        "outgoing",
        [distant(TILES, 8, 128), resident(TILES, CAP, dtype=I32)],
        [HBM] * 2,
        [
            pltpu.VMEM((4, PTS), F32),
            pltpu.VMEM((TILES, 8, 128), F32),
            dma((2,)),
            dma((TILES // 8,)),
        ],
        microseconds=3.0,
        out_specs=[HBM, VMEM],
        mark=True,
    )(in_hbm(send_rows), in_hbm(forcing))
    arrived = lax.all_to_all(outgoing, "tile", split_axis=0, concat_axis=0, tiled=True)

    inner, outer, spec, near, slot, weight, mark = call(
        rim_kernel,
        "rims",
        [distant(GS, ND, RIM), distant(GS, ND, RIM), resident(GS, ND, PTS)]
        + [resident(4, PTS, dtype=I32), resident(4, PTS, dtype=I32), resident(4, PTS)],
        [HBM] * 5,
        [
            pltpu.VMEM((2, RIM), I32),
            pltpu.VMEM((GS, ND, RIM), F32),
            pltpu.VMEM((GS, ND, RIM), F32),
            dma((5,)),
        ],
        microseconds=3.0,
        out_specs=[HBM, HBM] + [VMEM] * 4,
        behind=True,
        mark=True,
    )(*map(in_hbm, (halo_send.reshape(2, RIM), spectrum, neighbours, point_slot, remap_weight)), mark)
    trades = []
    for first in (0, 1):
        pairs = [(d, d + 1) for d in range(first, TILES - 1, 2)]
        trades.append(pairs + [(b, a) for a, b in pairs])
    inner_rim = lax.ppermute(inner, "tile", trades[0])
    outer_rim = lax.ppermute(outer, "tile", trades[1])
    operand, mark = call(
        operand_kernel,
        "operand",
        [resident(ND * 16, EXT, dtype=BF)],
        [VMEM],
        microseconds=3.0,
        behind=True,
        mark=True,
    )(spec, mark)

    operand, wind, moments, mark = call(
        wind_kernel,
        "wind",
        [resident(ND * 16, EXT, dtype=BF), array(80, 128), array(80, 128)],
        [VMEM] * 6,
        [pltpu.VMEM((256, 6 * 256), BF)],
        microseconds=6.0,
        behind=True,
        mark=True,
        aliases={0: 0},
    )(operand, arrived, inner_rim, outer_rim, slot, weight, mark)
    others = [lax.ppermute(moments, "freq", [(i, (i + n) % 4) for i in range(4)]) for n in (1, 2, 3)]

    def move(half, mark):
        return call(
            functools.partial(move_kernel, half),
            f"move{half}",
            [resident(GS, ND, PARTS[half][1])],
            [VMEM] * 2,
            microseconds=5.5,
            behind=True,
            mark=True,
        )(near, operand, mark)

    moved0, mark = move(0, mark)
    state, slot_sums, mark = call(
        field_kernel,
        "fields",
        [resident(96, 128), distant(TILES, 2, 128)],
        [VMEM] * 7,
        [
            pltpu.VMEM((16, 128), F32),
            pltpu.VMEM((TILES, 2, 128), F32),
            dma((1,)),
        ],
        microseconds=3.0,
        out_specs=[VMEM, HBM],
        behind=True,
        mark=True,
    )(moments, *others, wind, slot, weight, mark)
    arrived_sums = lax.all_to_all(slot_sums, "tile", split_axis=0, concat_axis=0, tiled=True)

    moved1, mark = move(1, mark)
    new_spectrum, mark = call(
        source_kernel,
        "source",
        [array(GS, ND, PTS)],
        [VMEM] * 3,
        [pltpu.VMEM((PTS // 128, 40, 128), F32), pltpu.VMEM((GS, ND, PTS), F32), dma((GS,))],
        microseconds=3.0,
        out_specs=[HBM],
        behind=True,
        mark=True,
    )(moved0, moved1, state, mark)

    (returned,) = call(
        band_kernel,
        "band",
        [array(16, 128)],
        [VMEM] * 2,
        microseconds=2.5,
        behind=True,
    )(arrived_sums, rows, mark)
    return (new_spectrum, returned.reshape(1, PTS))


def solution(mesh):
    placed = (
        P("freq", None, "tile"),
        P(None, "tile"),
        P("tile", None),
        P(None, "tile"),
        P(None, "tile"),
        P(None, "tile"),
        P("tile"),
    )
    return jax.shard_map(
        on_device,
        mesh=mesh,
        in_specs=placed,
        out_specs=(P("freq", None, "tile"), P("freq", "tile")),
        check_vma=False,
    )
```
